32 devices in a mesh: ctx: 4 (over y, core), head: 4 (over z), dp: 2 (over x).
Axes of the slice: x: 2, y: 2, z: 4, core: 2. Of those that a mesh axis runs over, the one named last changes fastest.
Arguments:
- queries: bfloat16 [2048, 8192], P(('dp', 'ctx', 'head')), parts along dimension 0, may hold values from -100 to 100, as said below
- unscaled_key_rows: bfloat16 [2048, 1024], P(('dp', 'ctx', 'head')), parts along dimension 0, may hold values from -4 to 4
- unscaled_value_rows: bfloat16 [2048, 1024], P(('dp', 'ctx', 'head')), parts along dimension 0, may hold values from -12 to 12
- key_block_scale: float32 [16, 8], P('dp', 'head'), parts along dimension 0, may hold values from 0.8 to 1.6
- value_block_scale: float32 [16, 8], P('dp', 'head'), parts along dimension 0, may hold values from 0.5 to 2
- span_order: int32 [8], replicated, may hold values from 0 to 7, each once
- block_keep: int32 [8, 8], replicated, may hold values 0 or 1
Outputs:
- attended: bfloat16 [2048, 8192], P(('dp', 'ctx', 'head')), parts along dimension 0
- row_check: float32 [2048, 64], P(('dp', 'ctx', 'head')), parts along dimension 0
The draws below stay inside these ranges and needn't reach their ends.
There are 2 independent parts, one for each index of `dp`. The reference program is written for one: setup_inputs(seed, part) draws one part's arguments, and reference() takes and returns one part's arrays. A program takes and returns all parts, laid end to end along the dimension named above; an argument that names none is the same for every part. Nothing has to cross between parts.
Inputs may be any that keep to these rules, and one draw needn't show every extreme that they name: `queries`: queries of one head and token.
All inputs are finite; a program needn't handle non-finite values.
Results may differ from the reference program's by a relative error of at most 0.004.
Values may be sent and summed in bfloat16 or wider, within the bound.
No kernel may reach another device: no remote copies, remote signals or barrier semaphores. Data moves between devices by JAX's collectives and lax.ppermute only.
A program may use at most 64 MiB of HBM per device.

```python
import math
import jax
import jax.numpy as jnp
from jax import lax

QUERY_HEADS = 64
KEY_VALUE_HEADS = 8
HEAD_WIDTH = 128
SPAN = 128
SEQUENCE_TOKENS = 1024
STORED_BLOCKS = 8


def shared_keys(key):
    random_seed_key = jax.random.fold_in(key, 7)
    gaussian_keys = jax.random.normal(jax.random.fold_in(random_seed_key, 1), (SEQUENCE_TOKENS, KEY_VALUE_HEADS, HEAD_WIDTH), jnp.float32)
    clipped = jnp.clip(gaussian_keys, -4.0, 4.0)
    normalized_rows = clipped
    return normalized_rows


def draw_unscaled_key_rows(key, part):
    normalized_rows = shared_keys(key)
    return normalized_rows.reshape(SEQUENCE_TOKENS, KEY_VALUE_HEADS * HEAD_WIDTH).astype(jnp.bfloat16)


def draw_queries(key, part):
    normal_rows = jax.random.normal(jax.random.fold_in(key, 9), (SEQUENCE_TOKENS, QUERY_HEADS, HEAD_WIDTH), jnp.float32)
    query_rows = jnp.clip(normal_rows, -4.0, 4.0)
    return query_rows.reshape(SEQUENCE_TOKENS, QUERY_HEADS * HEAD_WIDTH).astype(jnp.bfloat16)


def draw_unscaled_value_rows(key, part):
    stored_block_count = SEQUENCE_TOKENS // SPAN
    offset_sample = jnp.clip(jax.random.normal(jax.random.fold_in(key, 21), (stored_block_count, KEY_VALUE_HEADS * HEAD_WIDTH), jnp.float32), -3.0, 3.0)
    offsets = 2.0 * offset_sample
    random_jitter = jnp.clip(jax.random.normal(jax.random.fold_in(key, 23), (SEQUENCE_TOKENS, KEY_VALUE_HEADS * HEAD_WIDTH), jnp.float32), -4.0, 4.0)
    return (jnp.repeat(offsets, SPAN, axis=0) + random_jitter).astype(jnp.bfloat16)


def set_ends(result, stream_key, smallest, largest):
    place = [jax.random.randint(jax.random.fold_in(stream_key, axis), (), 0, length) for axis, length in enumerate(result.shape)]
    main_axis = result.shape.index(max(result.shape))
    beside = place[:main_axis] + [(place[main_axis] + 1) % result.shape[main_axis]] + place[main_axis + 1:]
    return result.at[tuple(place)].set(smallest).at[tuple(beside)].set(largest)


def steps_of(own_key, dims, pieces, smallest, top_value):
    level, own = 1.0, jax.random.fold_in(own_key, 6)
    for dim, blocks in pieces:
        heights = jnp.exp(jax.random.uniform(jax.random.fold_in(own, dim), (blocks,), jnp.float32, smallest / len(pieces), top_value / len(pieces)))
        level = level * jnp.repeat(heights, dims[dim] // blocks).reshape([-1 if axis == dim else 1 for axis in range(len(dims))])
    return level


def setup_inputs(seed: int = 0, part: int = 0) -> dict:
    splits = jax.random.split(jax.random.key(seed), 8)
    own_keys = jax.random.split(jax.random.fold_in(splits[7], part), 8)
    return {
        "queries": draw_queries(jax.random.fold_in(jax.random.fold_in(splits[7], part), 71), part),
        "unscaled_key_rows": draw_unscaled_key_rows(jax.random.fold_in(jax.random.fold_in(splits[7], part), 71), part),
        "unscaled_value_rows": draw_unscaled_value_rows(jax.random.fold_in(jax.random.fold_in(splits[7], part), 71), part),
        "key_block_scale": jnp.clip(jnp.exp(math.log(1.6) - 0.6931472 * jax.random.uniform(own_keys[3], (STORED_BLOCKS, KEY_VALUE_HEADS), jnp.float32) ** steps_of(own_keys[3], (STORED_BLOCKS, KEY_VALUE_HEADS), ((1, 4),), -0.2, 0.2)), 0.8, 1.6),
        "value_block_scale": jnp.clip(jnp.exp(math.log(2.0) - 1.3862944 * jax.random.uniform(own_keys[4], (STORED_BLOCKS, KEY_VALUE_HEADS), jnp.float32) ** steps_of(own_keys[4], (STORED_BLOCKS, KEY_VALUE_HEADS), ((1, 4),), -0.2, 0.2)), 0.5, 2.0),
        "span_order": jax.random.permutation(splits[5], STORED_BLOCKS).astype(jnp.int32),
        "block_keep": set_ends((jax.random.randint(splits[6], (STORED_BLOCKS, STORED_BLOCKS), 0, 4) < 3).astype(jnp.int32), jax.random.fold_in(splits[6], 1), 0, 1),
    }


def reference(queries, unscaled_key_rows, unscaled_value_rows, key_block_scale, value_block_scale, span_order, block_keep):
    inverse_root = 1.0 / math.sqrt(HEAD_WIDTH)
    query_group_count = QUERY_HEADS // KEY_VALUE_HEADS
    token_index = jnp.arange(SEQUENCE_TOKENS, dtype=jnp.int32)
    token_span = (token_index // SPAN).astype(jnp.int32)
    position = span_order[token_span] * SPAN + token_index % SPAN
    same_span = token_span[:, None] == token_span[None, :]
    pair_keep = (block_keep[token_span][:, token_span] > 0) | same_span
    allowed = pair_keep & (position[:, None] >= position[None, :])
    query_heads = queries.reshape(SEQUENCE_TOKENS, QUERY_HEADS, HEAD_WIDTH)
    key_head_count = unscaled_key_rows.reshape(SEQUENCE_TOKENS, KEY_VALUE_HEADS, HEAD_WIDTH)
    value_head_count = unscaled_value_rows.reshape(SEQUENCE_TOKENS, KEY_VALUE_HEADS, HEAD_WIDTH)
    key_factor = key_block_scale[token_span] * inverse_root
    value_factor = value_block_scale[token_span]
    value_check = value_factor * lax.optimization_barrier(jnp.sum(value_head_count.astype(jnp.float32), axis=2)) * inverse_root

    def one_head(head_number):
        shared = head_number // query_group_count
        query_col = lax.dynamic_index_in_dim(query_heads, head_number, 1, keepdims=False)
        key_col = lax.dynamic_index_in_dim(key_head_count, shared, 1, keepdims=False)
        value_col = lax.dynamic_index_in_dim(value_head_count, shared, 1, keepdims=False)
        scale_col = lax.dynamic_index_in_dim(key_factor, shared, 1, keepdims=False)
        vfactor_col = lax.dynamic_index_in_dim(value_factor, shared, 1, keepdims=False)
        vcheck_col = lax.dynamic_index_in_dim(value_check, shared, 1, keepdims=False)
        scores = jnp.dot(query_col, key_col.T, preferred_element_type=jnp.float32) * scale_col[None, :]
        scores = jnp.where(allowed, scores, jnp.float32(-1e+30))
        highest = lax.optimization_barrier(jnp.max(scores, axis=1, keepdims=True))
        weights = jnp.where(allowed, jnp.exp(scores - highest), jnp.float32(0.0))
        totals = lax.optimization_barrier(jnp.sum(weights, axis=1))
        rounded = weights.astype(jnp.bfloat16).astype(jnp.float32)
        mixed = jnp.dot(rounded * vfactor_col[None, :], value_col.astype(jnp.float32), precision=lax.Precision.HIGHEST)
        checks = jnp.dot(rounded, vcheck_col, precision=lax.Precision.HIGHEST)
        return ((mixed / totals[:, None]).astype(jnp.bfloat16), checks / totals)
    head_outs, head_checks = lax.map(one_head, jnp.arange(QUERY_HEADS, dtype=jnp.int32))
    attended = jnp.transpose(head_outs, (1, 0, 2)).reshape(SEQUENCE_TOKENS, QUERY_HEADS * HEAD_WIDTH)
    return (attended, jnp.transpose(head_checks, (1, 0)))
```

```python
import functools
import math

import jax
import jax.numpy as jnp
from jax import lax
from jax.experimental import pallas as pl
from jax.experimental.pallas import tpu as pltpu
from jax.sharding import PartitionSpec as P

HEAD_WIDTH = 128
SPAN = 128
LOG2E = 1.4426950408889634
MASKED = -1e30


def attend_kernel(
    place_ref,
    order_ref,
    keep_ref,
    scale_ref,
    q_ref,
    k_ref,
    v_ref,
    out_ref,
    check_ref,
    bias_ref,
    x_ref,
    p_ref,
    *,
    groups,
    kv_local,
):
    g = pl.program_id(0)
    tokens = q_ref.shape[0]
    blocks = k_ref.shape[0] // SPAN
    own = place_ref[0]
    offset = place_ref[1]
    inverse_root = 1.0 / math.sqrt(HEAD_WIDTH)
    row = lax.broadcasted_iota(jnp.int32, (tokens, SPAN), 0)
    col = lax.broadcasted_iota(jnp.int32, (tokens, SPAN), 1)

    @pl.when(g == 0)
    def _():
        causal = jnp.where(col <= row + offset, 0.0, MASKED)
        for b in range(blocks):
            seen = (order_ref[b] < order_ref[own]) & (keep_ref[own, b] > 0)
            whole = jnp.where(seen, 0.0, MASKED)
            bias_ref[b] = jnp.where(own == b, causal, whole)
        check_ref[...] = jnp.zeros_like(check_ref)

    heads = [q_ref[:, h * HEAD_WIDTH : (h + 1) * HEAD_WIDTH] for h in range(groups)]
    q = jnp.concatenate(heads, axis=0)
    for b in range(blocks):
        k = k_ref[b * SPAN : (b + 1) * SPAN, :]
        x_ref[b] = lax.dot_general(
            q, k, (((1,), (1,)), ((), ())), preferred_element_type=jnp.float32
        )
    owner, member = g // kv_local, g % kv_local
    key_factor = [
        scale_ref[owner, 0, b, member] * (inverse_root * LOG2E) for b in range(blocks)
    ]
    value_factor = [scale_ref[owner, 1, b, member] for b in range(blocks)]
    totals = []
    for h in range(groups):
        rows = slice(h * tokens, (h + 1) * tokens)
        top = None
        for b in range(blocks):
            x = x_ref[b, rows, :] * key_factor[b] + bias_ref[b]
            x_ref[b, rows, :] = x
            top = x if top is None else jnp.maximum(top, x)
        top = jnp.max(top, axis=1, keepdims=True)
        total = None
        for b in range(blocks):
            weight = jnp.exp2(x_ref[b, rows, :] - top)
            p_ref[b, rows, :] = weight.astype(jnp.bfloat16)
            total = weight if total is None else total + weight
        totals.append(jnp.sum(total, axis=1, keepdims=True))
    mixed = None
    for b in range(blocks):
        v = v_ref[b * SPAN : (b + 1) * SPAN, :]
        part = value_factor[b] * jnp.dot(p_ref[b], v, preferred_element_type=jnp.float32)
        mixed = part if mixed is None else mixed + part
    lane = lax.broadcasted_iota(jnp.int32, check_ref.shape, 1)
    checks = check_ref[...]
    for h in range(groups):
        rows = slice(h * tokens, (h + 1) * tokens)
        attended = mixed[rows] * (1.0 / totals[h])
        out_ref[:, h * HEAD_WIDTH : (h + 1) * HEAD_WIDTH] = attended.astype(out_ref.dtype)
        check = jnp.sum(attended, axis=1, keepdims=True) * inverse_root
        checks = jnp.where(lane == g * groups + h, check, checks)
    check_ref[...] = checks


def local(queries, keys, values, key_scale, value_scale, span_order, block_keep):
    tokens, width = queries.shape
    kv_heads = keys.shape[1] // HEAD_WIDTH
    groups = width // HEAD_WIDTH // kv_heads
    kv_local = key_scale.shape[1]
    all_keys = lax.all_gather(keys, ("ctx", "head"), axis=0, tiled=True)
    all_values = lax.all_gather(values, ("ctx", "head"), axis=0, tiled=True)
    scales = lax.all_gather(jnp.stack([key_scale, value_scale]), "head", axis=0)
    first = (lax.axis_index("ctx") * lax.axis_size("head") + lax.axis_index("head")) * tokens
    place = jnp.stack([first // SPAN, first % SPAN]).astype(jnp.int32)
    length = all_keys.shape[0]
    blocks = length // SPAN
    smem = pl.BlockSpec(memory_space=pltpu.SMEM)
    rows = groups * tokens
    return pl.pallas_call(
        functools.partial(attend_kernel, groups=groups, kv_local=kv_local),
        grid=(kv_heads,),
        in_specs=[
            smem,
            smem,
            smem,
            smem,
            pl.BlockSpec((tokens, groups * HEAD_WIDTH), lambda g: (0, g)),
            pl.BlockSpec((length, HEAD_WIDTH), lambda g: (0, g)),
            pl.BlockSpec((length, HEAD_WIDTH), lambda g: (0, g)),
        ],
        out_specs=[
            pl.BlockSpec((tokens, groups * HEAD_WIDTH), lambda g: (0, g)),
            pl.BlockSpec((tokens, kv_heads * groups), lambda g: (0, 0)),
        ],
        out_shape=[
            jax.ShapeDtypeStruct((tokens, width), jnp.bfloat16),
            jax.ShapeDtypeStruct((tokens, kv_heads * groups), jnp.float32),
        ],
        scratch_shapes=[
            pltpu.VMEM((blocks, tokens, SPAN), jnp.float32),
            pltpu.VMEM((blocks, rows, SPAN), jnp.float32),
            pltpu.VMEM((blocks, rows, SPAN), jnp.bfloat16),
        ],
        compiler_params=pltpu.CompilerParams(vmem_limit_bytes=40 * 1024 * 1024),
        cost_estimate=pl.CostEstimate(
            flops=4 * tokens * width * length,
            bytes_accessed=4 * (tokens * width + length * kv_heads * HEAD_WIDTH),
            transcendentals=tokens * width // HEAD_WIDTH * length,
        ),
    )(place, span_order, block_keep, scales, queries, all_keys, all_values)


def solution(mesh):
    rows = P(("dp", "ctx", "head"), None)
    return jax.shard_map(
        local,
        mesh=mesh,
        in_specs=(rows, rows, rows, P("dp", "head"), P("dp", "head"), P(), P()),
        out_specs=(rows, rows),
        check_vma=False,
    )
```

```python
import functools
import math

import jax
import jax.numpy as jnp
from jax import lax
from jax.experimental import pallas as pl
from jax.experimental.pallas import tpu as pltpu
from jax.sharding import PartitionSpec as P

HEAD_WIDTH = 128
SPAN = 128
LOG2E = 1.4426950408889634
MASKED = -1e30


def attend_kernel(order_ref, keep_ref, *refs, groups, kv_heads, kv_local, sources, ctx_size, head_size):
    scale_in = refs[:head_size]
    pieces = refs[head_size : head_size + len(sources)]
    (q_ref, out_ref, check_ref, scale_ref, kv_ref, mask_ref, qa_ref, x_ref, p_ref, scale_sem, kv_sem) = refs[
        head_size + len(sources) :
    ]
    g = pl.program_id(0)
    tokens = q_ref.shape[0]
    length = kv_ref.shape[0]
    blocks = length // SPAN
    inverse_root = 1.0 / math.sqrt(HEAD_WIDTH)
    ctx, head = lax.axis_index("ctx"), lax.axis_index("head")

    @pl.when(g == 0)
    def _():
        copies = []
        for shift in range(head_size):
            owner = lax.rem(head - shift + head_size, head_size)
            copies.append(
                pltpu.make_async_copy(scale_in[shift], scale_ref.at[owner], scale_sem.at[shift])
            )
        for i, (flip, shift) in enumerate(sources):
            owner = lax.rem(head - shift + head_size, head_size)
            first = pl.multiple_of(((ctx ^ flip) * head_size + owner) * tokens, tokens)
            copies.append(
                pltpu.make_async_copy(pieces[i], kv_ref.at[pl.ds(first, tokens), :], kv_sem.at[i])
            )
        for copy in copies:
            copy.start()
        first = (ctx * head_size + head) * tokens
        own, offset = first // SPAN, first % SPAN
        key = lax.broadcasted_iota(jnp.int32, (SPAN, SPAN), 0)
        token = lax.broadcasted_iota(jnp.int32, (SPAN, SPAN), 1)
        causal = jnp.where(key <= token + offset, 0.0, MASKED)
        for b in range(blocks):
            seen = (order_ref[b] < order_ref[own]) & (keep_ref[own, b] > 0)
            whole = jnp.where(seen, 0.0, MASKED)
            mask = jnp.where(own == b, causal, whole)
            mask_ref[b * SPAN : (b + 1) * SPAN, :] = mask.astype(jnp.bfloat16)
        row = lax.broadcasted_iota(jnp.int32, (tokens, SPAN), 0)
        col = lax.broadcasted_iota(jnp.int32, (tokens, SPAN), 1)
        one_hot = jnp.where(row == col, 1.0, 0.0).astype(jnp.bfloat16)
        for h in range(groups):
            qa_ref[h * tokens : (h + 1) * tokens, HEAD_WIDTH:] = one_hot
        check_ref[...] = jnp.zeros_like(check_ref)
        for copy in copies:
            copy.wait()

    for h in range(groups):
        qa_ref[h * tokens : (h + 1) * tokens, :HEAD_WIDTH] = q_ref[
            :, h * HEAD_WIDTH : (h + 1) * HEAD_WIDTH
        ]
    k_cols = pl.ds(pl.multiple_of(g * HEAD_WIDTH, HEAD_WIDTH), HEAD_WIDTH)
    v_cols = pl.ds(pl.multiple_of((g + kv_heads) * HEAD_WIDTH, HEAD_WIDTH), HEAD_WIDTH)
    q = qa_ref[...]
    for b in range(blocks):
        keys = slice(b * SPAN, (b + 1) * SPAN)
        k = jnp.concatenate([kv_ref[keys, k_cols], mask_ref[keys, :]], axis=1)
        x_ref[b] = lax.dot_general(
            q, k, (((1,), (1,)), ((), ())), preferred_element_type=jnp.float32
        )
    owner, member = g // kv_local, g % kv_local
    key_factor = [scale_ref[owner, b, member] * (inverse_root * LOG2E) for b in range(blocks)]
    value_factor = [scale_ref[owner, b, kv_local + member] for b in range(blocks)]
    totals = []
    for h in range(groups):
        rows = slice(h * tokens, (h + 1) * tokens)
        top = None
        for b in range(blocks):
            x = x_ref[b, rows, :] * key_factor[b]
            top = x if top is None else jnp.maximum(top, x)
        top = jnp.max(top, axis=1, keepdims=True)
        total = None
        for b in range(blocks):
            weight = jnp.exp2(x_ref[b, rows, :] * key_factor[b] - top)
            p_ref[b, rows, :] = weight.astype(jnp.bfloat16)
            total = weight if total is None else total + weight
        totals.append(jnp.sum(total, axis=1, keepdims=True))
    mixed = None
    for b in range(blocks):
        v = kv_ref[b * SPAN : (b + 1) * SPAN, v_cols]
        part = value_factor[b] * jnp.dot(p_ref[b], v, preferred_element_type=jnp.float32)
        mixed = part if mixed is None else mixed + part
    lane = lax.broadcasted_iota(jnp.int32, check_ref.shape, 1)
    checks = check_ref[...]
    for h in range(groups):
        rows = slice(h * tokens, (h + 1) * tokens)
        attended = mixed[rows] * (1.0 / totals[h])
        out_ref[:, h * HEAD_WIDTH : (h + 1) * HEAD_WIDTH] = attended.astype(out_ref.dtype)
        check = jnp.sum(attended, axis=1, keepdims=True) * inverse_root
        checks = jnp.where(lane == g * groups + h, check, checks)
    check_ref[...] = checks


def local(queries, keys, values, key_scale, value_scale, span_order, block_keep):
    tokens, width = queries.shape
    kv_heads = keys.shape[1] // HEAD_WIDTH
    groups = width // HEAD_WIDTH // kv_heads
    kv_local = key_scale.shape[1]
    ctx_size, head_size = lax.axis_size("ctx"), lax.axis_size("head")

    def along_head(block, distance):
        return lax.ppermute(block, "head", [(i, (i + distance) % head_size) for i in range(head_size)])

    def across_ctx(block, flip):
        return lax.ppermute(block, "ctx", [(i, i ^ flip) for i in range(ctx_size)])

    moving = jnp.concatenate([keys, values], axis=1)
    scale = jnp.concatenate([key_scale, value_scale], axis=1)
    scales = [scale] + [along_head(scale, s) for s in range(1, head_size)]
    pieces, sources = [], []
    for shift in range(head_size):
        if shift:
            moving = along_head(moving, 1)
        held = [(0, moving)]
        flip = ctx_size // 2
        while flip:
            held = held + [(f ^ flip, across_ctx(block, flip)) for f, block in held]
            flip //= 2
        pieces += [block for _, block in held]
        sources += [(f, shift) for f, _ in held]

    length = tokens * ctx_size * head_size
    blocks = length // SPAN
    smem = pl.BlockSpec(memory_space=pltpu.SMEM)
    anywhere = pl.BlockSpec(memory_space=pl.ANY)
    rows = groups * tokens
    return pl.pallas_call(
        functools.partial(
            attend_kernel,
            groups=groups,
            kv_heads=kv_heads,
            kv_local=kv_local,
            sources=sources,
            ctx_size=ctx_size,
            head_size=head_size,
        ),
        grid=(kv_heads,),
        in_specs=[smem, smem]
        + [anywhere] * (head_size + len(pieces))
        + [pl.BlockSpec((tokens, groups * HEAD_WIDTH), lambda g: (0, g))],
        out_specs=[
            pl.BlockSpec((tokens, groups * HEAD_WIDTH), lambda g: (0, g)),
            pl.BlockSpec((tokens, kv_heads * groups), lambda g: (0, 0)),
        ],
        out_shape=[
            jax.ShapeDtypeStruct((tokens, width), jnp.bfloat16),
            jax.ShapeDtypeStruct((tokens, kv_heads * groups), jnp.float32),
        ],
        scratch_shapes=[
            pltpu.SMEM((head_size,) + scale.shape, jnp.float32),
            pltpu.VMEM((length, 2 * kv_heads * HEAD_WIDTH), jnp.bfloat16),
            pltpu.VMEM((length, SPAN), jnp.bfloat16),
            pltpu.VMEM((rows, HEAD_WIDTH + SPAN), jnp.bfloat16),
            pltpu.VMEM((blocks, rows, SPAN), jnp.float32),
            pltpu.VMEM((blocks, rows, SPAN), jnp.bfloat16),
            pltpu.SemaphoreType.DMA((head_size,)),
            pltpu.SemaphoreType.DMA((len(pieces),)),
        ],
        compiler_params=pltpu.CompilerParams(vmem_limit_bytes=60 * 1024 * 1024),
        cost_estimate=pl.CostEstimate(
            flops=4 * tokens * width * length,
            bytes_accessed=4 * (tokens * width + length * kv_heads * HEAD_WIDTH),
            transcendentals=tokens * width // HEAD_WIDTH * length,
        ),
    )(span_order, block_keep, *scales, *pieces, queries)


def solution(mesh):
    rows = P(("dp", "ctx", "head"), None)
    return jax.shard_map(
        local,
        mesh=mesh,
        in_specs=(rows, rows, rows, P("dp", "head"), P("dp", "head"), P(), P()),
        out_specs=(rows, rows),
        check_vma=False,
    )
```

```python
import functools
import math

import jax
import jax.numpy as jnp
from jax import lax
from jax.experimental import pallas as pl
from jax.experimental.pallas import tpu as pltpu
from jax.sharding import PartitionSpec as P

HEAD_WIDTH = 128
SPAN = 128
LOG2E = 1.4426950408889634
MASKED = -1e30


def absorb_kernel(
    order_ref, keep_ref, *refs, groups, per_step, kv_heads, kv_local, sources, ctx_size, head_size, first, last
):
    refs = list(refs)
    scale_in = [refs.pop(0) for _ in range(head_size)]
    pieces = [refs.pop(0) for _ in sources]
    q_ref = refs.pop(0)
    mixed_in, stats_in = (None, None) if first else (refs.pop(0), refs.pop(0))
    result_ref, stats_ref, scale_ref, mask_ref, x_ref, p_ref, scale_sem = refs
    step = pl.program_id(0)
    tokens = q_ref.shape[0]
    width = tokens * len(sources)
    inverse_root = 1.0 / math.sqrt(HEAD_WIDTH)
    ctx, head = lax.axis_index("ctx"), lax.axis_index("head")
    starts = [
        ((ctx ^ flip) * head_size + lax.rem(head - shift + head_size, head_size)) * tokens
        for flip, shift in sources
    ]
    spans = [start // SPAN for start in starts]

    @pl.when(step == 0)
    def _():
        copies = []
        for shift in range(head_size):
            owner = lax.rem(head - shift + head_size, head_size)
            copies.append(
                pltpu.make_async_copy(scale_in[shift], scale_ref.at[owner], scale_sem.at[shift])
            )
        for copy in copies:
            copy.start()
        own_start = (ctx * head_size + head) * tokens
        own = own_start // SPAN
        key = lax.broadcasted_iota(jnp.int32, (tokens, SPAN), 0)
        token = lax.broadcasted_iota(jnp.int32, (tokens, SPAN), 1)
        for i, (start, span) in enumerate(zip(starts, spans)):
            seen = (order_ref[span] < order_ref[own]) & (keep_ref[own, span] > 0)
            whole = jnp.where(seen, 0.0, MASKED)
            causal = jnp.where(key + (start - own_start) <= token, 0.0, MASKED)
            mask = jnp.where(own == span, causal, whole)
            mask_ref[i * tokens : (i + 1) * tokens, :] = mask.astype(jnp.bfloat16)
        for copy in copies:
            copy.wait()

    row = lax.broadcasted_iota(jnp.int32, (tokens, SPAN), 0)
    lane = lax.broadcasted_iota(jnp.int32, (tokens, SPAN), 1)
    lane_row = lax.broadcasted_iota(jnp.int32, (1, SPAN), 1)
    one_hot = jnp.where(row == lane, 1.0, 0.0).astype(jnp.bfloat16)
    if last:
        checks = stats_ref[...]
        check_lane = lax.broadcasted_iota(jnp.int32, checks.shape, 1)
    for u in range(per_step):
        g = step * per_step + u
        k_cols = pl.ds(pl.multiple_of(g * HEAD_WIDTH, HEAD_WIDTH), HEAD_WIDTH)
        q = [
            q_ref[:, (u * groups + h) * HEAD_WIDTH : (u * groups + h + 1) * HEAD_WIDTH]
            for h in range(groups)
        ]
        q = jnp.concatenate(
            [jnp.concatenate(q, axis=0), jnp.concatenate([one_hot] * groups, axis=0)], axis=1
        )
        k = jnp.concatenate([piece[:, k_cols] for piece in pieces], axis=0)
        k = jnp.concatenate([k, mask_ref[...]], axis=1)
        x_ref[u] = lax.dot_general(
            q, k, (((1,), (1,)), ((), ())), preferred_element_type=jnp.float32
        )
    for u in range(per_step):
        g = step * per_step + u
        owner, member = g // kv_local, g % kv_local
        per_tile = SPAN // tokens
        factors = []
        for tile in range(width // SPAN):
            vector = None
            for j in range(per_tile):
                value = scale_ref[owner, spans[tile * per_tile + j], member] * (inverse_root * LOG2E)
                vector = (
                    jnp.full((1, SPAN), value, jnp.float32)
                    if vector is None
                    else jnp.where(lane_row >= j * tokens, value, vector)
                )
            factors.append(vector)
        v_cols = pl.ds(pl.multiple_of((g + kv_heads) * HEAD_WIDTH, HEAD_WIDTH), HEAD_WIDTH)
        high, low = [], []
        for i, piece in enumerate(pieces):
            v = piece[:, v_cols].astype(jnp.float32) * scale_ref[owner, spans[i], kv_local + member]
            high.append(v.astype(jnp.bfloat16))
            low.append((v - high[-1].astype(jnp.float32)).astype(jnp.bfloat16))
        v = jnp.concatenate(
            [jnp.concatenate(high, axis=0), jnp.concatenate(low, axis=0)], axis=1
        )
        tops, totals, fades = [], [], []
        for h in range(groups):
            rows = slice(h * tokens, (h + 1) * tokens)
            xs = [
                x_ref[u, rows, i * SPAN : (i + 1) * SPAN] * factor
                for i, factor in enumerate(factors)
            ]
            top = xs[0]
            for x in xs[1:]:
                top = jnp.maximum(top, x)
            top = jnp.max(top, axis=1, keepdims=True)
            if not first:
                before = stats_in[u, 0, :, h : h + 1]
                top = jnp.maximum(top, before)
                fades.append(jnp.exp2(before - top))
            total = None
            for i, x in enumerate(xs):
                weight = jnp.exp2(x - top)
                p_ref[u, rows, i * SPAN : (i + 1) * SPAN] = weight.astype(jnp.bfloat16)
                total = weight if total is None else total + weight
            total = jnp.sum(total, axis=1, keepdims=True)
            if not first:
                total = total + fades[h] * stats_in[u, 1, :, h : h + 1]
            tops.append(top)
            totals.append(total)
        both = jnp.dot(p_ref[u], v, preferred_element_type=jnp.float32)
        new_top = new_total = jnp.zeros((tokens, SPAN), jnp.float32)
        for h in range(groups):
            rows = slice(h * tokens, (h + 1) * tokens)
            cols = slice((u * groups + h) * HEAD_WIDTH, (u * groups + h + 1) * HEAD_WIDTH)
            mixed = both[rows, :HEAD_WIDTH] + both[rows, HEAD_WIDTH:]
            if not first:
                mixed = mixed + fades[h] * mixed_in[:, cols]
            if last:
                mixed = mixed * (1.0 / totals[h])
                check = jnp.sum(mixed, axis=1, keepdims=True) * inverse_root
                checks = jnp.where(check_lane == g * groups + h, check, checks)
            else:
                new_top = jnp.where(lane == h, tops[h], new_top)
                new_total = jnp.where(lane == h, totals[h], new_total)
            result_ref[:, cols] = mixed.astype(result_ref.dtype)
        if not last:
            stats_ref[u, 0] = new_top
            stats_ref[u, 1] = new_total
    if last:
        stats_ref[...] = checks


def absorb(queries, chunk, scales, span_order, block_keep, state, last, kv_heads, kv_local, sizes):
    tokens, width = queries.shape
    groups = width // HEAD_WIDTH // kv_heads
    per_step = 2 if kv_heads % 2 == 0 else 1
    pieces = [block for _, _, block in chunk]
    sources = [(flip, shift) for flip, shift, _ in chunk]
    keys = tokens * len(chunk)
    first = state is None
    columns = pl.BlockSpec((tokens, per_step * groups * HEAD_WIDTH), lambda s: (0, s))
    stats = pl.BlockSpec((per_step, 2, tokens, SPAN), lambda s: (s, 0, 0, 0))
    smem = pl.BlockSpec(memory_space=pltpu.SMEM)
    in_specs = [smem, smem] + [pl.BlockSpec(memory_space=pl.ANY)] * len(scales)
    in_specs += [pl.BlockSpec(piece.shape, lambda s: (0, 0)) for piece in pieces]
    in_specs += [columns] + ([] if first else [columns, stats])
    if last:
        out_specs = [columns, pl.BlockSpec((tokens, kv_heads * groups), lambda s: (0, 0))]
        out_shape = [
            jax.ShapeDtypeStruct((tokens, width), jnp.bfloat16),
            jax.ShapeDtypeStruct((tokens, kv_heads * groups), jnp.float32),
        ]
    else:
        out_specs = [columns, stats]
        out_shape = [
            jax.ShapeDtypeStruct((tokens, width), jnp.float32),
            jax.ShapeDtypeStruct((kv_heads, 2, tokens, SPAN), jnp.float32),
        ]
    return pl.pallas_call(
        functools.partial(
            absorb_kernel,
            groups=groups,
            per_step=per_step,
            kv_heads=kv_heads,
            kv_local=kv_local,
            sources=sources,
            ctx_size=sizes[0],
            head_size=sizes[1],
            first=first,
            last=last,
        ),
        grid=(kv_heads // per_step,),
        in_specs=in_specs,
        out_specs=out_specs,
        out_shape=out_shape,
        scratch_shapes=[
            pltpu.SMEM((len(scales),) + scales[0].shape, jnp.float32),
            pltpu.VMEM((keys, SPAN), jnp.bfloat16),
            pltpu.VMEM((per_step, groups * tokens, keys), jnp.float32),
            pltpu.VMEM((per_step, groups * tokens, keys), jnp.bfloat16),
            pltpu.SemaphoreType.DMA((len(scales),)),
        ],
        compiler_params=pltpu.CompilerParams(vmem_limit_bytes=24 * 1024 * 1024),
        cost_estimate=pl.CostEstimate(
            flops=16 * tokens * width * keys,
            bytes_accessed=16 * tokens * width,
            transcendentals=tokens * width // HEAD_WIDTH * keys,
        ),
    )(span_order, block_keep, *scales, *pieces, queries, *(() if first else state))


def local(queries, keys, values, key_scale, value_scale, span_order, block_keep):
    tokens, width = queries.shape
    kv_heads = keys.shape[1] // HEAD_WIDTH
    ctx_size, head_size = lax.axis_size("ctx"), lax.axis_size("head")
    levels = ctx_size.bit_length() - 1
    batch = 2 * SPAN // tokens

    def along_head(block, distance):
        return lax.ppermute(block, "head", [(i, (i + distance) % head_size) for i in range(head_size)])

    def across_ctx(block, flip):
        return lax.ppermute(block, "ctx", [(i, i ^ flip) for i in range(ctx_size)])

    def attend(chunk, state, last):
        return absorb(
            queries,
            chunk,
            scales,
            span_order,
            block_keep,
            state,
            last,
            kv_heads,
            key_scale.shape[1],
            (ctx_size, head_size),
        )

    scale = jnp.concatenate([key_scale, value_scale], axis=1)
    block = jnp.concatenate([keys, values], axis=1)
    arrived = [(0, 0, -1, block)]
    waiting, state, scales = [(0, 0, block)], None, None
    while arrived:
        coming = []
        for flip, shift, level, block in arrived:
            if level < 0 and shift + 1 < head_size:
                coming.append((flip, shift + 1, level, along_head(block, 1)))
            for later in range(level + 1, levels):
                bit = ctx_size >> (later + 1)
                coming.append((flip ^ bit, shift, later, across_ctx(block, bit)))
        if scales is None:
            scales = [scale] + [along_head(scale, s) for s in range(1, head_size)]
        ready = len(waiting) // batch * batch
        if ready:
            state = attend(waiting[:ready], state, not coming)
            waiting = waiting[ready:]
        if coming:
            blocks = [block for _, _, _, block in coming]
            blocks, state, scales = lax.optimization_barrier((blocks, state, scales))
            coming = [(f, s, l, b) for (f, s, l, _), b in zip(coming, blocks)]
        waiting += [(f, s, b) for f, s, _, b in coming]
        arrived = coming
    attended, row_check = state
    return attended, row_check


def solution(mesh):
    rows = P(("dp", "ctx", "head"), None)
    return jax.shard_map(
        local,
        mesh=mesh,
        in_specs=(rows, rows, rows, P("dp", "head"), P("dp", "head"), P(), P()),
        out_specs=(rows, rows),
        check_vma=False,
    )
```

```python
import functools
import math

import jax
import jax.numpy as jnp
from jax import lax
from jax.experimental import pallas as pl
from jax.experimental.pallas import tpu as pltpu
from jax.sharding import PartitionSpec as P

HEAD_WIDTH = 128
SPAN = 128
LOG2E = 1.4426950408889634
MASKED = -1e30


def pack_kernel(k_ref, v_ref, key_scale_ref, value_scale_ref, block_ref, scale_ref, sems):
    tokens = k_ref.shape[0]
    copies = [
        pltpu.make_async_copy(k_ref, block_ref.at[pl.ds(0, tokens), :], sems.at[0]),
        pltpu.make_async_copy(v_ref, block_ref.at[pl.ds(tokens, tokens), :], sems.at[1]),
        pltpu.make_async_copy(key_scale_ref, scale_ref.at[0], sems.at[2]),
        pltpu.make_async_copy(value_scale_ref, scale_ref.at[1], sems.at[3]),
    ]
    for copy in copies:
        copy.start()
    for copy in copies:
        copy.wait()


def pack(keys, values, key_scale, value_scale):
    tokens, width = keys.shape
    anywhere = pl.BlockSpec(memory_space=pl.ANY)
    return pl.pallas_call(
        pack_kernel,
        in_specs=[anywhere] * 4,
        out_specs=[anywhere] * 2,
        out_shape=[
            jax.ShapeDtypeStruct((2 * tokens, width), keys.dtype),
            jax.ShapeDtypeStruct((2,) + key_scale.shape, key_scale.dtype),
        ],
        scratch_shapes=[pltpu.SemaphoreType.DMA((4,))],
        compiler_params=pltpu.CompilerParams(vmem_limit_bytes=56 * 1024 * 1024),
    )(keys, values, key_scale, value_scale)


def absorb_kernel(
    order_ref, keep_ref, *refs, groups, per_step, kv_local, sources, ctx_size, head_size, first, last
):
    refs = list(refs)
    scale_in = [refs.pop(0) for _ in range(head_size)]
    pieces = [refs.pop(0) for _ in sources]
    q_ref = refs.pop(0)
    mixed_in, stats_in = (None, None) if first else (refs.pop(0), refs.pop(0))
    result_ref, stats_ref, scale_ref, mask_ref, x_ref, p_ref, check_ref, scale_sem = refs
    step = pl.program_id(0)
    tokens = q_ref.shape[0]
    inverse_root = 1.0 / math.sqrt(HEAD_WIDTH)
    ctx, head = lax.axis_index("ctx"), lax.axis_index("head")
    starts = [
        ((ctx ^ flip) * head_size + lax.rem(head - shift + head_size, head_size)) * tokens
        for flip, shift in sources
    ]
    spans = [start // SPAN for start in starts]

    @pl.when(step == 0)
    def _():
        copies = []
        for shift in range(head_size):
            owner = lax.rem(head - shift + head_size, head_size)
            copies.append(
                pltpu.make_async_copy(scale_in[shift], scale_ref.at[owner], scale_sem.at[shift])
            )
        for copy in copies:
            copy.start()
        own_start = (ctx * head_size + head) * tokens
        own = own_start // SPAN
        key = lax.broadcasted_iota(jnp.int32, (tokens, SPAN), 0)
        token = lax.broadcasted_iota(jnp.int32, (tokens, SPAN), 1)
        for i, (start, span) in enumerate(zip(starts, spans)):
            seen = (order_ref[span] < order_ref[own]) & (keep_ref[own, span] > 0)
            whole = jnp.where(seen, 0.0, MASKED)
            causal = jnp.where(key + (start - own_start) <= token, 0.0, MASKED)
            mask = jnp.where(own == span, causal, whole)
            mask_ref[i * tokens : (i + 1) * tokens, :] = mask.astype(jnp.bfloat16)
        for copy in copies:
            copy.wait()

    row = lax.broadcasted_iota(jnp.int32, (tokens, SPAN), 0)
    lane = lax.broadcasted_iota(jnp.int32, (tokens, SPAN), 1)
    one_hot = jnp.where(row == lane, 1.0, 0.0).astype(jnp.bfloat16)
    for u in range(per_step):
        g = step * per_step + u
        cols = pl.ds(pl.multiple_of(g * HEAD_WIDTH, HEAD_WIDTH), HEAD_WIDTH)
        q = [
            q_ref[:, (u * groups + h) * HEAD_WIDTH : (u * groups + h + 1) * HEAD_WIDTH]
            for h in range(groups)
        ]
        q = jnp.concatenate(
            [jnp.concatenate(q, axis=0), jnp.concatenate([one_hot] * groups, axis=0)], axis=1
        )
        k = jnp.concatenate([piece[:tokens, cols] for piece in pieces], axis=0)
        k = jnp.concatenate([k, mask_ref[...]], axis=1)
        x_ref[u] = lax.dot_general(
            k, q, (((1,), (1,)), ((), ())), preferred_element_type=jnp.float32
        )
    for u in range(per_step):
        g = step * per_step + u
        owner, member = g // kv_local, g % kv_local
        factors = [scale_ref[owner, 0, span, member] * (inverse_root * LOG2E) for span in spans]
        cols = pl.ds(pl.multiple_of(g * HEAD_WIDTH, HEAD_WIDTH), HEAD_WIDTH)
        high, low = [], []
        for i, piece in enumerate(pieces):
            v = piece[tokens:, cols].astype(jnp.float32) * scale_ref[owner, 1, spans[i], member]
            high.append(v.astype(jnp.bfloat16))
            low.append((v - high[-1].astype(jnp.float32)).astype(jnp.bfloat16))
        v = jnp.concatenate(
            [jnp.concatenate(high, axis=0), jnp.concatenate(low, axis=0)], axis=1
        )
        tops, totals, fades = [], [], []
        for tile in range(groups * tokens // SPAN):
            lanes = slice(tile * SPAN, (tile + 1) * SPAN)
            top = None
            for i, factor in enumerate(factors):
                x = x_ref[u, i * tokens : (i + 1) * tokens, lanes]
                highest = jnp.max(x.reshape(tokens // 8, 8, SPAN), axis=0) * factor
                top = highest if top is None else jnp.maximum(top, highest)
            top = jnp.max(top, axis=0, keepdims=True)
            if not first:
                before = stats_in[u, 0:1, lanes]
                top = jnp.maximum(top, before)
                fades.append(jnp.exp2(before - top))
            total = None
            for i, factor in enumerate(factors):
                keys = slice(i * tokens, (i + 1) * tokens)
                weight = jnp.exp2(x_ref[u, keys, lanes] * factor - top)
                p_ref[u, keys, lanes] = weight.astype(jnp.bfloat16)
                part = jnp.sum(weight.reshape(tokens // 8, 8, SPAN), axis=0)
                total = part if total is None else total + part
            total = jnp.sum(total, axis=0, keepdims=True)
            if not first:
                total = total + fades[tile] * stats_in[u, 1:2, lanes]
            tops.append(top)
            totals.append(total)
        both = lax.dot_general(
            v, p_ref[u], (((0,), (0,)), ((), ())), preferred_element_type=jnp.float32
        )
        for tile in range(groups * tokens // SPAN):
            lanes = slice(tile * SPAN, (tile + 1) * SPAN)
            mixed = both[:HEAD_WIDTH, lanes] + both[HEAD_WIDTH:, lanes]
            if not first:
                mixed = mixed + fades[tile] * mixed_in[u, :, lanes]
            if not last:
                result_ref[u, :, lanes] = mixed
                stats_ref[u, 0:1, lanes] = tops[tile]
                stats_ref[u, 1:2, lanes] = totals[tile]
                continue
            mixed = mixed * (1.0 / totals[tile])
            check = jnp.sum(mixed, axis=0, keepdims=True) * inverse_root
            mixed = jnp.transpose(mixed).astype(result_ref.dtype)
            for j in range(SPAN // tokens):
                h = tile * (SPAN // tokens) + j
                at = (u * groups + h) * HEAD_WIDTH
                result_ref[:, at : at + HEAD_WIDTH] = mixed[j * tokens : (j + 1) * tokens]
                check_ref[pl.ds(g * groups + h, 1), :] = check[:, j * tokens : (j + 1) * tokens]
    if last:

        @pl.when(step == pl.num_programs(0) - 1)
        def _():
            stats_ref[...] = jnp.transpose(check_ref[...])


def absorb(queries, chunk, scales, span_order, block_keep, state, last, kv_heads, kv_local, sizes):
    tokens, width = queries.shape
    groups = width // HEAD_WIDTH // kv_heads
    per_step = 2 if kv_heads % 2 == 0 else 1
    pieces = [block for _, _, block in chunk]
    sources = [(flip, shift) for flip, shift, _ in chunk]
    keys = tokens * len(chunk)
    first = state is None
    rows = groups * tokens
    columns = pl.BlockSpec((tokens, per_step * groups * HEAD_WIDTH), lambda s: (0, s))
    mixed = pl.BlockSpec((per_step, HEAD_WIDTH, rows), lambda s: (s, 0, 0))
    stats = pl.BlockSpec((per_step, 2, rows), lambda s: (s, 0, 0))
    smem = pl.BlockSpec(memory_space=pltpu.SMEM)
    in_specs = [smem, smem] + [pl.BlockSpec(memory_space=pl.ANY)] * len(scales)
    in_specs += [pl.BlockSpec(piece.shape, lambda s: (0, 0)) for piece in pieces]
    in_specs += [columns] + ([] if first else [mixed, stats])
    if last:
        out_specs = [columns, pl.BlockSpec((tokens, kv_heads * groups), lambda s: (0, 0))]
        out_shape = [
            jax.ShapeDtypeStruct((tokens, width), jnp.bfloat16),
            jax.ShapeDtypeStruct((tokens, kv_heads * groups), jnp.float32),
        ]
    else:
        out_specs = [mixed, stats]
        out_shape = [
            jax.ShapeDtypeStruct((kv_heads, HEAD_WIDTH, rows), jnp.float32),
            jax.ShapeDtypeStruct((kv_heads, 2, rows), jnp.float32),
        ]
    return pl.pallas_call(
        functools.partial(
            absorb_kernel,
            groups=groups,
            per_step=per_step,
            kv_local=kv_local,
            sources=sources,
            ctx_size=sizes[0],
            head_size=sizes[1],
            first=first,
            last=last,
        ),
        grid=(kv_heads // per_step,),
        in_specs=in_specs,
        out_specs=out_specs,
        out_shape=out_shape,
        scratch_shapes=[
            pltpu.SMEM((len(scales),) + scales[0].shape, jnp.float32),
            pltpu.VMEM((keys, SPAN), jnp.bfloat16),
            pltpu.VMEM((per_step, keys, rows), jnp.float32),
            pltpu.VMEM((per_step, keys, rows), jnp.bfloat16),
            pltpu.VMEM((kv_heads * groups, tokens), jnp.float32),
            pltpu.SemaphoreType.DMA((len(scales),)),
        ],
        compiler_params=pltpu.CompilerParams(vmem_limit_bytes=32 * 1024 * 1024),
        cost_estimate=pl.CostEstimate(
            flops=16 * tokens * width * keys,
            bytes_accessed=16 * tokens * width,
            transcendentals=tokens * width // HEAD_WIDTH * keys,
        ),
    )(span_order, block_keep, *scales, *pieces, queries, *(() if first else state))


def local(queries, keys, values, key_scale, value_scale, span_order, block_keep):
    tokens, width = queries.shape
    kv_heads = keys.shape[1] // HEAD_WIDTH
    ctx_size, head_size = lax.axis_size("ctx"), lax.axis_size("head")
    levels = ctx_size.bit_length() - 1
    batch = 2 * SPAN // tokens

    def along_head(block, distance):
        return lax.ppermute(block, "head", [(i, (i + distance) % head_size) for i in range(head_size)])

    def across_ctx(block, flip):
        return lax.ppermute(block, "ctx", [(i, i ^ flip) for i in range(ctx_size)])

    def attend(chunk, state, last):
        return absorb(
            queries,
            chunk,
            scales,
            span_order,
            block_keep,
            state,
            last,
            kv_heads,
            key_scale.shape[1],
            (ctx_size, head_size),
        )

    block, scale = pack(keys, values, key_scale, value_scale)
    arrived = [(0, 0, -1, block)]
    waiting, state, scales = [(0, 0, block)], None, [scale]
    while arrived:
        coming = []
        for flip, shift, level, block in arrived:
            if level < 0 and shift + 1 < head_size:
                coming.append((flip, shift + 1, level, along_head(block, 1)))
            for later in range(level + 1, levels):
                bit = ctx_size >> (later + 1)
                coming.append((flip ^ bit, shift, later, across_ctx(block, bit)))
        complete = len(scales) == head_size
        for shift in range(len(scales), min(head_size, len(scales) + head_size // 2)):
            scales = scales + [along_head(scale, shift)]
        ready = len(waiting) // batch * batch if complete else 0
        if ready:
            state = attend(waiting[:ready], state, not coming)
            waiting = waiting[ready:]
        if coming:
            blocks = [block for _, _, _, block in coming]
            blocks, state, scales = lax.optimization_barrier((blocks, state, scales))
            coming = [(f, s, l, b) for (f, s, l, _), b in zip(coming, blocks)]
        waiting += [(f, s, b) for f, s, _, b in coming]
        arrived = coming
    attended, row_check = state
    return attended, row_check


def solution(mesh):
    rows = P(("dp", "ctx", "head"), None)
    return jax.shard_map(
        local,
        mesh=mesh,
        in_specs=(rows, rows, rows, P("dp", "head"), P("dp", "head"), P(), P()),
        out_specs=(rows, rows),
        check_vma=False,
    )
```

```python
import functools
import math

import jax
import jax.numpy as jnp
from jax import lax
from jax.experimental import pallas as pl
from jax.experimental.pallas import tpu as pltpu
from jax.sharding import PartitionSpec as P

HEAD_WIDTH = 128
SPAN = 128
LOG2E = 1.4426950408889634
MASKED = -1e30


def prepare_kernel(order_ref, keep_ref, *refs, groups, per_step, kv_local, sources, ctx_size, head_size):
    refs = list(refs)
    scale_in = [refs.pop(0) for _ in range(head_size)]
    q_ref, qa_ref, mask_ref, key_scale_ref, value_scale_ref, scale_ref, scale_sem = refs
    step = pl.program_id(0)
    tokens = q_ref.shape[0]
    inverse_root = 1.0 / math.sqrt(HEAD_WIDTH)
    ctx, head = lax.axis_index("ctx"), lax.axis_index("head")
    starts = [
        ((ctx ^ flip) * head_size + lax.rem(head - shift + head_size, head_size)) * tokens
        for flip, shift in sources
    ]
    spans = [start // SPAN for start in starts]
    row = lax.broadcasted_iota(jnp.int32, (tokens, SPAN), 0)
    lane = lax.broadcasted_iota(jnp.int32, (tokens, SPAN), 1)

    @pl.when(step == 0)
    def _():
        copies = []
        for shift in range(head_size):
            owner = lax.rem(head - shift + head_size, head_size)
            copies.append(
                pltpu.make_async_copy(scale_in[shift], scale_ref.at[owner], scale_sem.at[shift])
            )
        for copy in copies:
            copy.start()
        own_start = (ctx * head_size + head) * tokens
        own = own_start // SPAN
        for i, (start, span) in enumerate(zip(starts, spans)):
            seen = (order_ref[span] < order_ref[own]) & (keep_ref[own, span] > 0)
            whole = jnp.where(seen, 0.0, MASKED)
            causal = jnp.where(row + (start - own_start) <= lane, 0.0, MASKED)
            mask = jnp.where(own == span, causal, whole)
            mask_ref[i * tokens : (i + 1) * tokens, :] = mask.astype(jnp.bfloat16)
        for copy in copies:
            copy.wait()

    one_hot = jnp.where(row == lane, 1.0, 0.0).astype(jnp.bfloat16)
    for u in range(per_step):
        g = step * per_step + u
        owner, member = g // kv_local, g % kv_local
        for h in range(groups):
            at = (u * groups + h) * HEAD_WIDTH
            qa_ref[u, h * tokens : (h + 1) * tokens, :HEAD_WIDTH] = q_ref[:, at : at + HEAD_WIDTH]
            qa_ref[u, h * tokens : (h + 1) * tokens, HEAD_WIDTH:] = one_hot
        for i, span in enumerate(spans):
            factor = scale_ref[owner, member, span] * (inverse_root * LOG2E)
            key_scale_ref[u, i : i + 1, :] = jnp.full((1, SPAN), factor, jnp.float32)
            factor = scale_ref[owner, kv_local + member, span]
            value_scale_ref[u, i : i + 1, :] = jnp.full((1, SPAN), factor, jnp.float32)


def prepare(queries, scales, span_order, block_keep, sources, kv_heads, kv_local, sizes):
    tokens, width = queries.shape
    groups = width // HEAD_WIDTH // kv_heads
    per_step = 2 if kv_heads % 2 == 0 else 1
    rows = groups * tokens
    smem = pl.BlockSpec(memory_space=pltpu.SMEM)
    scale_rows = pl.BlockSpec((per_step, len(sources), SPAN), lambda s: (s, 0, 0))
    return pl.pallas_call(
        functools.partial(
            prepare_kernel,
            groups=groups,
            per_step=per_step,
            kv_local=kv_local,
            sources=sources,
            ctx_size=sizes[0],
            head_size=sizes[1],
        ),
        grid=(kv_heads // per_step,),
        in_specs=[smem, smem]
        + [pl.BlockSpec(memory_space=pl.ANY)] * len(scales)
        + [pl.BlockSpec((tokens, per_step * groups * HEAD_WIDTH), lambda s: (0, s))],
        out_specs=[
            pl.BlockSpec((per_step, rows, HEAD_WIDTH + SPAN), lambda s: (s, 0, 0)),
            pl.BlockSpec((tokens * len(sources), SPAN), lambda s: (0, 0)),
            scale_rows,
            scale_rows,
        ],
        out_shape=[
            jax.ShapeDtypeStruct((kv_heads, rows, HEAD_WIDTH + SPAN), jnp.bfloat16),
            jax.ShapeDtypeStruct((tokens * len(sources), SPAN), jnp.bfloat16),
            jax.ShapeDtypeStruct((kv_heads, len(sources), SPAN), jnp.float32),
            jax.ShapeDtypeStruct((kv_heads, len(sources), SPAN), jnp.float32),
        ],
        scratch_shapes=[
            pltpu.SMEM((len(scales),) + scales[0].shape, jnp.float32),
            pltpu.SemaphoreType.DMA((len(scales),)),
        ],
        compiler_params=pltpu.CompilerParams(vmem_limit_bytes=32 * 1024 * 1024),
        cost_estimate=pl.CostEstimate(
            flops=8 * tokens * width, bytes_accessed=16 * tokens * width, transcendentals=0
        ),
    )(span_order, block_keep, *scales, queries)


def absorb_kernel(*refs, groups, tokens, per_step, begin, count, first, last):
    refs = list(refs)
    pieces = [refs.pop(0) for _ in range(count)]
    qa_ref, mask_ref, key_scale_ref, value_scale_ref = [refs.pop(0) for _ in range(4)]
    mixed_in, stats_in = (None, None) if first else (refs.pop(0), refs.pop(0))
    result_ref, stats_ref, x_ref, p_ref, check_ref = refs
    step = pl.program_id(0)
    inverse_root = 1.0 / math.sqrt(HEAD_WIDTH)
    for u in range(per_step):
        g = step * per_step + u
        cols = pl.ds(pl.multiple_of(g * HEAD_WIDTH, HEAD_WIDTH), HEAD_WIDTH)
        k = jnp.concatenate([piece[:tokens, cols] for piece in pieces], axis=0)
        k = jnp.concatenate([k, mask_ref[begin * tokens : (begin + count) * tokens, :]], axis=1)
        x_ref[u] = lax.dot_general(
            k, qa_ref[u], (((1,), (1,)), ((), ())), preferred_element_type=jnp.float32
        )
    for u in range(per_step):
        g = step * per_step + u
        cols = pl.ds(pl.multiple_of(g * HEAD_WIDTH, HEAD_WIDTH), HEAD_WIDTH)
        factors = [key_scale_ref[u, begin + i : begin + i + 1, :] for i in range(count)]
        high, low = [], []
        for i, piece in enumerate(pieces):
            factor = value_scale_ref[u, begin + i : begin + i + 1, :]
            v = piece[tokens:, cols].astype(jnp.float32) * factor
            high.append(v.astype(jnp.bfloat16))
            low.append((v - high[-1].astype(jnp.float32)).astype(jnp.bfloat16))
        v = jnp.concatenate(
            [jnp.concatenate(high, axis=0), jnp.concatenate(low, axis=0)], axis=1
        )
        tops, totals, fades = [], [], []
        for tile in range(groups * tokens // SPAN):
            lanes = slice(tile * SPAN, (tile + 1) * SPAN)
            top = None
            for i, factor in enumerate(factors):
                x = x_ref[u, i * tokens : (i + 1) * tokens, lanes]
                highest = jnp.max(x.reshape(tokens // 8, 8, SPAN), axis=0) * factor
                top = highest if top is None else jnp.maximum(top, highest)
            top = jnp.max(top, axis=0, keepdims=True)
            if not first:
                before = stats_in[u, 0:1, lanes]
                top = jnp.maximum(top, before)
                fades.append(jnp.exp2(before - top))
            total = None
            for i, factor in enumerate(factors):
                keys = slice(i * tokens, (i + 1) * tokens)
                weight = jnp.exp2(x_ref[u, keys, lanes] * factor - top)
                p_ref[u, keys, lanes] = weight.astype(jnp.bfloat16)
                part = jnp.sum(weight.reshape(tokens // 8, 8, SPAN), axis=0)
                total = part if total is None else total + part
            total = jnp.sum(total, axis=0, keepdims=True)
            if not first:
                total = total + fades[tile] * stats_in[u, 1:2, lanes]
            tops.append(top)
            totals.append(total)
        both = lax.dot_general(
            v, p_ref[u], (((0,), (0,)), ((), ())), preferred_element_type=jnp.float32
        )
        for tile in range(groups * tokens // SPAN):
            lanes = slice(tile * SPAN, (tile + 1) * SPAN)
            mixed = both[:HEAD_WIDTH, lanes] + both[HEAD_WIDTH:, lanes]
            if not first:
                mixed = mixed + fades[tile] * mixed_in[u, :, lanes]
            if not last:
                result_ref[u, :, lanes] = mixed
                stats_ref[u, 0:1, lanes] = tops[tile]
                stats_ref[u, 1:2, lanes] = totals[tile]
                continue
            mixed = mixed * (1.0 / totals[tile])
            check = jnp.sum(mixed, axis=0, keepdims=True) * inverse_root
            mixed = jnp.transpose(mixed).astype(result_ref.dtype)
            for j in range(SPAN // tokens):
                h = tile * (SPAN // tokens) + j
                at = (u * groups + h) * HEAD_WIDTH
                result_ref[:, at : at + HEAD_WIDTH] = mixed[j * tokens : (j + 1) * tokens]
                check_ref[pl.ds(g * groups + h, 1), :] = check[:, j * tokens : (j + 1) * tokens]
    if last:

        @pl.when(step == pl.num_programs(0) - 1)
        def _():
            stats_ref[...] = jnp.transpose(check_ref[...])


def absorb(prepared, pieces, begin, state, last, tokens):
    kv_heads, rows, depth = prepared[0].shape
    groups = rows // tokens
    count = len(pieces)
    per_step = 2 if kv_heads % 2 == 0 else 1
    keys = tokens * count
    width = kv_heads * groups * HEAD_WIDTH
    first = state is None
    mixed = pl.BlockSpec((per_step, HEAD_WIDTH, rows), lambda s: (s, 0, 0))
    stats = pl.BlockSpec((per_step, 2, rows), lambda s: (s, 0, 0))
    scale_rows = pl.BlockSpec((per_step,) + prepared[2].shape[1:], lambda s: (s, 0, 0))
    in_specs = [pl.BlockSpec(piece.shape, lambda s: (0, 0)) for piece in pieces]
    in_specs += [
        pl.BlockSpec((per_step, rows, depth), lambda s: (s, 0, 0)),
        pl.BlockSpec(prepared[1].shape, lambda s: (0, 0)),
        scale_rows,
        scale_rows,
    ]
    in_specs += [] if first else [mixed, stats]
    if last:
        out_specs = [
            pl.BlockSpec((tokens, per_step * groups * HEAD_WIDTH), lambda s: (0, s)),
            pl.BlockSpec((tokens, kv_heads * groups), lambda s: (0, 0)),
        ]
        out_shape = [
            jax.ShapeDtypeStruct((tokens, width), jnp.bfloat16),
            jax.ShapeDtypeStruct((tokens, kv_heads * groups), jnp.float32),
        ]
    else:
        out_specs = [mixed, stats]
        out_shape = [
            jax.ShapeDtypeStruct((kv_heads, HEAD_WIDTH, rows), jnp.float32),
            jax.ShapeDtypeStruct((kv_heads, 2, rows), jnp.float32),
        ]
    return pl.pallas_call(
        functools.partial(
            absorb_kernel,
            groups=groups,
            tokens=tokens,
            per_step=per_step,
            begin=begin,
            count=count,
            first=first,
            last=last,
        ),
        grid=(kv_heads // per_step,),
        in_specs=in_specs,
        out_specs=out_specs,
        out_shape=out_shape,
        scratch_shapes=[
            pltpu.VMEM((per_step, keys, rows), jnp.float32),
            pltpu.VMEM((per_step, keys, rows), jnp.bfloat16),
            pltpu.VMEM((kv_heads * groups, tokens), jnp.float32),
        ],
        compiler_params=pltpu.CompilerParams(vmem_limit_bytes=32 * 1024 * 1024),
        cost_estimate=pl.CostEstimate(
            flops=16 * tokens * width * keys,
            bytes_accessed=16 * tokens * width,
            transcendentals=tokens * width // HEAD_WIDTH * keys,
        ),
    )(*pieces, *prepared, *(() if first else state))


def local(queries, keys, values, key_scale, value_scale, span_order, block_keep):
    tokens = queries.shape[0]
    kv_heads = keys.shape[1] // HEAD_WIDTH
    ctx_size, head_size = lax.axis_size("ctx"), lax.axis_size("head")
    levels = ctx_size.bit_length() - 1
    batch = 2 * SPAN // tokens

    def along_head(block, distance):
        return lax.ppermute(block, "head", [(i, (i + distance) % head_size) for i in range(head_size)])

    def across_ctx(block, flip):
        return lax.ppermute(block, "ctx", [(i, i ^ flip) for i in range(ctx_size)])

    plan, arrived = [[(0, 0, -1)]], [(0, 0, -1)]
    while arrived:
        coming = []
        for index, (flip, shift, level) in enumerate(arrived):
            if level < 0 and shift + 1 < head_size:
                coming.append((flip, shift + 1, level, index, 0))
            for later in range(level + 1, levels):
                bit = ctx_size >> (later + 1)
                coming.append((flip ^ bit, shift, later, index, bit))
        if coming:
            plan.append(coming)
        arrived = [source[:3] for source in coming]
    sources = [source[:2] for phase in plan for source in phase]

    scale = jnp.concatenate([jnp.transpose(key_scale), jnp.transpose(value_scale)], axis=0)
    scales = [scale] + [along_head(scale, shift) for shift in range(1, head_size)]
    block = jnp.concatenate([keys, values], axis=0)
    block, scales = lax.optimization_barrier((block, scales))
    arrived, pieces, done = [block], [block], 0
    prepared, state = None, None
    for phase, routes in enumerate(plan[1:]):
        coming = [
            across_ctx(arrived[index], bit) if bit else along_head(arrived[index], 1)
            for _, _, _, index, bit in routes
        ]
        if phase == 0:
            prepared = prepare(
                queries,
                scales,
                span_order,
                block_keep,
                sources,
                kv_heads,
                key_scale.shape[1],
                (ctx_size, head_size),
            )
        elif phase > 1:
            ready = (len(pieces) - done) // batch * batch
            if ready:
                state = absorb(prepared, pieces[done : done + ready], done, state, False, tokens)
                done += ready
        arrived, prepared, state = lax.optimization_barrier((coming, prepared, state))
        pieces = pieces + list(arrived)
    return tuple(absorb(prepared, pieces[done:], done, state, True, tokens))


def solution(mesh):
    rows = P(("dp", "ctx", "head"), None)
    return jax.shard_map(
        local,
        mesh=mesh,
        in_specs=(rows, rows, rows, P("dp", "head"), P("dp", "head"), P(), P()),
        out_specs=(rows, rows),
        check_vma=False,
    )
```

```python
import functools
import math

import jax
import jax.numpy as jnp
from jax import lax
from jax.experimental import pallas as pl
from jax.experimental.pallas import tpu as pltpu
from jax.sharding import PartitionSpec as P

HEAD_WIDTH = 128
SPAN = 128
LOG2E = 1.4426950408889634
MASKED = -1e30


def prepare_kernel(order_ref, keep_ref, *refs, groups, per_step, kv_local, sources, ctx_size, head_size):
    refs = list(refs)
    scale_in = [refs.pop(0) for _ in range(head_size)]
    q_ref, qa_ref, mask_ref, key_scale_ref, value_scale_ref, scale_ref, scale_sem = refs
    step = pl.program_id(0)
    tokens = q_ref.shape[0]
    inverse_root = 1.0 / math.sqrt(HEAD_WIDTH)
    ctx, head = lax.axis_index("ctx"), lax.axis_index("head")
    starts = [
        ((ctx ^ flip) * head_size + lax.rem(head - shift + head_size, head_size)) * tokens
        for flip, shift in sources
    ]
    spans = [start // SPAN for start in starts]
    row = lax.broadcasted_iota(jnp.int32, (tokens, SPAN), 0)
    lane = lax.broadcasted_iota(jnp.int32, (tokens, SPAN), 1)

    @pl.when(step == 0)
    def _():
        copies = []
        for shift in range(head_size):
            owner = lax.rem(head - shift + head_size, head_size)
            copies.append(
                pltpu.make_async_copy(scale_in[shift], scale_ref.at[owner], scale_sem.at[shift])
            )
        for copy in copies:
            copy.start()
        own_start = (ctx * head_size + head) * tokens
        own = own_start // SPAN
        for i, (start, span) in enumerate(zip(starts, spans)):
            seen = (order_ref[span] < order_ref[own]) & (keep_ref[own, span] > 0)
            whole = jnp.where(seen, 0.0, MASKED)
            causal = jnp.where(row + (start - own_start) <= lane, 0.0, MASKED)
            mask = jnp.where(own == span, causal, whole)
            mask_ref[i * tokens : (i + 1) * tokens, :] = mask.astype(jnp.bfloat16)
        for copy in copies:
            copy.wait()

    one_hot = jnp.where(row == lane, 1.0, 0.0).astype(jnp.bfloat16)
    for u in range(per_step):
        g = step * per_step + u
        owner, member = g // kv_local, g % kv_local
        for h in range(groups):
            at = (u * groups + h) * HEAD_WIDTH
            qa_ref[u, h * tokens : (h + 1) * tokens, :HEAD_WIDTH] = q_ref[:, at : at + HEAD_WIDTH]
            qa_ref[u, h * tokens : (h + 1) * tokens, HEAD_WIDTH:] = one_hot
        for i, span in enumerate(spans):
            factor = scale_ref[owner, member, span] * (inverse_root * LOG2E)
            key_scale_ref[u, i : i + 1, :] = jnp.full((1, SPAN), factor, jnp.float32)
            factor = scale_ref[owner, kv_local + member, span]
            value_scale_ref[u, i : i + 1, :] = jnp.full((1, SPAN), factor, jnp.float32)


def prepare(queries, scales, span_order, block_keep, sources, kv_heads, kv_local, sizes):
    tokens, width = queries.shape
    groups = width // HEAD_WIDTH // kv_heads
    per_step = 2 if kv_heads % 2 == 0 else 1
    rows = groups * tokens
    smem = pl.BlockSpec(memory_space=pltpu.SMEM)
    scale_rows = pl.BlockSpec((per_step, len(sources), SPAN), lambda s: (s, 0, 0))
    return pl.pallas_call(
        functools.partial(
            prepare_kernel,
            groups=groups,
            per_step=per_step,
            kv_local=kv_local,
            sources=sources,
            ctx_size=sizes[0],
            head_size=sizes[1],
        ),
        grid=(kv_heads // per_step,),
        in_specs=[smem, smem]
        + [pl.BlockSpec(memory_space=pl.ANY)] * len(scales)
        + [pl.BlockSpec((tokens, per_step * groups * HEAD_WIDTH), lambda s: (0, s))],
        out_specs=[
            pl.BlockSpec((per_step, rows, HEAD_WIDTH + SPAN), lambda s: (s, 0, 0)),
            pl.BlockSpec((tokens * len(sources), SPAN), lambda s: (0, 0)),
            scale_rows,
            scale_rows,
        ],
        out_shape=[
            jax.ShapeDtypeStruct((kv_heads, rows, HEAD_WIDTH + SPAN), jnp.bfloat16),
            jax.ShapeDtypeStruct((tokens * len(sources), SPAN), jnp.bfloat16),
            jax.ShapeDtypeStruct((kv_heads, len(sources), SPAN), jnp.float32),
            jax.ShapeDtypeStruct((kv_heads, len(sources), SPAN), jnp.float32),
        ],
        scratch_shapes=[
            pltpu.SMEM((len(scales),) + scales[0].shape, jnp.float32),
            pltpu.SemaphoreType.DMA((len(scales),)),
        ],
        compiler_params=pltpu.CompilerParams(vmem_limit_bytes=32 * 1024 * 1024),
        cost_estimate=pl.CostEstimate(
            flops=8 * tokens * width, bytes_accessed=16 * tokens * width, transcendentals=0
        ),
    )(span_order, block_keep, *scales, queries)


def absorb_kernel(*refs, groups, tokens, per_step, begin, count, first, last, head_step, merge):
    refs = list(refs)
    pieces = [refs.pop(0) for _ in range(count)]
    qa_ref, mask_ref, key_scale_ref, value_scale_ref = [refs.pop(0) for _ in range(4)]
    mixed_in, stats_in = (None, None) if first else (refs.pop(0), refs.pop(0))
    checks_in = (refs.pop(0), refs.pop(0))[1] if merge else None
    result_ref, stats_ref, x_ref, p_ref, check_ref = refs
    step = pl.program_id(0)
    inverse_root = 1.0 / math.sqrt(HEAD_WIDTH)
    for u in range(per_step):
        g = step * per_step + u
        cols = pl.ds(pl.multiple_of(g * HEAD_WIDTH, HEAD_WIDTH), HEAD_WIDTH)
        k = jnp.concatenate([piece[:tokens, cols] for piece in pieces], axis=0)
        k = jnp.concatenate([k, mask_ref[begin * tokens : (begin + count) * tokens, :]], axis=1)
        x_ref[u] = lax.dot_general(
            k, qa_ref[u], (((1,), (1,)), ((), ())), preferred_element_type=jnp.float32
        )
    for u in range(per_step):
        g = step * per_step + u
        cols = pl.ds(pl.multiple_of(g * HEAD_WIDTH, HEAD_WIDTH), HEAD_WIDTH)
        factors = [key_scale_ref[u, begin + i : begin + i + 1, :] for i in range(count)]
        high, low = [], []
        for i, piece in enumerate(pieces):
            factor = value_scale_ref[u, begin + i : begin + i + 1, :]
            v = piece[tokens:, cols].astype(jnp.float32) * factor
            high.append(v.astype(jnp.bfloat16))
            low.append((v - high[-1].astype(jnp.float32)).astype(jnp.bfloat16))
        v = jnp.concatenate(
            [jnp.concatenate(high, axis=0), jnp.concatenate(low, axis=0)], axis=1
        )
        tops, totals, fades = [], [], []
        for tile in range(groups * tokens // SPAN):
            lanes = slice(tile * SPAN, (tile + 1) * SPAN)
            top = None
            for i, factor in enumerate(factors):
                x = x_ref[u, i * tokens : (i + 1) * tokens, lanes]
                highest = jnp.max(x.reshape(tokens // 8, 8, SPAN), axis=0) * factor
                top = highest if top is None else jnp.maximum(top, highest)
            top = jnp.max(top, axis=0, keepdims=True)
            if not first:
                before = stats_in[u, 0:1, lanes]
                top = jnp.maximum(top, before)
                fades.append(jnp.exp2(before - top))
            total = None
            for i, factor in enumerate(factors):
                keys = slice(i * tokens, (i + 1) * tokens)
                weight = jnp.exp2(x_ref[u, keys, lanes] * factor - top)
                p_ref[u, keys, lanes] = weight.astype(jnp.bfloat16)
                part = jnp.sum(weight.reshape(tokens // 8, 8, SPAN), axis=0)
                total = part if total is None else total + part
            total = jnp.sum(total, axis=0, keepdims=True)
            if not first:
                total = total + fades[tile] * stats_in[u, 1:2, lanes]
            tops.append(top)
            totals.append(total)
        both = lax.dot_general(
            v, p_ref[u], (((0,), (0,)), ((), ())), preferred_element_type=jnp.float32
        )
        for tile in range(groups * tokens // SPAN):
            lanes = slice(tile * SPAN, (tile + 1) * SPAN)
            mixed = both[:HEAD_WIDTH, lanes] + both[HEAD_WIDTH:, lanes]
            if not first:
                mixed = mixed + fades[tile] * mixed_in[u, :, lanes]
            if not last:
                result_ref[u, :, lanes] = mixed
                stats_ref[u, 0:1, lanes] = tops[tile]
                stats_ref[u, 1:2, lanes] = totals[tile]
                continue
            mixed = mixed * (1.0 / totals[tile])
            check = jnp.sum(mixed, axis=0, keepdims=True) * inverse_root
            mixed = jnp.transpose(mixed).astype(result_ref.dtype)
            for j in range(SPAN // tokens):
                h = tile * (SPAN // tokens) + j
                at = (u * groups + h) * HEAD_WIDTH
                result_ref[:, at : at + HEAD_WIDTH] = mixed[j * tokens : (j + 1) * tokens]
                check_ref[pl.ds((head_step * per_step + g) * groups + h, 1), :] = check[:, j * tokens : (j + 1) * tokens]
    if last:

        @pl.when(step == pl.num_programs(0) - 1)
        def _():
            lane = lax.broadcasted_iota(jnp.int32, stats_ref.shape, 1)
            checks = jnp.transpose(check_ref[...])
            if merge:
                checks = jnp.where(lane < head_step * per_step * groups, checks_in[...], checks)
            stats_ref[...] = checks


def absorb(prepared, pieces, begin, state, tokens, stream, streams, last, before):
    kv_heads, rows, depth = prepared[0].shape
    groups = rows // tokens
    count = len(pieces)
    own_heads = kv_heads // streams
    per_step = 2 if own_heads % 2 == 0 else 1
    head_step = stream * own_heads // per_step
    keys = tokens * count
    width = kv_heads * groups * HEAD_WIDTH
    first, merge = state is None, before is not None
    mixed = pl.BlockSpec((per_step, HEAD_WIDTH, rows), lambda s: (s, 0, 0))
    stats = pl.BlockSpec((per_step, 2, rows), lambda s: (s, 0, 0))
    scale_rows = pl.BlockSpec((per_step,) + prepared[2].shape[1:], lambda s: (s + head_step, 0, 0))
    checks = pl.BlockSpec((tokens, kv_heads * groups), lambda s: (0, 0))
    in_specs = [pl.BlockSpec(piece.shape, lambda s: (0, 0)) for piece in pieces]
    in_specs += [
        pl.BlockSpec((per_step, rows, depth), lambda s: (s + head_step, 0, 0)),
        pl.BlockSpec(prepared[1].shape, lambda s: (0, 0)),
        scale_rows,
        scale_rows,
    ]
    in_specs += [] if first else [mixed, stats]
    aliases = {}
    if merge:
        aliases = {len(in_specs): 0}
        in_specs += [pl.BlockSpec(memory_space=pl.ANY), checks]
    if last:
        out_specs = [
            pl.BlockSpec((tokens, per_step * groups * HEAD_WIDTH), lambda s: (0, s + head_step)),
            checks,
        ]
        out_shape = [
            jax.ShapeDtypeStruct((tokens, width), jnp.bfloat16),
            jax.ShapeDtypeStruct((tokens, kv_heads * groups), jnp.float32),
        ]
    else:
        out_specs = [mixed, stats]
        out_shape = [
            jax.ShapeDtypeStruct((own_heads, HEAD_WIDTH, rows), jnp.float32),
            jax.ShapeDtypeStruct((own_heads, 2, rows), jnp.float32),
        ]
    return pl.pallas_call(
        functools.partial(
            absorb_kernel,
            groups=groups,
            tokens=tokens,
            per_step=per_step,
            begin=begin,
            count=count,
            first=first,
            last=last,
            head_step=head_step,
            merge=merge,
        ),
        grid=(own_heads // per_step,),
        in_specs=in_specs,
        out_specs=out_specs,
        out_shape=out_shape,
        input_output_aliases=aliases,
        scratch_shapes=[
            pltpu.VMEM((per_step, keys, rows), jnp.float32),
            pltpu.VMEM((per_step, keys, rows), jnp.bfloat16),
            pltpu.VMEM((kv_heads * groups, tokens), jnp.float32),
        ],
        compiler_params=pltpu.CompilerParams(vmem_limit_bytes=32 * 1024 * 1024),
        cost_estimate=pl.CostEstimate(
            flops=16 * tokens * width * keys // streams,
            bytes_accessed=16 * tokens * width // streams,
            transcendentals=tokens * width // HEAD_WIDTH * keys // streams,
        ),
    )(*pieces, *prepared, *(() if first else state), *(before if merge else ()))


def local(queries, keys, values, key_scale, value_scale, span_order, block_keep):
    tokens = queries.shape[0]
    kv_heads = keys.shape[1] // HEAD_WIDTH
    ctx_size, head_size = lax.axis_size("ctx"), lax.axis_size("head")
    levels = ctx_size.bit_length() - 1
    batch = 2 * SPAN // tokens

    def along_head(block, distance):
        return lax.ppermute(block, "head", [(i, (i + distance) % head_size) for i in range(head_size)])

    def across_ctx(block, flip):
        return lax.ppermute(block, "ctx", [(i, i ^ flip) for i in range(ctx_size)])

    plan, arrived = [[(0, 0, -1)]], [(0, 0, -1)]
    while arrived:
        coming = []
        for index, (flip, shift, level) in enumerate(arrived):
            if level < 0 and shift + 1 < head_size:
                coming.append((flip, shift + 1, level, index, 0))
            for later in range(level + 1, levels):
                bit = ctx_size >> (later + 1)
                coming.append((flip ^ bit, shift, later, index, bit))
        if coming:
            plan.append(coming)
        arrived = [source[:3] for source in coming]
    sources = [source[:2] for phase in plan for source in phase]

    scale = jnp.concatenate([jnp.transpose(key_scale), jnp.transpose(value_scale)], axis=0)
    scales = [scale] + [along_head(scale, shift) for shift in range(1, head_size)]
    streams = 2 if kv_heads % 2 == 0 else 1
    part = keys.shape[1] // streams
    cuts = [slice(i * part, (i + 1) * part) for i in range(streams)]
    blocks = [jnp.concatenate([keys[:, cut], values[:, cut]], axis=0) for cut in cuts]
    blocks, scales = lax.optimization_barrier((blocks, scales))
    arrived = [[block] for block in blocks]
    pieces = [[block] for block in blocks]
    done, state = [0] * streams, [None] * streams
    prepared, result = None, None
    for phase, routes in enumerate(plan[1:]):
        for i in range(streams):
            coming = [
                across_ctx(arrived[i][index], bit) if bit else along_head(arrived[i][index], 1)
                for _, _, _, index, bit in routes
            ]
            if phase == 0 and i == 0:
                prepared = prepare(
                    queries,
                    scales,
                    span_order,
                    block_keep,
                    sources,
                    kv_heads,
                    key_scale.shape[1],
                    (ctx_size, head_size),
                )
            elif phase > 1:
                ready = (len(pieces[i]) - done[i]) // batch * batch
                if ready:
                    now = pieces[i][done[i] : done[i] + ready]
                    state[i] = absorb(prepared, now, done[i], state[i], tokens, i, streams, False, None)
                    done[i] += ready
            arrived[i], prepared, state[i] = lax.optimization_barrier((coming, prepared, state[i]))
            pieces[i] = pieces[i] + list(arrived[i])
    for i in range(streams):
        now = pieces[i][done[i] :]
        result = absorb(prepared, now, done[i], state[i], tokens, i, streams, True, result)
    return tuple(result)


def solution(mesh):
    rows = P(("dp", "ctx", "head"), None)
    return jax.shard_map(
        local,
        mesh=mesh,
        in_specs=(rows, rows, rows, P("dp", "head"), P("dp", "head"), P(), P()),
        out_specs=(rows, rows),
        check_vma=False,
    )
```

```python
import functools
import math

import jax
import jax.numpy as jnp
from jax import lax
from jax.experimental import pallas as pl
from jax.experimental.pallas import tpu as pltpu
from jax.sharding import PartitionSpec as P

HEAD_WIDTH = 128
SPAN = 128
LOG2E = 1.4426950408889634
MASKED = -1e30


def source_start(distance, flip, tokens, ctx_size, head_size):
    ctx, head = lax.axis_index("ctx"), lax.axis_index("head")
    size = ctx_size // 2 * head_size
    row = ctx // 2
    place = row * head_size + jnp.where(row % 2 == 0, head, head_size - 1 - head)
    place = lax.rem(place - distance + size, size)
    row, column = place // head_size, place % head_size
    column = jnp.where(row % 2 == 0, column, head_size - 1 - column)
    return ((2 * row + (ctx % 2) ^ flip) * head_size + column) * tokens


def prepare_kernel(order_ref, keep_ref, q_ref, qa_ref, mask_ref, *, groups, per_step, sources, ctx_size, head_size):
    step = pl.program_id(0)
    tokens = q_ref.shape[0]
    row = lax.broadcasted_iota(jnp.int32, (tokens, SPAN), 0)
    lane = lax.broadcasted_iota(jnp.int32, (tokens, SPAN), 1)

    @pl.when(step == 0)
    def _():
        own_start = source_start(0, 0, tokens, ctx_size, head_size)
        own = own_start // SPAN
        for i, source in enumerate(sources):
            start = source_start(*source, tokens, ctx_size, head_size)
            span = start // SPAN
            seen = (order_ref[span] < order_ref[own]) & (keep_ref[own, span] > 0)
            whole = jnp.where(seen, 0.0, MASKED)
            causal = jnp.where(row + (start - own_start) <= lane, 0.0, MASKED)
            mask = jnp.where(own == span, causal, whole)
            mask_ref[i * tokens : (i + 1) * tokens, :] = mask.astype(jnp.bfloat16)

    one_hot = jnp.where(row == lane, 1.0, 0.0).astype(jnp.bfloat16)
    for u in range(per_step):
        for h in range(groups):
            at = (u * groups + h) * HEAD_WIDTH
            qa_ref[u, h * tokens : (h + 1) * tokens, :HEAD_WIDTH] = q_ref[:, at : at + HEAD_WIDTH]
            qa_ref[u, h * tokens : (h + 1) * tokens, HEAD_WIDTH:] = one_hot


def prepare(queries, span_order, block_keep, sources, kv_heads, sizes):
    tokens, width = queries.shape
    groups = width // HEAD_WIDTH // kv_heads
    per_step = 2 if kv_heads % 2 == 0 else 1
    rows = groups * tokens
    smem = pl.BlockSpec(memory_space=pltpu.SMEM)
    return pl.pallas_call(
        functools.partial(
            prepare_kernel,
            groups=groups,
            per_step=per_step,
            sources=sources,
            ctx_size=sizes[0],
            head_size=sizes[1],
        ),
        grid=(kv_heads // per_step,),
        in_specs=[smem, smem, pl.BlockSpec((tokens, per_step * groups * HEAD_WIDTH), lambda s: (0, s))],
        out_specs=[
            pl.BlockSpec((per_step, rows, HEAD_WIDTH + SPAN), lambda s: (s, 0, 0)),
            pl.BlockSpec((tokens * len(sources), SPAN), lambda s: (0, 0)),
        ],
        out_shape=[
            jax.ShapeDtypeStruct((kv_heads, rows, HEAD_WIDTH + SPAN), jnp.bfloat16),
            jax.ShapeDtypeStruct((tokens * len(sources), SPAN), jnp.bfloat16),
        ],
        compiler_params=pltpu.CompilerParams(vmem_limit_bytes=32 * 1024 * 1024),
        cost_estimate=pl.CostEstimate(
            flops=8 * tokens * width, bytes_accessed=16 * tokens * width, transcendentals=0
        ),
    )(span_order, block_keep, queries)


def scale_rows_kernel(*refs, tokens, kv_local, sources, ctx_size, head_size):
    scale_in = refs[:head_size]
    key_scale_ref, value_scale_ref, scale_ref, scale_sem = refs[head_size:]
    inverse_root = 1.0 / math.sqrt(HEAD_WIDTH)
    head = lax.axis_index("head")
    copies = []
    for shift in range(head_size):
        owner = lax.rem(head - shift + head_size, head_size)
        copies.append(
            pltpu.make_async_copy(scale_in[shift], scale_ref.at[owner], scale_sem.at[shift])
        )
    for copy in copies:
        copy.start()
    spans = [
        source_start(*source, tokens, ctx_size, head_size) // SPAN for source in sources
    ]
    for copy in copies:
        copy.wait()
    for g in range(head_size * kv_local):
        owner, member = g // kv_local, g % kv_local
        for i, span in enumerate(spans):
            factor = scale_ref[owner, member, span] * (inverse_root * LOG2E)
            key_scale_ref[g, i : i + 1, :] = jnp.full((1, SPAN), factor, jnp.float32)
            factor = scale_ref[owner, kv_local + member, span]
            value_scale_ref[g, i : i + 1, :] = jnp.full((1, SPAN), factor, jnp.float32)


def scale_rows(scales, sources, tokens, sizes):
    kv_local = scales[0].shape[0] // 2
    shape = (sizes[1] * kv_local, len(sources), SPAN)
    return pl.pallas_call(
        functools.partial(
            scale_rows_kernel,
            tokens=tokens,
            kv_local=kv_local,
            sources=sources,
            ctx_size=sizes[0],
            head_size=sizes[1],
        ),
        in_specs=[pl.BlockSpec(memory_space=pl.ANY)] * len(scales),
        out_specs=[pl.BlockSpec(memory_space=pltpu.VMEM)] * 2,
        out_shape=[jax.ShapeDtypeStruct(shape, jnp.float32)] * 2,
        scratch_shapes=[
            pltpu.SMEM((len(scales),) + scales[0].shape, jnp.float32),
            pltpu.SemaphoreType.DMA((len(scales),)),
        ],
        compiler_params=pltpu.CompilerParams(vmem_limit_bytes=32 * 1024 * 1024),
        cost_estimate=pl.CostEstimate(
            flops=10**8, bytes_accessed=10**6, transcendentals=0
        ),
    )(*scales)


def absorb_kernel(*refs, groups, tokens, per_step, begin, count, first, last):
    refs = list(refs)
    pieces = [(refs.pop(0), refs.pop(0)) for _ in range(count)]
    qa_ref, mask_ref, key_scale_ref, value_scale_ref = [refs.pop(0) for _ in range(4)]
    mixed_in, stats_in = (None, None) if first else (refs.pop(0), refs.pop(0))
    result_ref, stats_ref, x_ref, p_ref, check_ref = refs
    step = pl.program_id(0)
    inverse_root = 1.0 / math.sqrt(HEAD_WIDTH)
    for u in range(per_step):
        g = step * per_step + u
        cols = pl.ds(pl.multiple_of(g * HEAD_WIDTH, HEAD_WIDTH), HEAD_WIDTH)
        k = jnp.concatenate([key_ref[:, cols] for key_ref, _ in pieces], axis=0)
        k = jnp.concatenate([k, mask_ref[begin * tokens : (begin + count) * tokens, :]], axis=1)
        x_ref[u] = lax.dot_general(
            k, qa_ref[u], (((1,), (1,)), ((), ())), preferred_element_type=jnp.float32
        )
    for u in range(per_step):
        g = step * per_step + u
        cols = pl.ds(pl.multiple_of(g * HEAD_WIDTH, HEAD_WIDTH), HEAD_WIDTH)
        factors = [key_scale_ref[u, begin + i : begin + i + 1, :] for i in range(count)]
        high, low = [], []
        for i, (_, value_ref) in enumerate(pieces):
            factor = value_scale_ref[u, begin + i : begin + i + 1, :]
            v = value_ref[:, cols].astype(jnp.float32) * factor
            high.append(v.astype(jnp.bfloat16))
            low.append((v - high[-1].astype(jnp.float32)).astype(jnp.bfloat16))
        v = jnp.concatenate(
            [jnp.concatenate(high, axis=0), jnp.concatenate(low, axis=0)], axis=1
        )
        tops, totals, fades = [], [], []
        for tile in range(groups * tokens // SPAN):
            lanes = slice(tile * SPAN, (tile + 1) * SPAN)
            top = None
            for i, factor in enumerate(factors):
                x = x_ref[u, i * tokens : (i + 1) * tokens, lanes]
                highest = jnp.max(x.reshape(tokens // 8, 8, SPAN), axis=0) * factor
                top = highest if top is None else jnp.maximum(top, highest)
            top = jnp.max(top, axis=0, keepdims=True)
            if not first:
                before = stats_in[u, 0:1, lanes]
                top = jnp.maximum(top, before)
                fades.append(jnp.exp2(before - top))
            total = None
            for i, factor in enumerate(factors):
                keys = slice(i * tokens, (i + 1) * tokens)
                weight = jnp.exp2(x_ref[u, keys, lanes] * factor - top)
                p_ref[u, keys, lanes] = weight.astype(jnp.bfloat16)
                part = jnp.sum(weight.reshape(tokens // 8, 8, SPAN), axis=0)
                total = part if total is None else total + part
            total = jnp.sum(total, axis=0, keepdims=True)
            if not first:
                total = total + fades[tile] * stats_in[u, 1:2, lanes]
            tops.append(top)
            totals.append(total)
        both = lax.dot_general(
            v, p_ref[u], (((0,), (0,)), ((), ())), preferred_element_type=jnp.float32
        )
        for tile in range(groups * tokens // SPAN):
            lanes = slice(tile * SPAN, (tile + 1) * SPAN)
            mixed = both[:HEAD_WIDTH, lanes] + both[HEAD_WIDTH:, lanes]
            if not first:
                mixed = mixed + fades[tile] * mixed_in[u, :, lanes]
            if not last:
                result_ref[u, :, lanes] = mixed
                stats_ref[u, 0:1, lanes] = tops[tile]
                stats_ref[u, 1:2, lanes] = totals[tile]
                continue
            mixed = mixed * (1.0 / totals[tile])
            check = jnp.sum(mixed, axis=0, keepdims=True) * inverse_root
            mixed = jnp.transpose(mixed).astype(result_ref.dtype)
            for j in range(SPAN // tokens):
                h = tile * (SPAN // tokens) + j
                at = (u * groups + h) * HEAD_WIDTH
                result_ref[:, at : at + HEAD_WIDTH] = mixed[j * tokens : (j + 1) * tokens]
                check_ref[pl.ds(g * groups + h, 1), :] = check[:, j * tokens : (j + 1) * tokens]
    if last:

        @pl.when(step == pl.num_programs(0) - 1)
        def _():
            stats_ref[...] = jnp.transpose(check_ref[...])


def absorb(prepared, pieces, begin, state, last, tokens):
    kv_heads, rows, depth = prepared[0].shape
    groups = rows // tokens
    count = len(pieces)
    per_step = 2 if kv_heads % 2 == 0 else 1
    keys = tokens * count
    width = kv_heads * groups * HEAD_WIDTH
    first = state is None
    mixed = pl.BlockSpec((per_step, HEAD_WIDTH, rows), lambda s: (s, 0, 0))
    stats = pl.BlockSpec((per_step, 2, rows), lambda s: (s, 0, 0))
    scale_rows = pl.BlockSpec((per_step,) + prepared[2].shape[1:], lambda s: (s, 0, 0))
    in_specs, operands = [], []
    for piece in pieces:
        joined = len(piece) == 1
        half = (tokens, piece[0].shape[1])
        in_specs.append(pl.BlockSpec(half, lambda s: (0, 0)))
        in_specs.append(pl.BlockSpec(half, lambda s: (1, 0)) if joined else in_specs[-1])
        operands += [piece[0], piece[-1]]
    in_specs += [
        pl.BlockSpec((per_step, rows, depth), lambda s: (s, 0, 0)),
        pl.BlockSpec(prepared[1].shape, lambda s: (0, 0)),
        scale_rows,
        scale_rows,
    ]
    in_specs += [] if first else [mixed, stats]
    if last:
        out_specs = [
            pl.BlockSpec((tokens, per_step * groups * HEAD_WIDTH), lambda s: (0, s)),
            pl.BlockSpec((tokens, kv_heads * groups), lambda s: (0, 0)),
        ]
        out_shape = [
            jax.ShapeDtypeStruct((tokens, width), jnp.bfloat16),
            jax.ShapeDtypeStruct((tokens, kv_heads * groups), jnp.float32),
        ]
    else:
        out_specs = [mixed, stats]
        out_shape = [
            jax.ShapeDtypeStruct((kv_heads, HEAD_WIDTH, rows), jnp.float32),
            jax.ShapeDtypeStruct((kv_heads, 2, rows), jnp.float32),
        ]
    return pl.pallas_call(
        functools.partial(
            absorb_kernel,
            groups=groups,
            tokens=tokens,
            per_step=per_step,
            begin=begin,
            count=count,
            first=first,
            last=last,
        ),
        grid=(kv_heads // per_step,),
        in_specs=in_specs,
        out_specs=out_specs,
        out_shape=out_shape,
        scratch_shapes=[
            pltpu.VMEM((per_step, keys, rows), jnp.float32),
            pltpu.VMEM((per_step, keys, rows), jnp.bfloat16),
            pltpu.VMEM((kv_heads * groups, tokens), jnp.float32),
        ],
        compiler_params=pltpu.CompilerParams(vmem_limit_bytes=32 * 1024 * 1024),
        cost_estimate=pl.CostEstimate(
            flops=16 * tokens * width * keys,
            bytes_accessed=16 * tokens * width,
            transcendentals=tokens * width // HEAD_WIDTH * keys,
        ),
    )(*operands, *prepared, *(() if first else state))


def local(queries, keys, values, key_scale, value_scale, span_order, block_keep):
    tokens = queries.shape[0]
    kv_heads = keys.shape[1] // HEAD_WIDTH
    sizes = ctx_size, head_size = lax.axis_size("ctx"), lax.axis_size("head")
    size = ctx_size // 2 * head_size
    batch = 2 * SPAN // tokens

    def device(place, core):
        row, column = place // head_size, place % head_size
        return (2 * row + core) * head_size + (column if row % 2 == 0 else head_size - 1 - column)

    def around(block, distance):
        route = [
            (device(p, core), device((p + distance) % size, core))
            for p in range(size)
            for core in range(2)
        ]
        return lax.ppermute(block, ("ctx", "head"), route)

    def to_other_core(piece):
        return [lax.ppermute(block, "ctx", [(i, i ^ 1) for i in range(ctx_size)]) for block in piece]

    def along_head(block, distance):
        return lax.ppermute(block, "head", [(i, (i + distance) % head_size) for i in range(head_size)])

    sources = [(0, 0)]
    for step in range(1, size // 2 + 2):
        if step < size // 2:
            sources += [(step, 0), (-step, 0)]
        elif step == size // 2:
            sources += [(step, 0)]
        if step == 1:
            sources += [(0, 1)]
        elif step <= size // 2:
            sources += [(step - 1, 1), (1 - step, 1)]
        else:
            sources += [(step - 1, 1)]

    block = jnp.concatenate([keys, values], axis=0)
    scale = jnp.concatenate([jnp.transpose(key_scale), jnp.transpose(value_scale)], axis=0)
    scales, pieces, done = [scale], [[block]], 0
    fresh, forward, backward = [[block]], block, block
    prepared, rows, state = None, None, None
    for step in range(1, size // 2 + 2):
        sent = []
        if step < size // 2:
            forward, backward = around(forward, 1), around(backward, -1)
            sent = [[forward], [backward]]
        elif step == size // 2:
            sent = [[around(forward[:tokens], 1), around(backward[tokens:], -1)]]
        coming = sent + [to_other_core(piece) for piece in fresh]
        complete = len(scales) == head_size
        if not complete:
            scales = scales + [along_head(scale, len(scales))]
        if step == 1:
            prepared = prepare(queries, span_order, block_keep, sources, kv_heads, sizes)
        if complete:
            if rows is None:
                rows = scale_rows(scales, sources, tokens, sizes)
            ready = (len(pieces) - done) // batch * batch
            if ready and step <= size // 2:
                now = pieces[done : done + ready]
                state = absorb((*prepared, *rows), now, done, state, False, tokens)
                done += ready
        coming, scales, prepared, rows, state = lax.optimization_barrier(
            (coming, scales, prepared, rows, state)
        )
        fresh = coming[: len(sent)]
        if step < size // 2:
            forward, backward = fresh[0][0], fresh[1][0]
        pieces = pieces + list(coming)
    return tuple(absorb((*prepared, *rows), pieces[done:], done, state, True, tokens))


def solution(mesh):
    rows = P(("dp", "ctx", "head"), None)
    return jax.shard_map(
        local,
        mesh=mesh,
        in_specs=(rows, rows, rows, P("dp", "head"), P("dp", "head"), P(), P()),
        out_specs=(rows, rows),
        check_vma=False,
    )
```

```python
import functools
import math

import jax
import jax.numpy as jnp
from jax import lax
from jax.experimental import pallas as pl
from jax.experimental.pallas import tpu as pltpu
from jax.sharding import PartitionSpec as P

HEAD_WIDTH = 128
SPAN = 128
LOG2E = 1.4426950408889634
MASKED = -1e30


def source_start(distance, flip, tokens, ctx_size, head_size):
    ctx, head = lax.axis_index("ctx"), lax.axis_index("head")
    size = ctx_size // 2 * head_size
    row = ctx // 2
    place = row * head_size + jnp.where(row % 2 == 0, head, head_size - 1 - head)
    place = lax.rem(place - distance + size, size)
    row, column = place // head_size, place % head_size
    column = jnp.where(row % 2 == 0, column, head_size - 1 - column)
    return ((2 * row + (ctx % 2) ^ flip) * head_size + column) * tokens


def prepare_kernel(order_ref, keep_ref, q_ref, qa_ref, mask_ref, *, groups, per_step, sources, ctx_size, head_size):
    step = pl.program_id(0)
    tokens = q_ref.shape[0]
    row = lax.broadcasted_iota(jnp.int32, (tokens, SPAN), 0)
    lane = lax.broadcasted_iota(jnp.int32, (tokens, SPAN), 1)

    @pl.when(step == 0)
    def _():
        own_start = source_start(0, 0, tokens, ctx_size, head_size)
        own = own_start // SPAN
        for i, source in enumerate(sources):
            start = source_start(*source, tokens, ctx_size, head_size)
            span = start // SPAN
            seen = (order_ref[span] < order_ref[own]) & (keep_ref[own, span] > 0)
            whole = jnp.where(seen, 0.0, MASKED)
            causal = jnp.where(row + (start - own_start) <= lane, 0.0, MASKED)
            mask = jnp.where(own == span, causal, whole)
            mask_ref[i * tokens : (i + 1) * tokens, :] = mask.astype(jnp.bfloat16)

    one_hot = jnp.where(row == lane, 1.0, 0.0).astype(jnp.bfloat16)
    for u in range(per_step):
        for h in range(groups):
            at = (u * groups + h) * HEAD_WIDTH
            qa_ref[u, h * tokens : (h + 1) * tokens, :HEAD_WIDTH] = q_ref[:, at : at + HEAD_WIDTH]
            qa_ref[u, h * tokens : (h + 1) * tokens, HEAD_WIDTH:] = one_hot


def prepare(queries, span_order, block_keep, sources, kv_heads, sizes):
    tokens, width = queries.shape
    groups = width // HEAD_WIDTH // kv_heads
    per_step = 2 if kv_heads % 2 == 0 else 1
    rows = groups * tokens
    smem = pl.BlockSpec(memory_space=pltpu.SMEM)
    return pl.pallas_call(
        functools.partial(
            prepare_kernel,
            groups=groups,
            per_step=per_step,
            sources=sources,
            ctx_size=sizes[0],
            head_size=sizes[1],
        ),
        grid=(kv_heads // per_step,),
        in_specs=[smem, smem, pl.BlockSpec((tokens, per_step * groups * HEAD_WIDTH), lambda s: (0, s))],
        out_specs=[
            pl.BlockSpec((per_step, rows, HEAD_WIDTH + SPAN), lambda s: (s, 0, 0)),
            pl.BlockSpec((tokens * len(sources), SPAN), lambda s: (0, 0)),
        ],
        out_shape=[
            jax.ShapeDtypeStruct((kv_heads, rows, HEAD_WIDTH + SPAN), jnp.bfloat16),
            jax.ShapeDtypeStruct((tokens * len(sources), SPAN), jnp.bfloat16),
        ],
        compiler_params=pltpu.CompilerParams(vmem_limit_bytes=32 * 1024 * 1024),
        cost_estimate=pl.CostEstimate(
            flops=8 * tokens * width, bytes_accessed=16 * tokens * width, transcendentals=0
        ),
    )(span_order, block_keep, queries)


def scale_rows_kernel(*refs, tokens, kv_local, sources, ctx_size, head_size):
    scale_in = refs[:head_size]
    key_scale_ref, value_scale_ref, scale_ref, scale_sem = refs[head_size:]
    inverse_root = 1.0 / math.sqrt(HEAD_WIDTH)
    head = lax.axis_index("head")
    copies = []
    for shift in range(head_size):
        owner = lax.rem(head - shift + head_size, head_size)
        copies.append(
            pltpu.make_async_copy(scale_in[shift], scale_ref.at[owner], scale_sem.at[shift])
        )
    for copy in copies:
        copy.start()
    spans = [
        source_start(*source, tokens, ctx_size, head_size) // SPAN for source in sources
    ]
    for copy in copies:
        copy.wait()
    for g in range(head_size * kv_local):
        owner, member = g // kv_local, g % kv_local
        for i, span in enumerate(spans):
            factor = scale_ref[owner, member, span] * (inverse_root * LOG2E)
            key_scale_ref[g, i : i + 1, :] = jnp.full((1, SPAN), factor, jnp.float32)
            factor = scale_ref[owner, kv_local + member, span]
            value_scale_ref[g, i : i + 1, :] = jnp.full((1, SPAN), factor, jnp.float32)


def scale_rows(scales, sources, tokens, sizes):
    kv_local = scales[0].shape[0] // 2
    shape = (sizes[1] * kv_local, len(sources), SPAN)
    return pl.pallas_call(
        functools.partial(
            scale_rows_kernel,
            tokens=tokens,
            kv_local=kv_local,
            sources=sources,
            ctx_size=sizes[0],
            head_size=sizes[1],
        ),
        in_specs=[pl.BlockSpec(memory_space=pl.ANY)] * len(scales),
        out_specs=[pl.BlockSpec(memory_space=pltpu.VMEM)] * 2,
        out_shape=[jax.ShapeDtypeStruct(shape, jnp.float32)] * 2,
        scratch_shapes=[
            pltpu.SMEM((len(scales),) + scales[0].shape, jnp.float32),
            pltpu.SemaphoreType.DMA((len(scales),)),
        ],
        compiler_params=pltpu.CompilerParams(vmem_limit_bytes=32 * 1024 * 1024),
        cost_estimate=pl.CostEstimate(
            flops=10**8, bytes_accessed=10**6, transcendentals=0
        ),
    )(*scales)


def absorb_kernel(*refs, groups, tokens, per_step, begin, count, first, last):
    refs = list(refs)
    pieces = [(refs.pop(0), refs.pop(0)) for _ in range(count)]
    qa_ref, mask_ref, key_scale_ref, value_scale_ref = [refs.pop(0) for _ in range(4)]
    mixed_in, stats_in = (None, None) if first else (refs.pop(0), refs.pop(0))
    result_ref, stats_ref, x_ref, p_ref, check_ref = refs
    step = pl.program_id(0)
    inverse_root = 1.0 / math.sqrt(HEAD_WIDTH)
    for u in range(per_step):
        g = step * per_step + u
        cols = pl.ds(pl.multiple_of(g * HEAD_WIDTH, HEAD_WIDTH), HEAD_WIDTH)
        k = jnp.concatenate([key_ref[:, cols] for key_ref, _ in pieces], axis=0)
        k = jnp.concatenate([k, mask_ref[begin * tokens : (begin + count) * tokens, :]], axis=1)
        x_ref[u] = lax.dot_general(
            k, qa_ref[u], (((1,), (1,)), ((), ())), preferred_element_type=jnp.float32
        )
    for u in range(per_step):
        g = step * per_step + u
        cols = pl.ds(pl.multiple_of(g * HEAD_WIDTH, HEAD_WIDTH), HEAD_WIDTH)
        factors = [key_scale_ref[u, begin + i : begin + i + 1, :] for i in range(count)]
        high, low = [], []
        for i, (_, value_ref) in enumerate(pieces):
            factor = value_scale_ref[u, begin + i : begin + i + 1, :]
            v = value_ref[:, cols].astype(jnp.float32) * factor
            high.append(v.astype(jnp.bfloat16))
            low.append((v - high[-1].astype(jnp.float32)).astype(jnp.bfloat16))
        v = jnp.concatenate(
            [jnp.concatenate(high, axis=0), jnp.concatenate(low, axis=0)], axis=1
        )
        tops, totals, fades = [], [], []
        for tile in range(groups * tokens // SPAN):
            lanes = slice(tile * SPAN, (tile + 1) * SPAN)
            top = None
            for i, factor in enumerate(factors):
                x = x_ref[u, i * tokens : (i + 1) * tokens, lanes]
                highest = jnp.max(x.reshape(tokens // 8, 8, SPAN), axis=0) * factor
                top = highest if top is None else jnp.maximum(top, highest)
            top = jnp.max(top, axis=0, keepdims=True)
            if not first:
                before = stats_in[u, 0:1, lanes]
                top = jnp.maximum(top, before)
                fades.append(jnp.exp2(before - top))
            total = None
            for i, factor in enumerate(factors):
                keys = slice(i * tokens, (i + 1) * tokens)
                weight = jnp.exp2(x_ref[u, keys, lanes] * factor - top)
                p_ref[u, keys, lanes] = weight.astype(jnp.bfloat16)
                part = jnp.sum(weight.reshape(tokens // 8, 8, SPAN), axis=0)
                total = part if total is None else total + part
            total = jnp.sum(total, axis=0, keepdims=True)
            if not first:
                total = total + fades[tile] * stats_in[u, 1:2, lanes]
            tops.append(top)
            totals.append(total)
        both = lax.dot_general(
            v, p_ref[u], (((0,), (0,)), ((), ())), preferred_element_type=jnp.float32
        )
        for tile in range(groups * tokens // SPAN):
            lanes = slice(tile * SPAN, (tile + 1) * SPAN)
            mixed = both[:HEAD_WIDTH, lanes] + both[HEAD_WIDTH:, lanes]
            if not first:
                mixed = mixed + fades[tile] * mixed_in[u, :, lanes]
            if not last:
                result_ref[u, :, lanes] = mixed
                stats_ref[u, 0:1, lanes] = tops[tile]
                stats_ref[u, 1:2, lanes] = totals[tile]
                continue
            mixed = mixed * (1.0 / totals[tile])
            check = jnp.sum(mixed, axis=0, keepdims=True) * inverse_root
            mixed = jnp.transpose(mixed).astype(result_ref.dtype)
            for j in range(SPAN // tokens):
                h = tile * (SPAN // tokens) + j
                at = (u * groups + h) * HEAD_WIDTH
                result_ref[:, at : at + HEAD_WIDTH] = mixed[j * tokens : (j + 1) * tokens]
                check_ref[pl.ds(g * groups + h, 1), :] = check[:, j * tokens : (j + 1) * tokens]
    if last:

        @pl.when(step == pl.num_programs(0) - 1)
        def _():
            stats_ref[...] = jnp.transpose(check_ref[...])


def absorb(prepared, pieces, begin, state, last, tokens):
    kv_heads, rows, depth = prepared[0].shape
    groups = rows // tokens
    count = len(pieces)
    per_step = 2 if kv_heads % 2 == 0 else 1
    keys = tokens * count
    width = kv_heads * groups * HEAD_WIDTH
    first = state is None
    mixed = pl.BlockSpec((per_step, HEAD_WIDTH, rows), lambda s: (s, 0, 0))
    stats = pl.BlockSpec((per_step, 2, rows), lambda s: (s, 0, 0))
    scale_rows = pl.BlockSpec((per_step,) + prepared[2].shape[1:], lambda s: (s, 0, 0))
    in_specs, operands = [], []
    for piece in pieces:
        joined = len(piece) == 1
        half = (tokens, piece[0].shape[1])
        in_specs.append(pl.BlockSpec(half, lambda s: (0, 0)))
        in_specs.append(pl.BlockSpec(half, lambda s: (1, 0)) if joined else in_specs[-1])
        operands += [piece[0], piece[-1]]
    in_specs += [
        pl.BlockSpec((per_step, rows, depth), lambda s: (s, 0, 0)),
        pl.BlockSpec(prepared[1].shape, lambda s: (0, 0)),
        scale_rows,
        scale_rows,
    ]
    in_specs += [] if first else [mixed, stats]
    if last:
        out_specs = [
            pl.BlockSpec((tokens, per_step * groups * HEAD_WIDTH), lambda s: (0, s)),
            pl.BlockSpec((tokens, kv_heads * groups), lambda s: (0, 0)),
        ]
        out_shape = [
            jax.ShapeDtypeStruct((tokens, width), jnp.bfloat16),
            jax.ShapeDtypeStruct((tokens, kv_heads * groups), jnp.float32),
        ]
    else:
        out_specs = [mixed, stats]
        out_shape = [
            jax.ShapeDtypeStruct((kv_heads, HEAD_WIDTH, rows), jnp.float32),
            jax.ShapeDtypeStruct((kv_heads, 2, rows), jnp.float32),
        ]
    return pl.pallas_call(
        functools.partial(
            absorb_kernel,
            groups=groups,
            tokens=tokens,
            per_step=per_step,
            begin=begin,
            count=count,
            first=first,
            last=last,
        ),
        grid=(kv_heads // per_step,),
        in_specs=in_specs,
        out_specs=out_specs,
        out_shape=out_shape,
        scratch_shapes=[
            pltpu.VMEM((per_step, keys, rows), jnp.float32),
            pltpu.VMEM((per_step, keys, rows), jnp.bfloat16),
            pltpu.VMEM((kv_heads * groups, tokens), jnp.float32),
        ],
        compiler_params=pltpu.CompilerParams(vmem_limit_bytes=32 * 1024 * 1024),
        cost_estimate=pl.CostEstimate(
            flops=16 * tokens * width * keys,
            bytes_accessed=16 * tokens * width,
            transcendentals=tokens * width // HEAD_WIDTH * keys,
        ),
    )(*operands, *prepared, *(() if first else state))


def local(queries, keys, values, key_scale, value_scale, span_order, block_keep):
    tokens = queries.shape[0]
    kv_heads = keys.shape[1] // HEAD_WIDTH
    sizes = ctx_size, head_size = lax.axis_size("ctx"), lax.axis_size("head")
    size = ctx_size // 2 * head_size
    batch = 2 * SPAN // tokens

    def device(place, core):
        row, column = place // head_size, place % head_size
        return (2 * row + core) * head_size + (column if row % 2 == 0 else head_size - 1 - column)

    def around(block, distance):
        route = [
            (device(p, core), device((p + distance) % size, core))
            for p in range(size)
            for core in range(2)
        ]
        return lax.ppermute(block, ("ctx", "head"), route)

    def to_other_core(piece):
        return [lax.ppermute(block, "ctx", [(i, i ^ 1) for i in range(ctx_size)]) for block in piece]

    def along_head(block, distance):
        return lax.ppermute(block, "head", [(i, (i + distance) % head_size) for i in range(head_size)])

    sources = [(0, 0)]
    for step in range(1, size // 2 + 2):
        if step < size // 2:
            sources += [(step, 0), (-step, 0)]
        elif step == size // 2:
            sources += [(step, 0)]
        if step == 1:
            sources += [(0, 1)]
        elif step <= size // 2:
            sources += [(step - 1, 1), (1 - step, 1)]
        else:
            sources += [(step - 1, 1)]

    block = lax.optimization_barrier(jnp.concatenate([keys, values], axis=0))
    scale = jnp.concatenate([jnp.transpose(key_scale), jnp.transpose(value_scale)], axis=0)
    scales, pieces, done = [scale], [[block]], 0
    fresh, forward, backward = [[block]], block, block
    prepared, rows, state = None, None, None
    for step in range(1, size // 2 + 2):
        crossed = [to_other_core(piece) for piece in fresh]
        sent = []
        if step < size // 2:
            forward, backward = around(forward, 1), around(backward, -1)
            sent = [[forward], [backward]]
        elif step == size // 2:
            sent = [[around(forward[:tokens], 1), around(backward[tokens:], -1)]]
        complete = len(scales) == head_size
        for shift in range(len(scales), min(head_size, len(scales) + 2)):
            scales = scales + [along_head(scale, shift)]
        if step == 1:
            prepared = prepare(queries, span_order, block_keep, sources, kv_heads, sizes)
        if complete:
            if rows is None:
                rows = scale_rows(scales, sources, tokens, sizes)
            ready = (len(pieces) - done) // batch * batch
            if ready and step <= size // 2:
                now = pieces[done : done + ready]
                state = absorb((*prepared, *rows), now, done, state, False, tokens)
                done += ready
        crossed, sent, scales, prepared, rows, state = lax.optimization_barrier(
            (crossed, sent, scales, prepared, rows, state)
        )
        fresh = sent
        if step < size // 2:
            forward, backward = fresh[0][0], fresh[1][0]
        pieces = pieces + sent + crossed
    return tuple(absorb((*prepared, *rows), pieces[done:], done, state, True, tokens))


def solution(mesh):
    rows = P(("dp", "ctx", "head"), None)
    return jax.shard_map(
        local,
        mesh=mesh,
        in_specs=(rows, rows, rows, P("dp", "head"), P("dp", "head"), P(), P()),
        out_specs=(rows, rows),
        check_vma=False,
    )
```

```python
import functools
import math

import jax
import jax.numpy as jnp
from jax import lax
from jax.experimental import pallas as pl
from jax.experimental.pallas import tpu as pltpu
from jax.sharding import PartitionSpec as P

HEAD_WIDTH = 128
SPAN = 128
LOG2E = 1.4426950408889634
MASKED = -1e30


def source_start(distance, flip, tokens, ctx_size, head_size):
    ctx, head = lax.axis_index("ctx"), lax.axis_index("head")
    size = ctx_size // 2 * head_size
    row = ctx // 2
    place = row * head_size + jnp.where(row % 2 == 0, head, head_size - 1 - head)
    place = lax.rem(place - distance + size, size)
    row, column = place // head_size, place % head_size
    column = jnp.where(row % 2 == 0, column, head_size - 1 - column)
    return ((2 * row + (ctx % 2) ^ flip) * head_size + column) * tokens


def prepare_kernel(order_ref, keep_ref, q_ref, qa_ref, mask_ref, *, groups, per_step, sources, ctx_size, head_size):
    step = pl.program_id(0)
    tokens = q_ref.shape[0]
    row = lax.broadcasted_iota(jnp.int32, (tokens, SPAN), 0)
    lane = lax.broadcasted_iota(jnp.int32, (tokens, SPAN), 1)

    @pl.when(step == 0)
    def _():
        own_start = source_start(0, 0, tokens, ctx_size, head_size)
        own = own_start // SPAN
        for i, source in enumerate(sources):
            start = source_start(*source, tokens, ctx_size, head_size)
            span = start // SPAN
            seen = (order_ref[span] < order_ref[own]) & (keep_ref[own, span] > 0)
            whole = jnp.where(seen, 0.0, MASKED)
            causal = jnp.where(row + (start - own_start) <= lane, 0.0, MASKED)
            mask = jnp.where(own == span, causal, whole)
            mask_ref[i * tokens : (i + 1) * tokens, :] = mask.astype(jnp.bfloat16)

    one_hot = jnp.where(row == lane, 1.0, 0.0).astype(jnp.bfloat16)
    for u in range(per_step):
        for h in range(groups):
            at = (u * groups + h) * HEAD_WIDTH
            qa_ref[u, h * tokens : (h + 1) * tokens, :HEAD_WIDTH] = q_ref[:, at : at + HEAD_WIDTH]
            qa_ref[u, h * tokens : (h + 1) * tokens, HEAD_WIDTH:] = one_hot


def prepare(queries, span_order, block_keep, sources, kv_heads, sizes):
    tokens, width = queries.shape
    groups = width // HEAD_WIDTH // kv_heads
    per_step = 2 if kv_heads % 2 == 0 else 1
    rows = groups * tokens
    smem = pl.BlockSpec(memory_space=pltpu.SMEM)
    return pl.pallas_call(
        functools.partial(
            prepare_kernel,
            groups=groups,
            per_step=per_step,
            sources=sources,
            ctx_size=sizes[0],
            head_size=sizes[1],
        ),
        grid=(kv_heads // per_step,),
        in_specs=[smem, smem, pl.BlockSpec((tokens, per_step * groups * HEAD_WIDTH), lambda s: (0, s))],
        out_specs=[
            pl.BlockSpec((per_step, rows, HEAD_WIDTH + SPAN), lambda s: (s, 0, 0)),
            pl.BlockSpec((tokens * len(sources), SPAN), lambda s: (0, 0)),
        ],
        out_shape=[
            jax.ShapeDtypeStruct((kv_heads, rows, HEAD_WIDTH + SPAN), jnp.bfloat16),
            jax.ShapeDtypeStruct((tokens * len(sources), SPAN), jnp.bfloat16),
        ],
        compiler_params=pltpu.CompilerParams(vmem_limit_bytes=32 * 1024 * 1024),
        cost_estimate=pl.CostEstimate(
            flops=8 * tokens * width, bytes_accessed=16 * tokens * width, transcendentals=0
        ),
    )(span_order, block_keep, queries)


def scale_rows_kernel(*refs, tokens, kv_local, sources, ctx_size, head_size):
    scale_in = refs[:head_size]
    key_scale_ref, value_scale_ref, scale_ref, scale_sem = refs[head_size:]
    inverse_root = 1.0 / math.sqrt(HEAD_WIDTH)
    head = lax.axis_index("head")
    copies = []
    for shift in range(head_size):
        owner = lax.rem(head - shift + head_size, head_size)
        copies.append(
            pltpu.make_async_copy(scale_in[shift], scale_ref.at[owner], scale_sem.at[shift])
        )
    for copy in copies:
        copy.start()
    spans = [
        source_start(*source, tokens, ctx_size, head_size) // SPAN for source in sources
    ]
    for copy in copies:
        copy.wait()
    for g in range(head_size * kv_local):
        owner, member = g // kv_local, g % kv_local
        for i, span in enumerate(spans):
            factor = scale_ref[owner, member, span] * (inverse_root * LOG2E)
            key_scale_ref[g, i : i + 1, :] = jnp.full((1, SPAN), factor, jnp.float32)
            factor = scale_ref[owner, kv_local + member, span]
            value_scale_ref[g, i : i + 1, :] = jnp.full((1, SPAN), factor, jnp.float32)


def scale_rows(scales, sources, tokens, sizes):
    kv_local = scales[0].shape[0] // 2
    shape = (sizes[1] * kv_local, len(sources), SPAN)
    return pl.pallas_call(
        functools.partial(
            scale_rows_kernel,
            tokens=tokens,
            kv_local=kv_local,
            sources=sources,
            ctx_size=sizes[0],
            head_size=sizes[1],
        ),
        in_specs=[pl.BlockSpec(memory_space=pl.ANY)] * len(scales),
        out_specs=[pl.BlockSpec(memory_space=pltpu.VMEM)] * 2,
        out_shape=[jax.ShapeDtypeStruct(shape, jnp.float32)] * 2,
        scratch_shapes=[
            pltpu.SMEM((len(scales),) + scales[0].shape, jnp.float32),
            pltpu.SemaphoreType.DMA((len(scales),)),
        ],
        compiler_params=pltpu.CompilerParams(vmem_limit_bytes=32 * 1024 * 1024),
        cost_estimate=pl.CostEstimate(
            flops=10**8, bytes_accessed=10**6, transcendentals=0
        ),
    )(*scales)


def absorb_kernel(*refs, groups, tokens, per_step, begin, count, first, last):
    refs = list(refs)
    pieces = [(refs.pop(0), refs.pop(0)) for _ in range(count)]
    qa_ref, mask_ref, key_scale_ref, value_scale_ref = [refs.pop(0) for _ in range(4)]
    mixed_in, stats_in = (None, None) if first else (refs.pop(0), refs.pop(0))
    result_ref, stats_ref, x_ref, p_ref, check_ref = refs
    step = pl.program_id(0)
    inverse_root = 1.0 / math.sqrt(HEAD_WIDTH)
    for u in range(per_step):
        cols = slice(u * HEAD_WIDTH, (u + 1) * HEAD_WIDTH)
        k = jnp.concatenate([key_ref[:, cols] for key_ref, _ in pieces], axis=0)
        k = jnp.concatenate([k, mask_ref[begin * tokens : (begin + count) * tokens, :]], axis=1)
        x_ref[u] = lax.dot_general(
            k, qa_ref[u], (((1,), (1,)), ((), ())), preferred_element_type=jnp.float32
        )
    for u in range(per_step):
        g = step * per_step + u
        cols = slice(u * HEAD_WIDTH, (u + 1) * HEAD_WIDTH)
        factors = [key_scale_ref[u, begin + i : begin + i + 1, :] for i in range(count)]
        high, low = [], []
        for i, (_, value_ref) in enumerate(pieces):
            factor = value_scale_ref[u, begin + i : begin + i + 1, :]
            v = value_ref[:, cols].astype(jnp.float32) * factor
            high.append(v.astype(jnp.bfloat16))
            low.append((v - high[-1].astype(jnp.float32)).astype(jnp.bfloat16))
        v = jnp.concatenate(
            [jnp.concatenate(high, axis=0), jnp.concatenate(low, axis=0)], axis=1
        )
        tops, totals, fades = [], [], []
        for tile in range(groups * tokens // SPAN):
            lanes = slice(tile * SPAN, (tile + 1) * SPAN)
            top = None
            for i, factor in enumerate(factors):
                x = x_ref[u, i * tokens : (i + 1) * tokens, lanes]
                highest = jnp.max(x.reshape(tokens // 8, 8, SPAN), axis=0) * factor
                top = highest if top is None else jnp.maximum(top, highest)
            top = jnp.max(top, axis=0, keepdims=True)
            if not first:
                before = stats_in[u, 0:1, lanes]
                top = jnp.maximum(top, before)
                fades.append(jnp.exp2(before - top))
            total = None
            for i, factor in enumerate(factors):
                keys = slice(i * tokens, (i + 1) * tokens)
                weight = jnp.exp2(x_ref[u, keys, lanes] * factor - top)
                p_ref[u, keys, lanes] = weight.astype(jnp.bfloat16)
                part = jnp.sum(weight.reshape(tokens // 8, 8, SPAN), axis=0)
                total = part if total is None else total + part
            total = jnp.sum(total, axis=0, keepdims=True)
            if not first:
                total = total + fades[tile] * stats_in[u, 1:2, lanes]
            tops.append(top)
            totals.append(total)
        both = lax.dot_general(
            v, p_ref[u], (((0,), (0,)), ((), ())), preferred_element_type=jnp.float32
        )
        for tile in range(groups * tokens // SPAN):
            lanes = slice(tile * SPAN, (tile + 1) * SPAN)
            mixed = both[:HEAD_WIDTH, lanes] + both[HEAD_WIDTH:, lanes]
            if not first:
                mixed = mixed + fades[tile] * mixed_in[u, :, lanes]
            if not last:
                result_ref[u, :, lanes] = mixed
                stats_ref[u, 0:1, lanes] = tops[tile]
                stats_ref[u, 1:2, lanes] = totals[tile]
                continue
            mixed = mixed * (1.0 / totals[tile])
            check = jnp.sum(mixed, axis=0, keepdims=True) * inverse_root
            mixed = jnp.transpose(mixed.astype(result_ref.dtype))
            for j in range(SPAN // tokens):
                h = tile * (SPAN // tokens) + j
                at = (u * groups + h) * HEAD_WIDTH
                result_ref[:, at : at + HEAD_WIDTH] = mixed[j * tokens : (j + 1) * tokens]
                check_ref[pl.ds(g * groups + h, 1), :] = check[:, j * tokens : (j + 1) * tokens]
    if last:

        @pl.when(step == pl.num_programs(0) - 1)
        def _():
            stats_ref[...] = jnp.transpose(check_ref[...])


def absorb(prepared, pieces, begin, state, last, tokens):
    kv_heads, rows, depth = prepared[0].shape
    groups = rows // tokens
    count = len(pieces)
    per_step = 2 if kv_heads % 2 == 0 else 1
    keys = tokens * count
    width = kv_heads * groups * HEAD_WIDTH
    first = state is None
    mixed = pl.BlockSpec((per_step, HEAD_WIDTH, rows), lambda s: (s, 0, 0))
    stats = pl.BlockSpec((per_step, 2, rows), lambda s: (s, 0, 0))
    scale_rows = pl.BlockSpec((per_step,) + prepared[2].shape[1:], lambda s: (s, 0, 0))
    in_specs, operands = [], []
    for piece in pieces:
        joined = len(piece) == 1
        half = (tokens, per_step * HEAD_WIDTH)
        in_specs.append(pl.BlockSpec(half, lambda s: (0, s)))
        in_specs.append(pl.BlockSpec(half, lambda s: (1, s)) if joined else in_specs[-1])
        operands += [piece[0], piece[-1]]
    in_specs += [
        pl.BlockSpec((per_step, rows, depth), lambda s: (s, 0, 0)),
        pl.BlockSpec(prepared[1].shape, lambda s: (0, 0)),
        scale_rows,
        scale_rows,
    ]
    in_specs += [] if first else [mixed, stats]
    if last:
        out_specs = [
            pl.BlockSpec((tokens, per_step * groups * HEAD_WIDTH), lambda s: (0, s)),
            pl.BlockSpec((tokens, kv_heads * groups), lambda s: (0, 0)),
        ]
        out_shape = [
            jax.ShapeDtypeStruct((tokens, width), jnp.bfloat16),
            jax.ShapeDtypeStruct((tokens, kv_heads * groups), jnp.float32),
        ]
    else:
        out_specs = [mixed, stats]
        out_shape = [
            jax.ShapeDtypeStruct((kv_heads, HEAD_WIDTH, rows), jnp.float32),
            jax.ShapeDtypeStruct((kv_heads, 2, rows), jnp.float32),
        ]
    return pl.pallas_call(
        functools.partial(
            absorb_kernel,
            groups=groups,
            tokens=tokens,
            per_step=per_step,
            begin=begin,
            count=count,
            first=first,
            last=last,
        ),
        grid=(kv_heads // per_step,),
        in_specs=in_specs,
        out_specs=out_specs,
        out_shape=out_shape,
        scratch_shapes=[
            pltpu.VMEM((per_step, keys, rows), jnp.float32),
            pltpu.VMEM((per_step, keys, rows), jnp.bfloat16),
            pltpu.VMEM((kv_heads * groups, tokens), jnp.float32),
        ],
        compiler_params=pltpu.CompilerParams(vmem_limit_bytes=32 * 1024 * 1024),
        cost_estimate=pl.CostEstimate(
            flops=16 * tokens * width * keys,
            bytes_accessed=16 * tokens * width,
            transcendentals=tokens * width // HEAD_WIDTH * keys,
        ),
    )(*operands, *prepared, *(() if first else state))


def local(queries, keys, values, key_scale, value_scale, span_order, block_keep):
    tokens = queries.shape[0]
    kv_heads = keys.shape[1] // HEAD_WIDTH
    sizes = ctx_size, head_size = lax.axis_size("ctx"), lax.axis_size("head")
    size = ctx_size // 2 * head_size
    batch = 2 * SPAN // tokens

    def device(place, core):
        row, column = place // head_size, place % head_size
        return (2 * row + core) * head_size + (column if row % 2 == 0 else head_size - 1 - column)

    def around(block, distance):
        route = [
            (device(p, core), device((p + distance) % size, core))
            for p in range(size)
            for core in range(2)
        ]
        return lax.ppermute(block, ("ctx", "head"), route)

    def to_other_core(piece):
        return [lax.ppermute(block, "ctx", [(i, i ^ 1) for i in range(ctx_size)]) for block in piece]

    def along_head(block, distance):
        return lax.ppermute(block, "head", [(i, (i + distance) % head_size) for i in range(head_size)])

    sources = [(0, 0)]
    for step in range(1, size // 2 + 2):
        if step < size // 2:
            sources += [(step, 0), (-step, 0)]
        elif step == size // 2:
            sources += [(step, 0)]
        if step == 1:
            sources += [(0, 1)]
        elif step <= size // 2:
            sources += [(step - 1, 1), (1 - step, 1)]
        else:
            sources += [(step - 1, 1)]

    block = lax.optimization_barrier(jnp.concatenate([keys, values], axis=0))
    scale = jnp.concatenate([jnp.transpose(key_scale), jnp.transpose(value_scale)], axis=0)
    scales, pieces, done = [scale], [[block]], 0
    fresh, forward, backward = [[block]], block, block
    prepared, rows, state = None, None, None
    for step in range(1, size // 2 + 2):
        crossed = [to_other_core(piece) for piece in fresh]
        sent = []
        if step < size // 2:
            forward, backward = around(forward, 1), around(backward, -1)
            sent = [[forward], [backward]]
        elif step == size // 2:
            sent = [[around(forward[:tokens], 1), around(backward[tokens:], -1)]]
        complete = len(scales) == head_size
        for shift in range(len(scales), min(head_size, len(scales) + 2)):
            scales = scales + [along_head(scale, shift)]
        if step == 2:
            prepared = prepare(queries, span_order, block_keep, sources, kv_heads, sizes)
        if complete:
            if rows is None:
                rows = scale_rows(scales, sources, tokens, sizes)
            ready = (len(pieces) - done) // batch * batch
            if ready and step <= size // 2:
                now = pieces[done : done + ready]
                state = absorb((*prepared, *rows), now, done, state, False, tokens)
                done += ready
        crossed, sent, scales, prepared, rows, state = lax.optimization_barrier(
            (crossed, sent, scales, prepared, rows, state)
        )
        fresh = sent
        if step < size // 2:
            forward, backward = fresh[0][0], fresh[1][0]
        pieces = pieces + sent + crossed
    return tuple(absorb((*prepared, *rows), pieces[done:], done, state, True, tokens))


def solution(mesh):
    rows = P(("dp", "ctx", "head"), None)
    return jax.shard_map(
        local,
        mesh=mesh,
        in_specs=(rows, rows, rows, P("dp", "head"), P("dp", "head"), P(), P()),
        out_specs=(rows, rows),
        check_vma=False,
    )
```

```python
import functools
import math

import jax
import jax.numpy as jnp
from jax import lax
from jax.experimental import pallas as pl
from jax.experimental.pallas import tpu as pltpu
from jax.sharding import PartitionSpec as P

HEAD_WIDTH = 128
SPAN = 128
LOG2E = 1.4426950408889634
MASKED = -1e30


def source_start(distance, flip, tokens, ctx_size, head_size):
    ctx, head = lax.axis_index("ctx"), lax.axis_index("head")
    size = ctx_size // 2 * head_size
    row = ctx // 2
    place = row * head_size + jnp.where(row % 2 == 0, head, head_size - 1 - head)
    place = lax.rem(place - distance + size, size)
    row, column = place // head_size, place % head_size
    column = jnp.where(row % 2 == 0, column, head_size - 1 - column)
    return ((2 * row + (ctx % 2) ^ flip) * head_size + column) * tokens


def prepare_kernel(order_ref, keep_ref, q_ref, qa_ref, mask_ref, *, groups, per_step, sources, ctx_size, head_size):
    step = pl.program_id(0)
    tokens = q_ref.shape[0]
    row = lax.broadcasted_iota(jnp.int32, (tokens, SPAN), 0)
    lane = lax.broadcasted_iota(jnp.int32, (tokens, SPAN), 1)

    @pl.when(step == 0)
    def _():
        own_start = source_start(0, 0, tokens, ctx_size, head_size)
        own = own_start // SPAN
        for i, source in enumerate(sources):
            start = source_start(*source, tokens, ctx_size, head_size)
            span = start // SPAN
            seen = (order_ref[span] < order_ref[own]) & (keep_ref[own, span] > 0)
            whole = jnp.where(seen, 0.0, MASKED)
            causal = jnp.where(row + (start - own_start) <= lane, 0.0, MASKED)
            mask = jnp.where(own == span, causal, whole)
            mask_ref[i * tokens : (i + 1) * tokens, :] = mask.astype(jnp.bfloat16)

    for u in range(per_step):
        for h in range(groups):
            at = (u * groups + h) * HEAD_WIDTH
            qa_ref[u, h * tokens : (h + 1) * tokens, :] = q_ref[:, at : at + HEAD_WIDTH]


def prepare(queries, span_order, block_keep, sources, kv_heads, sizes):
    tokens, width = queries.shape
    groups = width // HEAD_WIDTH // kv_heads
    per_step = 2 if kv_heads % 2 == 0 else 1
    rows = groups * tokens
    smem = pl.BlockSpec(memory_space=pltpu.SMEM)
    return pl.pallas_call(
        functools.partial(
            prepare_kernel,
            groups=groups,
            per_step=per_step,
            sources=sources,
            ctx_size=sizes[0],
            head_size=sizes[1],
        ),
        grid=(kv_heads // per_step,),
        in_specs=[smem, smem, pl.BlockSpec((tokens, per_step * groups * HEAD_WIDTH), lambda s: (0, s))],
        out_specs=[
            pl.BlockSpec((per_step, rows, HEAD_WIDTH), lambda s: (s, 0, 0)),
            pl.BlockSpec((tokens * len(sources), SPAN), lambda s: (0, 0)),
        ],
        out_shape=[
            jax.ShapeDtypeStruct((kv_heads, rows, HEAD_WIDTH), jnp.bfloat16),
            jax.ShapeDtypeStruct((tokens * len(sources), SPAN), jnp.bfloat16),
        ],
        compiler_params=pltpu.CompilerParams(vmem_limit_bytes=32 * 1024 * 1024),
        cost_estimate=pl.CostEstimate(
            flops=8 * tokens * width, bytes_accessed=16 * tokens * width, transcendentals=0
        ),
    )(span_order, block_keep, queries)


def scale_rows_kernel(*refs, owners, tokens, kv_local, sources, ctx_size, head_size):
    scale_in = refs[: len(owners)]
    key_scale_ref, value_scale_ref, scale_ref, scale_sem = refs[len(owners) :]
    inverse_root = 1.0 / math.sqrt(HEAD_WIDTH)
    head = lax.axis_index("head")
    copies, flip = [], 0
    for ref, count in zip(scale_in, owners):
        for i in range(count):
            copies.append(
                pltpu.make_async_copy(ref.at[i], scale_ref.at[head ^ flip], scale_sem.at[flip])
            )
            flip += 1
    for copy in copies:
        copy.start()
    spans = [
        source_start(*source, tokens, ctx_size, head_size) // SPAN for source in sources
    ]
    for copy in copies:
        copy.wait()
    for g in range(head_size * kv_local):
        owner, member = g // kv_local, g % kv_local
        for i, span in enumerate(spans):
            factor = scale_ref[owner, member, span] * (inverse_root * LOG2E)
            key_scale_ref[g, i : i + 1, :] = jnp.full((1, SPAN), factor, jnp.float32)
            factor = scale_ref[owner, kv_local + member, span]
            value_scale_ref[g, i : i + 1, :] = jnp.full((1, SPAN), factor, jnp.float32)


def scale_rows(scales, sources, tokens, sizes):
    kv_local = scales[0].shape[1] // 2
    shape = (sizes[1] * kv_local, len(sources), SPAN)
    return pl.pallas_call(
        functools.partial(
            scale_rows_kernel,
            owners=[scale.shape[0] for scale in scales],
            tokens=tokens,
            kv_local=kv_local,
            sources=sources,
            ctx_size=sizes[0],
            head_size=sizes[1],
        ),
        in_specs=[pl.BlockSpec(memory_space=pl.ANY)] * len(scales),
        out_specs=[pl.BlockSpec(memory_space=pltpu.VMEM)] * 2,
        out_shape=[jax.ShapeDtypeStruct(shape, jnp.float32)] * 2,
        scratch_shapes=[
            pltpu.SMEM((sizes[1],) + scales[0].shape[1:], jnp.float32),
            pltpu.SemaphoreType.DMA((sizes[1],)),
        ],
        compiler_params=pltpu.CompilerParams(vmem_limit_bytes=32 * 1024 * 1024),
        cost_estimate=pl.CostEstimate(
            flops=10**8, bytes_accessed=10**6, transcendentals=0
        ),
    )(*scales)


def absorb_kernel(*refs, groups, tokens, per_step, begin, count, first, last):
    refs = list(refs)
    pieces = [(refs.pop(0), refs.pop(0)) for _ in range(count)]
    qa_ref, mask_ref, key_scale_ref, value_scale_ref = [refs.pop(0) for _ in range(4)]
    mixed_in, stats_in = (None, None) if first else (refs.pop(0), refs.pop(0))
    result_ref, stats_ref, x_ref, p_ref, check_ref = refs
    step = pl.program_id(0)
    inverse_root = 1.0 / math.sqrt(HEAD_WIDTH)
    row = lax.broadcasted_iota(jnp.int32, (tokens, SPAN), 0)
    lane = lax.broadcasted_iota(jnp.int32, (tokens, SPAN), 1)
    one_hot = jnp.where(row == lane, 1.0, 0.0).astype(jnp.bfloat16)
    one_hot = jnp.concatenate([one_hot] * groups, axis=0)
    for u in range(per_step):
        g = step * per_step + u
        cols = pl.ds(pl.multiple_of(g * HEAD_WIDTH, HEAD_WIDTH), HEAD_WIDTH)
        k = jnp.concatenate([key_ref[:, cols] for key_ref, _ in pieces], axis=0)
        k = jnp.concatenate([k, mask_ref[begin * tokens : (begin + count) * tokens, :]], axis=1)
        x_ref[u] = lax.dot_general(
            k,
            jnp.concatenate([qa_ref[u], one_hot], axis=1),
            (((1,), (1,)), ((), ())),
            preferred_element_type=jnp.float32,
        )
    for u in range(per_step):
        g = step * per_step + u
        cols = pl.ds(pl.multiple_of(g * HEAD_WIDTH, HEAD_WIDTH), HEAD_WIDTH)
        factors = [key_scale_ref[u, begin + i : begin + i + 1, :] for i in range(count)]
        high, low = [], []
        for i, (_, value_ref) in enumerate(pieces):
            factor = value_scale_ref[u, begin + i : begin + i + 1, :]
            v = value_ref[:, cols].astype(jnp.float32) * factor
            high.append(v.astype(jnp.bfloat16))
            low.append((v - high[-1].astype(jnp.float32)).astype(jnp.bfloat16))
        v = jnp.concatenate(
            [jnp.concatenate(high, axis=0), jnp.concatenate(low, axis=0)], axis=1
        )
        tops, totals, fades = [], [], []
        for tile in range(groups * tokens // SPAN):
            lanes = slice(tile * SPAN, (tile + 1) * SPAN)
            top = None
            for i, factor in enumerate(factors):
                x = x_ref[u, i * tokens : (i + 1) * tokens, lanes]
                highest = jnp.max(x.reshape(tokens // 8, 8, SPAN), axis=0) * factor
                top = highest if top is None else jnp.maximum(top, highest)
            top = jnp.max(top, axis=0, keepdims=True)
            if not first:
                before = stats_in[u, 0:1, lanes]
                top = jnp.maximum(top, before)
                fades.append(jnp.exp2(before - top))
            total = None
            for i, factor in enumerate(factors):
                keys = slice(i * tokens, (i + 1) * tokens)
                weight = jnp.exp2(x_ref[u, keys, lanes] * factor - top)
                p_ref[u, keys, lanes] = weight.astype(jnp.bfloat16)
                part = jnp.sum(weight.reshape(tokens // 8, 8, SPAN), axis=0)
                total = part if total is None else total + part
            total = jnp.sum(total, axis=0, keepdims=True)
            if not first:
                total = total + fades[tile] * stats_in[u, 1:2, lanes]
            tops.append(top)
            totals.append(total)
        both = lax.dot_general(
            v, p_ref[u], (((0,), (0,)), ((), ())), preferred_element_type=jnp.float32
        )
        for tile in range(groups * tokens // SPAN):
            lanes = slice(tile * SPAN, (tile + 1) * SPAN)
            mixed = both[:HEAD_WIDTH, lanes] + both[HEAD_WIDTH:, lanes]
            if not first:
                mixed = mixed + fades[tile] * mixed_in[u, :, lanes]
            if not last:
                result_ref[u, :, lanes] = mixed
                stats_ref[u, 0:1, lanes] = tops[tile]
                stats_ref[u, 1:2, lanes] = totals[tile]
                continue
            mixed = mixed * (1.0 / totals[tile])
            check = jnp.sum(mixed, axis=0, keepdims=True) * inverse_root
            mixed = jnp.transpose(mixed).astype(result_ref.dtype)
            for j in range(SPAN // tokens):
                h = tile * (SPAN // tokens) + j
                at = (u * groups + h) * HEAD_WIDTH
                result_ref[:, at : at + HEAD_WIDTH] = mixed[j * tokens : (j + 1) * tokens]
                check_ref[pl.ds(g * groups + h, 1), :] = check[:, j * tokens : (j + 1) * tokens]
    if last:

        @pl.when(step == pl.num_programs(0) - 1)
        def _():
            stats_ref[...] = jnp.transpose(check_ref[...])


def absorb(prepared, pieces, begin, state, last, tokens):
    kv_heads, rows, depth = prepared[0].shape
    groups = rows // tokens
    count = len(pieces)
    per_step = 2 if kv_heads % 2 == 0 else 1
    keys = tokens * count
    width = kv_heads * groups * HEAD_WIDTH
    first = state is None
    mixed = pl.BlockSpec((per_step, HEAD_WIDTH, rows), lambda s: (s, 0, 0))
    stats = pl.BlockSpec((per_step, 2, rows), lambda s: (s, 0, 0))
    scale_rows = pl.BlockSpec((per_step,) + prepared[2].shape[1:], lambda s: (s, 0, 0))
    in_specs, operands = [], []
    for piece in pieces:
        joined = len(piece) == 1
        half = (tokens, piece[0].shape[1])
        in_specs.append(pl.BlockSpec(half, lambda s: (0, 0)))
        in_specs.append(pl.BlockSpec(half, lambda s: (1, 0)) if joined else in_specs[-1])
        operands += [piece[0], piece[-1]]
    in_specs += [
        pl.BlockSpec((per_step, rows, depth), lambda s: (s, 0, 0)),
        pl.BlockSpec(prepared[1].shape, lambda s: (0, 0)),
        scale_rows,
        scale_rows,
    ]
    in_specs += [] if first else [mixed, stats]
    if last:
        out_specs = [
            pl.BlockSpec((tokens, per_step * groups * HEAD_WIDTH), lambda s: (0, s)),
            pl.BlockSpec((tokens, kv_heads * groups), lambda s: (0, 0)),
        ]
        out_shape = [
            jax.ShapeDtypeStruct((tokens, width), jnp.bfloat16),
            jax.ShapeDtypeStruct((tokens, kv_heads * groups), jnp.float32),
        ]
    else:
        out_specs = [mixed, stats]
        out_shape = [
            jax.ShapeDtypeStruct((kv_heads, HEAD_WIDTH, rows), jnp.float32),
            jax.ShapeDtypeStruct((kv_heads, 2, rows), jnp.float32),
        ]
    return pl.pallas_call(
        functools.partial(
            absorb_kernel,
            groups=groups,
            tokens=tokens,
            per_step=per_step,
            begin=begin,
            count=count,
            first=first,
            last=last,
        ),
        grid=(kv_heads // per_step,),
        in_specs=in_specs,
        out_specs=out_specs,
        out_shape=out_shape,
        scratch_shapes=[
            pltpu.VMEM((per_step, keys, rows), jnp.float32),
            pltpu.VMEM((per_step, keys, rows), jnp.bfloat16),
            pltpu.VMEM((kv_heads * groups, tokens), jnp.float32),
        ],
        compiler_params=pltpu.CompilerParams(vmem_limit_bytes=32 * 1024 * 1024),
        cost_estimate=pl.CostEstimate(
            flops=16 * tokens * width * keys,
            bytes_accessed=16 * tokens * width,
            transcendentals=tokens * width // HEAD_WIDTH * keys,
        ),
    )(*operands, *prepared, *(() if first else state))


def local(queries, keys, values, key_scale, value_scale, span_order, block_keep):
    tokens = queries.shape[0]
    kv_heads = keys.shape[1] // HEAD_WIDTH
    sizes = ctx_size, head_size = lax.axis_size("ctx"), lax.axis_size("head")
    size = ctx_size // 2 * head_size
    batch = 2 * SPAN // tokens

    def device(place, core):
        row, column = place // head_size, place % head_size
        return (2 * row + core) * head_size + (column if row % 2 == 0 else head_size - 1 - column)

    def around(block, distance):
        route = [
            (device(p, core), device((p + distance) % size, core))
            for p in range(size)
            for core in range(2)
        ]
        return lax.ppermute(block, ("ctx", "head"), route)

    def to_other_core(piece):
        return [lax.ppermute(block, "ctx", [(i, i ^ 1) for i in range(ctx_size)]) for block in piece]

    def swap_heads(block, flip):
        return lax.ppermute(block, "head", [(i, i ^ flip) for i in range(head_size)])

    sources = [(0, 0)]
    for step in range(1, size // 2 + 2):
        if step < size // 2:
            sources += [(step, 0), (-step, 0)]
        elif step == size // 2:
            sources += [(step - 1, 1), (1 - step, 1), (step, 0)]
        if step == 1:
            sources += [(0, 1)]
        elif step < size // 2:
            sources += [(step - 1, 1), (1 - step, 1)]
        elif step > size // 2:
            sources += [(step - 1, 1)]

    block = lax.optimization_barrier(jnp.concatenate([keys, values], axis=0))
    scale = jnp.concatenate([jnp.transpose(key_scale), jnp.transpose(value_scale)], axis=0)
    scales, pieces, done = [scale[None]], [[block]], 0
    fresh, forward, backward = [[block]], block, block
    prepared, rows, state = None, None, None
    for step in range(1, size // 2 + 2):
        crossed = [to_other_core(piece) for piece in fresh]
        sent = []
        if step < size // 2:
            forward, backward = around(forward, 1), around(backward, -1)
            sent = [[forward], [backward]]
        elif step == size // 2:
            sent = [[around(forward[:tokens], 1), around(backward[tokens:], -1)]]
        held = sum(scale.shape[0] for scale in scales)
        complete = held == head_size
        if not complete:
            scales = scales + [swap_heads(jnp.concatenate(scales, axis=0), held)]
        if step == 2:
            prepared = prepare(queries, span_order, block_keep, sources, kv_heads, sizes)
        if complete:
            if rows is None:
                rows = scale_rows(scales, sources, tokens, sizes)
            ready = (len(pieces) - done) // batch * batch if step < size // 2 else 0
            now = pieces[done : done + ready]
            if step == size // 2:
                now = pieces[done:] + crossed
                ready = len(now)
            if ready:
                state = absorb((*prepared, *rows), now, done, state, False, tokens)
                done += ready
        sent, crossed, scales, prepared, rows, state = lax.optimization_barrier(
            (sent, crossed, scales, prepared, rows, state)
        )
        fresh = sent
        if step < size // 2:
            forward, backward = fresh[0][0], fresh[1][0]
        pieces = pieces + (sent + crossed if step < size // 2 else crossed + sent)
    return tuple(absorb((*prepared, *rows), pieces[done:], done, state, True, tokens))


def solution(mesh):
    rows = P(("dp", "ctx", "head"), None)
    return jax.shard_map(
        local,
        mesh=mesh,
        in_specs=(rows, rows, rows, P("dp", "head"), P("dp", "head"), P(), P()),
        out_specs=(rows, rows),
        check_vma=False,
    )
```

```python
import functools
import math

import jax
import jax.numpy as jnp
from jax import lax
from jax.experimental import pallas as pl
from jax.experimental.pallas import tpu as pltpu
from jax.sharding import PartitionSpec as P

HEAD_WIDTH = 128
SPAN = 128
LOG2E = 1.4426950408889634
MASKED = -1e30


def source_start(distance, flip, tokens, ctx_size, head_size):
    ctx, head = lax.axis_index("ctx"), lax.axis_index("head")
    size = ctx_size // 2 * head_size
    row = ctx // 2
    place = row * head_size + jnp.where(row % 2 == 0, head, head_size - 1 - head)
    place = lax.rem(place - distance + size, size)
    row, column = place // head_size, place % head_size
    column = jnp.where(row % 2 == 0, column, head_size - 1 - column)
    return ((2 * row + (ctx % 2) ^ flip) * head_size + column) * tokens


def prepare_kernel(order_ref, keep_ref, q_ref, qa_ref, mask_ref, *, groups, per_step, sources, ctx_size, head_size):
    step = pl.program_id(0)
    tokens = q_ref.shape[0]
    row = lax.broadcasted_iota(jnp.int32, (tokens, SPAN), 0)
    lane = lax.broadcasted_iota(jnp.int32, (tokens, SPAN), 1)

    @pl.when(step == 0)
    def _():
        own_start = source_start(0, 0, tokens, ctx_size, head_size)
        own = own_start // SPAN
        for i, source in enumerate(sources):
            start = source_start(*source, tokens, ctx_size, head_size)
            span = start // SPAN
            seen = (order_ref[span] < order_ref[own]) & (keep_ref[own, span] > 0)
            whole = jnp.where(seen, 0.0, MASKED)
            causal = jnp.where(row + (start - own_start) <= lane, 0.0, MASKED)
            mask = jnp.where(own == span, causal, whole)
            mask_ref[i * tokens : (i + 1) * tokens, :] = mask.astype(jnp.bfloat16)

    for u in range(per_step):
        for h in range(groups):
            at = (u * groups + h) * HEAD_WIDTH
            qa_ref[u, h * tokens : (h + 1) * tokens, :] = q_ref[:, at : at + HEAD_WIDTH]


def prepare(queries, span_order, block_keep, sources, kv_heads, sizes):
    tokens, width = queries.shape
    groups = width // HEAD_WIDTH // kv_heads
    per_step = 2 if kv_heads % 2 == 0 else 1
    rows = groups * tokens
    smem = pl.BlockSpec(memory_space=pltpu.SMEM)
    return pl.pallas_call(
        functools.partial(
            prepare_kernel,
            groups=groups,
            per_step=per_step,
            sources=sources,
            ctx_size=sizes[0],
            head_size=sizes[1],
        ),
        grid=(kv_heads // per_step,),
        in_specs=[smem, smem, pl.BlockSpec((tokens, per_step * groups * HEAD_WIDTH), lambda s: (0, s))],
        out_specs=[
            pl.BlockSpec((per_step, rows, HEAD_WIDTH), lambda s: (s, 0, 0)),
            pl.BlockSpec((tokens * len(sources), SPAN), lambda s: (0, 0)),
        ],
        out_shape=[
            jax.ShapeDtypeStruct((kv_heads, rows, HEAD_WIDTH), jnp.bfloat16),
            jax.ShapeDtypeStruct((tokens * len(sources), SPAN), jnp.bfloat16),
        ],
        compiler_params=pltpu.CompilerParams(vmem_limit_bytes=32 * 1024 * 1024),
        cost_estimate=pl.CostEstimate(
            flops=8 * tokens * width, bytes_accessed=16 * tokens * width, transcendentals=0
        ),
    )(span_order, block_keep, queries)


def scale_rows_kernel(*refs, owners, tokens, kv_local, sources, ctx_size, head_size):
    scale_in = refs[: len(owners)]
    key_scale_ref, value_scale_ref, scale_ref, scale_sem = refs[len(owners) :]
    inverse_root = 1.0 / math.sqrt(HEAD_WIDTH)
    head = lax.axis_index("head")
    copies, flip = [], 0
    for ref, count in zip(scale_in, owners):
        for i in range(count):
            copies.append(
                pltpu.make_async_copy(ref.at[i], scale_ref.at[head ^ flip], scale_sem.at[flip])
            )
            flip += 1
    for copy in copies:
        copy.start()
    spans = [
        source_start(*source, tokens, ctx_size, head_size) // SPAN for source in sources
    ]
    for copy in copies:
        copy.wait()
    for g in range(head_size * kv_local):
        owner, member = g // kv_local, g % kv_local
        for i, span in enumerate(spans):
            factor = scale_ref[owner, member, span] * (inverse_root * LOG2E)
            key_scale_ref[g, i : i + 1, :] = jnp.full((1, SPAN), factor, jnp.float32)
            factor = scale_ref[owner, kv_local + member, span]
            value_scale_ref[g, i : i + 1, :] = jnp.full((1, SPAN), factor, jnp.float32)


def scale_rows(scales, sources, tokens, sizes):
    kv_local = scales[0].shape[1] // 2
    shape = (sizes[1] * kv_local, len(sources), SPAN)
    return pl.pallas_call(
        functools.partial(
            scale_rows_kernel,
            owners=[scale.shape[0] for scale in scales],
            tokens=tokens,
            kv_local=kv_local,
            sources=sources,
            ctx_size=sizes[0],
            head_size=sizes[1],
        ),
        in_specs=[pl.BlockSpec(memory_space=pl.ANY)] * len(scales),
        out_specs=[pl.BlockSpec(memory_space=pltpu.VMEM)] * 2,
        out_shape=[jax.ShapeDtypeStruct(shape, jnp.float32)] * 2,
        scratch_shapes=[
            pltpu.SMEM((sizes[1],) + scales[0].shape[1:], jnp.float32),
            pltpu.SemaphoreType.DMA((sizes[1],)),
        ],
        compiler_params=pltpu.CompilerParams(vmem_limit_bytes=32 * 1024 * 1024),
        cost_estimate=pl.CostEstimate(
            flops=10**8, bytes_accessed=10**6, transcendentals=0
        ),
    )(*scales)


def absorb_kernel(*refs, groups, tokens, per_step, begin, whole, first, last):
    count = len(whole)
    refs = list(refs)
    pieces = []
    for joined in whole:
        ref = refs.pop(0)
        if joined:
            pieces.append((ref.at[pl.ds(0, tokens)], ref.at[pl.ds(tokens, tokens)]))
        else:
            pieces.append((ref, refs.pop(0)))
    qa_ref, mask_ref, key_scale_ref, value_scale_ref = [refs.pop(0) for _ in range(4)]
    mixed_in, stats_in = (None, None) if first else (refs.pop(0), refs.pop(0))
    result_ref, stats_ref, x_ref, p_ref, check_ref = refs
    kv_heads = qa_ref.shape[0]
    inverse_root = 1.0 / math.sqrt(HEAD_WIDTH)
    row = lax.broadcasted_iota(jnp.int32, (tokens, SPAN), 0)
    lane = lax.broadcasted_iota(jnp.int32, (tokens, SPAN), 1)
    one_hot = jnp.where(row == lane, 1.0, 0.0).astype(jnp.bfloat16)
    one_hot = jnp.concatenate([one_hot] * groups, axis=0)

    @pl.loop(0, kv_heads // per_step)
    def _(step):
        for u in range(per_step):
            g = step * per_step + u
            cols = pl.ds(pl.multiple_of(g * HEAD_WIDTH, HEAD_WIDTH), HEAD_WIDTH)
            k = jnp.concatenate([key_ref[:, cols] for key_ref, _ in pieces], axis=0)
            k = jnp.concatenate([k, mask_ref[begin * tokens : (begin + count) * tokens, :]], axis=1)
            x_ref[u] = lax.dot_general(
                k,
                jnp.concatenate([qa_ref[g], one_hot], axis=1),
                (((1,), (1,)), ((), ())),
                preferred_element_type=jnp.float32,
            )
        for u in range(per_step):
            g = step * per_step + u
            cols = pl.ds(pl.multiple_of(g * HEAD_WIDTH, HEAD_WIDTH), HEAD_WIDTH)
            factors = [key_scale_ref[g, begin + i : begin + i + 1, :] for i in range(count)]
            high, low = [], []
            for i, (_, value_ref) in enumerate(pieces):
                factor = value_scale_ref[g, begin + i : begin + i + 1, :]
                v = value_ref[:, cols].astype(jnp.float32) * factor
                high.append(v.astype(jnp.bfloat16))
                low.append((v - high[-1].astype(jnp.float32)).astype(jnp.bfloat16))
            v = jnp.concatenate(
                [jnp.concatenate(high, axis=0), jnp.concatenate(low, axis=0)], axis=1
            )
            tops, totals, fades = [], [], []
            for tile in range(groups * tokens // SPAN):
                lanes = slice(tile * SPAN, (tile + 1) * SPAN)
                top = None
                for i, factor in enumerate(factors):
                    x = x_ref[u, i * tokens : (i + 1) * tokens, lanes]
                    highest = jnp.max(x.reshape(tokens // 8, 8, SPAN), axis=0) * factor
                    top = highest if top is None else jnp.maximum(top, highest)
                top = jnp.max(top, axis=0, keepdims=True)
                if not first:
                    before = stats_in[g, 0:1, lanes]
                    top = jnp.maximum(top, before)
                    fades.append(jnp.exp2(before - top))
                total = None
                for i, factor in enumerate(factors):
                    keys = slice(i * tokens, (i + 1) * tokens)
                    weight = jnp.exp2(x_ref[u, keys, lanes] * factor - top)
                    p_ref[u, keys, lanes] = weight.astype(jnp.bfloat16)
                    part = jnp.sum(weight.reshape(tokens // 8, 8, SPAN), axis=0)
                    total = part if total is None else total + part
                total = jnp.sum(total, axis=0, keepdims=True)
                if not first:
                    total = total + fades[tile] * stats_in[g, 1:2, lanes]
                tops.append(top)
                totals.append(total)
            both = lax.dot_general(
                v, p_ref[u], (((0,), (0,)), ((), ())), preferred_element_type=jnp.float32
            )
            for tile in range(groups * tokens // SPAN):
                lanes = slice(tile * SPAN, (tile + 1) * SPAN)
                mixed = both[:HEAD_WIDTH, lanes] + both[HEAD_WIDTH:, lanes]
                if not first:
                    mixed = mixed + fades[tile] * mixed_in[g, :, lanes]
                if not last:
                    result_ref[g, :, lanes] = mixed
                    stats_ref[g, 0:1, lanes] = tops[tile]
                    stats_ref[g, 1:2, lanes] = totals[tile]
                    continue
                mixed = mixed * (1.0 / totals[tile])
                check = jnp.sum(mixed, axis=0, keepdims=True) * inverse_root
                mixed = jnp.transpose(mixed).astype(result_ref.dtype)
                for j in range(SPAN // tokens):
                    h = tile * (SPAN // tokens) + j
                    at = pl.multiple_of((g * groups + h) * HEAD_WIDTH, HEAD_WIDTH)
                    result_ref[:, pl.ds(at, HEAD_WIDTH)] = mixed[j * tokens : (j + 1) * tokens]
                    check_ref[pl.ds(g * groups + h, 1), :] = check[:, j * tokens : (j + 1) * tokens]

    if last:
        stats_ref[...] = jnp.transpose(check_ref[...])


def absorb(prepared, pieces, begin, state, last, tokens):
    kv_heads, rows, depth = prepared[0].shape
    groups = rows // tokens
    count = len(pieces)
    per_step = 2 if kv_heads % 2 == 0 else 1
    keys = tokens * count
    width = kv_heads * groups * HEAD_WIDTH
    first = state is None
    whole = [len(piece) == 1 for piece in pieces]
    operands = [block for piece in pieces for block in piece]
    vmem = pl.BlockSpec(memory_space=pltpu.VMEM)
    operands += [*prepared, *(() if first else state)]
    if last:
        out_shape = [
            jax.ShapeDtypeStruct((tokens, width), jnp.bfloat16),
            jax.ShapeDtypeStruct((tokens, kv_heads * groups), jnp.float32),
        ]
    else:
        out_shape = [
            jax.ShapeDtypeStruct((kv_heads, HEAD_WIDTH, rows), jnp.float32),
            jax.ShapeDtypeStruct((kv_heads, 2, rows), jnp.float32),
        ]
    return pl.pallas_call(
        functools.partial(
            absorb_kernel,
            groups=groups,
            tokens=tokens,
            per_step=per_step,
            begin=begin,
            whole=whole,
            first=first,
            last=last,
        ),
        in_specs=[vmem] * len(operands),
        out_specs=[vmem] * 2,
        out_shape=out_shape,
        scratch_shapes=[
            pltpu.VMEM((per_step, keys, rows), jnp.float32),
            pltpu.VMEM((per_step, keys, rows), jnp.bfloat16),
            pltpu.VMEM((kv_heads * groups, tokens), jnp.float32),
        ],
        compiler_params=pltpu.CompilerParams(vmem_limit_bytes=32 * 1024 * 1024),
        cost_estimate=pl.CostEstimate(
            flops=16 * tokens * width * keys,
            bytes_accessed=16 * tokens * width,
            transcendentals=tokens * width // HEAD_WIDTH * keys,
        ),
    )(*operands)


def local(queries, keys, values, key_scale, value_scale, span_order, block_keep):
    tokens = queries.shape[0]
    kv_heads = keys.shape[1] // HEAD_WIDTH
    sizes = ctx_size, head_size = lax.axis_size("ctx"), lax.axis_size("head")
    size = ctx_size // 2 * head_size
    batch = 2 * SPAN // tokens

    def device(place, core):
        row, column = place // head_size, place % head_size
        return (2 * row + core) * head_size + (column if row % 2 == 0 else head_size - 1 - column)

    def around(block, distance):
        route = [
            (device(p, core), device((p + distance) % size, core))
            for p in range(size)
            for core in range(2)
        ]
        return lax.ppermute(block, ("ctx", "head"), route)

    def to_other_core(piece):
        return [lax.ppermute(block, "ctx", [(i, i ^ 1) for i in range(ctx_size)]) for block in piece]

    def swap_heads(block, flip):
        return lax.ppermute(block, "head", [(i, i ^ flip) for i in range(head_size)])

    sources = [(0, 0)]
    for step in range(1, size // 2 + 2):
        if step < size // 2:
            sources += [(step, 0), (-step, 0)]
        elif step == size // 2:
            sources += [(step - 1, 1), (1 - step, 1), (step, 0)]
        if step == 1:
            sources += [(0, 1)]
        elif step < size // 2:
            sources += [(step - 1, 1), (1 - step, 1)]
        elif step > size // 2:
            sources += [(step - 1, 1)]

    block = lax.optimization_barrier(jnp.concatenate([keys, values], axis=0))
    scale = jnp.concatenate([jnp.transpose(key_scale), jnp.transpose(value_scale)], axis=0)
    scales, pieces, done = [scale[None]], [[block]], 0
    fresh, forward, backward = [[block]], block, block
    prepared, rows, state = None, None, None
    for step in range(1, size // 2 + 2):
        crossed = [to_other_core(piece) for piece in fresh]
        sent = []
        if step < size // 2:
            forward, backward = around(forward, 1), around(backward, -1)
            sent = [[forward], [backward]]
        elif step == size // 2:
            sent = [[around(forward[:tokens], 1), around(backward[tokens:], -1)]]
        held = sum(scale.shape[0] for scale in scales)
        complete = held == head_size
        if not complete:
            scales = scales + [swap_heads(jnp.concatenate(scales, axis=0), held)]
        if step == 2:
            prepared = prepare(queries, span_order, block_keep, sources, kv_heads, sizes)
        if complete:
            if rows is None:
                rows = scale_rows(scales, sources, tokens, sizes)
            ready = (len(pieces) - done) // batch * batch if step < size // 2 else 0
            now = pieces[done : done + ready]
            if step == size // 2:
                now = pieces[done:] + crossed
                ready = len(now)
            if ready:
                state = absorb((*prepared, *rows), now, done, state, False, tokens)
                done += ready
        sent, crossed, scales, prepared, rows, state = lax.optimization_barrier(
            (sent, crossed, scales, prepared, rows, state)
        )
        fresh = sent
        if step < size // 2:
            forward, backward = fresh[0][0], fresh[1][0]
        pieces = pieces + (sent + crossed if step < size // 2 else crossed + sent)
    return tuple(absorb((*prepared, *rows), pieces[done:], done, state, True, tokens))


def solution(mesh):
    rows = P(("dp", "ctx", "head"), None)
    return jax.shard_map(
        local,
        mesh=mesh,
        in_specs=(rows, rows, rows, P("dp", "head"), P("dp", "head"), P(), P()),
        out_specs=(rows, rows),
        check_vma=False,
    )
```

```python
import functools
import math

import jax
import jax.numpy as jnp
from jax import lax
from jax.experimental import pallas as pl
from jax.experimental.pallas import tpu as pltpu
from jax.sharding import PartitionSpec as P

HEAD_WIDTH = 128
SPAN = 128
LOG2E = 1.4426950408889634
MASKED = -1e30


def source_start(distance, flip, tokens, ctx_size, head_size):
    ctx, head = lax.axis_index("ctx"), lax.axis_index("head")
    size = ctx_size // 2 * head_size
    row = ctx // 2
    place = row * head_size + jnp.where(row % 2 == 0, head, head_size - 1 - head)
    place = lax.rem(place - distance + size, size)
    row, column = place // head_size, place % head_size
    column = jnp.where(row % 2 == 0, column, head_size - 1 - column)
    return ((2 * row + (ctx % 2) ^ flip) * head_size + column) * tokens


def prepare_kernel(order_ref, keep_ref, q_ref, qa_ref, hot_ref, mask_ref, *, groups, per_step, sources, ctx_size, head_size):
    step = pl.program_id(0)
    tokens = q_ref.shape[0]
    row = lax.broadcasted_iota(jnp.int32, (tokens, SPAN), 0)
    lane = lax.broadcasted_iota(jnp.int32, (tokens, SPAN), 1)

    @pl.when(step == 0)
    def _():
        own_start = source_start(0, 0, tokens, ctx_size, head_size)
        own = own_start // SPAN
        for i, source in enumerate(sources):
            start = source_start(*source, tokens, ctx_size, head_size)
            span = start // SPAN
            seen = (order_ref[span] < order_ref[own]) & (keep_ref[own, span] > 0)
            whole = jnp.where(seen, 0.0, MASKED)
            causal = jnp.where(row + (start - own_start) <= lane, 0.0, MASKED)
            mask = jnp.where(own == span, causal, whole)
            mask_ref[i * tokens : (i + 1) * tokens, :] = mask.astype(jnp.bfloat16)
        row_all = lax.broadcasted_iota(jnp.int32, hot_ref.shape, 0)
        lane_all = lax.broadcasted_iota(jnp.int32, hot_ref.shape, 1)
        hot = jnp.where(row_all == lane_all % tokens, 1.0, 0.0)
        hot_ref[...] = hot.astype(jnp.bfloat16)

    for u in range(per_step):
        heads = [
            q_ref[:, (u * groups + h) * HEAD_WIDTH : (u * groups + h + 1) * HEAD_WIDTH]
            for h in range(groups)
        ]
        qa_ref[u] = jnp.transpose(jnp.concatenate(heads, axis=0))


def prepare(queries, span_order, block_keep, sources, kv_heads, sizes):
    tokens, width = queries.shape
    groups = width // HEAD_WIDTH // kv_heads
    per_step = 2 if kv_heads % 2 == 0 else 1
    rows = groups * tokens
    smem = pl.BlockSpec(memory_space=pltpu.SMEM)
    return pl.pallas_call(
        functools.partial(
            prepare_kernel,
            groups=groups,
            per_step=per_step,
            sources=sources,
            ctx_size=sizes[0],
            head_size=sizes[1],
        ),
        grid=(kv_heads // per_step,),
        in_specs=[smem, smem, pl.BlockSpec((tokens, per_step * groups * HEAD_WIDTH), lambda s: (0, s))],
        out_specs=[
            pl.BlockSpec((per_step, HEAD_WIDTH, rows), lambda s: (s, 0, 0)),
            pl.BlockSpec((SPAN, rows), lambda s: (0, 0)),
            pl.BlockSpec((tokens * len(sources), SPAN), lambda s: (0, 0)),
        ],
        out_shape=[
            jax.ShapeDtypeStruct((kv_heads, HEAD_WIDTH, rows), jnp.bfloat16),
            jax.ShapeDtypeStruct((SPAN, rows), jnp.bfloat16),
            jax.ShapeDtypeStruct((tokens * len(sources), SPAN), jnp.bfloat16),
        ],
        compiler_params=pltpu.CompilerParams(vmem_limit_bytes=32 * 1024 * 1024),
        cost_estimate=pl.CostEstimate(
            flops=8 * tokens * width, bytes_accessed=16 * tokens * width, transcendentals=0
        ),
    )(span_order, block_keep, queries)


def scale_rows_kernel(*refs, owners, tokens, kv_local, sources, ctx_size, head_size):
    scale_in = refs[: len(owners)]
    key_scale_ref, value_scale_ref, scale_ref, scale_sem = refs[len(owners) :]
    inverse_root = 1.0 / math.sqrt(HEAD_WIDTH)
    head = lax.axis_index("head")
    copies, flip = [], 0
    for ref, count in zip(scale_in, owners):
        for i in range(count):
            copies.append(
                pltpu.make_async_copy(ref.at[i], scale_ref.at[head ^ flip], scale_sem.at[flip])
            )
            flip += 1
    for copy in copies:
        copy.start()
    spans = [
        source_start(*source, tokens, ctx_size, head_size) // SPAN for source in sources
    ]
    for copy in copies:
        copy.wait()
    lane = lax.broadcasted_iota(jnp.int32, (1, SPAN), 1)
    for g in range(head_size * kv_local):
        owner, member = g // kv_local, g % kv_local
        for i, span in enumerate(spans):
            factor = scale_ref[owner, member, span] * (inverse_root * LOG2E)
            key_scale_ref[g, i : i + 1, :] = jnp.full((1, SPAN), factor, jnp.float32)
        per_tile = SPAN // tokens
        for tile in range(len(sources) // per_tile):
            row = None
            for i in range(per_tile):
                factor = scale_ref[owner, kv_local + member, spans[tile * per_tile + i]]
                if row is None:
                    row = jnp.full((1, SPAN), factor, jnp.float32)
                else:
                    row = jnp.where(lane >= i * tokens, factor, row)
            value_scale_ref[g, :, tile * SPAN : (tile + 1) * SPAN] = row


def scale_rows(scales, sources, tokens, sizes):
    kv_local = scales[0].shape[1] // 2
    kv_heads = sizes[1] * kv_local
    return pl.pallas_call(
        functools.partial(
            scale_rows_kernel,
            owners=[scale.shape[0] for scale in scales],
            tokens=tokens,
            kv_local=kv_local,
            sources=sources,
            ctx_size=sizes[0],
            head_size=sizes[1],
        ),
        in_specs=[pl.BlockSpec(memory_space=pl.ANY)] * len(scales),
        out_specs=[pl.BlockSpec(memory_space=pltpu.VMEM)] * 2,
        out_shape=[
            jax.ShapeDtypeStruct((kv_heads, len(sources), SPAN), jnp.float32),
            jax.ShapeDtypeStruct((kv_heads, 1, len(sources) * tokens), jnp.float32),
        ],
        scratch_shapes=[
            pltpu.SMEM((sizes[1],) + scales[0].shape[1:], jnp.float32),
            pltpu.SemaphoreType.DMA((sizes[1],)),
        ],
        compiler_params=pltpu.CompilerParams(vmem_limit_bytes=32 * 1024 * 1024),
        cost_estimate=pl.CostEstimate(
            flops=10**8, bytes_accessed=10**6, transcendentals=0
        ),
    )(*scales)


def absorb_kernel(*refs, groups, tokens, per_step, begin, count, first, last):
    refs = list(refs)
    pieces = [(refs.pop(0), refs.pop(0)) for _ in range(count)]
    qa_ref, hot_ref, mask_ref, key_scale_ref, value_scale_ref = [refs.pop(0) for _ in range(5)]
    mixed_in, stats_in = (None, None) if first else (refs.pop(0), refs.pop(0))
    result_ref, stats_ref, x_ref, p_ref, check_ref = refs
    step = pl.program_id(0)
    inverse_root = 1.0 / math.sqrt(HEAD_WIDTH)
    for u in range(per_step):
        g = step * per_step + u
        cols = pl.ds(pl.multiple_of(g * HEAD_WIDTH, HEAD_WIDTH), HEAD_WIDTH)
        k = jnp.concatenate([key_ref[:, cols] for key_ref, _ in pieces], axis=0)
        k = jnp.concatenate([k, mask_ref[begin * tokens : (begin + count) * tokens, :]], axis=1)
        x_ref[u] = jnp.dot(
            k,
            jnp.concatenate([qa_ref[u], hot_ref[...]], axis=0),
            preferred_element_type=jnp.float32,
        )
    for u in range(per_step):
        g = step * per_step + u
        cols = pl.ds(pl.multiple_of(g * HEAD_WIDTH, HEAD_WIDTH), HEAD_WIDTH)
        factors = [key_scale_ref[u, begin + i : begin + i + 1, :] for i in range(count)]
        v = jnp.concatenate([value_ref[:, cols] for _, value_ref in pieces], axis=0)
        v = jnp.transpose(v).astype(jnp.float32)
        v = v * value_scale_ref[u, :, begin * tokens : (begin + count) * tokens]
        high = v.astype(jnp.bfloat16)
        low = (v - high.astype(jnp.float32)).astype(jnp.bfloat16)
        v = jnp.concatenate([high, low], axis=0)
        tops, totals, fades = [], [], []
        for tile in range(groups * tokens // SPAN):
            lanes = slice(tile * SPAN, (tile + 1) * SPAN)
            top = None
            for i, factor in enumerate(factors):
                x = x_ref[u, i * tokens : (i + 1) * tokens, lanes]
                highest = jnp.max(x.reshape(tokens // 8, 8, SPAN), axis=0) * factor
                top = highest if top is None else jnp.maximum(top, highest)
            top = jnp.max(top, axis=0, keepdims=True)
            if not first:
                before = stats_in[u, 0:1, lanes]
                top = jnp.maximum(top, before)
                fades.append(jnp.exp2(before - top))
            total = None
            for i, factor in enumerate(factors):
                keys = slice(i * tokens, (i + 1) * tokens)
                weight = jnp.exp2(x_ref[u, keys, lanes] * factor - top)
                p_ref[u, keys, lanes] = weight.astype(jnp.bfloat16)
                part = jnp.sum(weight.reshape(tokens // 8, 8, SPAN), axis=0)
                total = part if total is None else total + part
            total = jnp.sum(total, axis=0, keepdims=True)
            if not first:
                total = total + fades[tile] * stats_in[u, 1:2, lanes]
            tops.append(top)
            totals.append(total)
        both = jnp.dot(v, p_ref[u], preferred_element_type=jnp.float32)
        for tile in range(groups * tokens // SPAN):
            lanes = slice(tile * SPAN, (tile + 1) * SPAN)
            mixed = both[:HEAD_WIDTH, lanes] + both[HEAD_WIDTH:, lanes]
            if not first:
                mixed = mixed + fades[tile] * mixed_in[u, :, lanes]
            if not last:
                result_ref[u, :, lanes] = mixed
                stats_ref[u, 0:1, lanes] = tops[tile]
                stats_ref[u, 1:2, lanes] = totals[tile]
                continue
            mixed = mixed * (1.0 / totals[tile])
            check = jnp.sum(mixed, axis=0, keepdims=True) * inverse_root
            mixed = jnp.transpose(mixed).astype(result_ref.dtype)
            for j in range(SPAN // tokens):
                h = tile * (SPAN // tokens) + j
                at = (u * groups + h) * HEAD_WIDTH
                result_ref[:, at : at + HEAD_WIDTH] = mixed[j * tokens : (j + 1) * tokens]
                check_ref[pl.ds(g * groups + h, 1), :] = check[:, j * tokens : (j + 1) * tokens]
    if last:

        @pl.when(step == pl.num_programs(0) - 1)
        def _():
            stats_ref[...] = jnp.transpose(check_ref[...])


def absorb(prepared, pieces, begin, state, last, tokens):
    kv_heads, _, rows = prepared[0].shape
    groups = rows // tokens
    count = len(pieces)
    per_step = 2 if kv_heads % 2 == 0 else 1
    keys = tokens * count
    width = kv_heads * groups * HEAD_WIDTH
    first = state is None
    mixed = pl.BlockSpec((per_step, HEAD_WIDTH, rows), lambda s: (s, 0, 0))
    stats = pl.BlockSpec((per_step, 2, rows), lambda s: (s, 0, 0))
    in_specs, operands = [], []
    for piece in pieces:
        joined = len(piece) == 1
        half = (tokens, piece[0].shape[1])
        in_specs.append(pl.BlockSpec(half, lambda s: (0, 0)))
        in_specs.append(pl.BlockSpec(half, lambda s: (1, 0)) if joined else in_specs[-1])
        operands += [piece[0], piece[-1]]
    in_specs += [
        pl.BlockSpec((per_step,) + prepared[0].shape[1:], lambda s: (s, 0, 0)),
        pl.BlockSpec(prepared[1].shape, lambda s: (0, 0)),
        pl.BlockSpec(prepared[2].shape, lambda s: (0, 0)),
        pl.BlockSpec((per_step,) + prepared[3].shape[1:], lambda s: (s, 0, 0)),
        pl.BlockSpec((per_step,) + prepared[4].shape[1:], lambda s: (s, 0, 0)),
    ]
    in_specs += [] if first else [mixed, stats]
    if last:
        out_specs = [
            pl.BlockSpec((tokens, per_step * groups * HEAD_WIDTH), lambda s: (0, s)),
            pl.BlockSpec((tokens, kv_heads * groups), lambda s: (0, 0)),
        ]
        out_shape = [
            jax.ShapeDtypeStruct((tokens, width), jnp.bfloat16),
            jax.ShapeDtypeStruct((tokens, kv_heads * groups), jnp.float32),
        ]
    else:
        out_specs = [mixed, stats]
        out_shape = [
            jax.ShapeDtypeStruct((kv_heads, HEAD_WIDTH, rows), jnp.float32),
            jax.ShapeDtypeStruct((kv_heads, 2, rows), jnp.float32),
        ]
    return pl.pallas_call(
        functools.partial(
            absorb_kernel,
            groups=groups,
            tokens=tokens,
            per_step=per_step,
            begin=begin,
            count=count,
            first=first,
            last=last,
        ),
        grid=(kv_heads // per_step,),
        in_specs=in_specs,
        out_specs=out_specs,
        out_shape=out_shape,
        scratch_shapes=[
            pltpu.VMEM((per_step, keys, rows), jnp.float32),
            pltpu.VMEM((per_step, keys, rows), jnp.bfloat16),
            pltpu.VMEM((kv_heads * groups, tokens), jnp.float32),
        ],
        compiler_params=pltpu.CompilerParams(vmem_limit_bytes=32 * 1024 * 1024),
        cost_estimate=pl.CostEstimate(
            flops=16 * tokens * width * keys,
            bytes_accessed=16 * tokens * width,
            transcendentals=tokens * width // HEAD_WIDTH * keys,
        ),
    )(*operands, *prepared, *(() if first else state))


def local(queries, keys, values, key_scale, value_scale, span_order, block_keep):
    tokens = queries.shape[0]
    kv_heads = keys.shape[1] // HEAD_WIDTH
    sizes = ctx_size, head_size = lax.axis_size("ctx"), lax.axis_size("head")
    size = ctx_size // 2 * head_size
    batch = 2 * SPAN // tokens

    def device(place, core):
        row, column = place // head_size, place % head_size
        return (2 * row + core) * head_size + (column if row % 2 == 0 else head_size - 1 - column)

    def around(block, distance):
        route = [
            (device(p, core), device((p + distance) % size, core))
            for p in range(size)
            for core in range(2)
        ]
        return lax.ppermute(block, ("ctx", "head"), route)

    def to_other_core(piece):
        return [lax.ppermute(block, "ctx", [(i, i ^ 1) for i in range(ctx_size)]) for block in piece]

    def swap_heads(block, flip):
        return lax.ppermute(block, "head", [(i, i ^ flip) for i in range(head_size)])

    sources = [(0, 0)]
    for step in range(1, size // 2 + 2):
        if step < size // 2:
            sources += [(step, 0), (-step, 0)]
        elif step == size // 2:
            sources += [(step - 1, 1), (1 - step, 1), (step, 0)]
        if step == 1:
            sources += [(0, 1)]
        elif step < size // 2:
            sources += [(step - 1, 1), (1 - step, 1)]
        elif step > size // 2:
            sources += [(step - 1, 1)]

    block = lax.optimization_barrier(jnp.concatenate([keys, values], axis=0))
    scale = jnp.concatenate([jnp.transpose(key_scale), jnp.transpose(value_scale)], axis=0)
    scales, pieces, done = [scale[None]], [[block]], 0
    fresh, forward, backward = [[block]], block, block
    prepared, rows, state = None, None, None
    for step in range(1, size // 2 + 2):
        crossed = [to_other_core(piece) for piece in fresh]
        sent = []
        if step < size // 2:
            forward, backward = around(forward, 1), around(backward, -1)
            sent = [[forward], [backward]]
        elif step == size // 2:
            sent = [[around(forward[:tokens], 1), around(backward[tokens:], -1)]]
        held = sum(scale.shape[0] for scale in scales)
        complete = held == head_size
        if not complete:
            scales = scales + [swap_heads(jnp.concatenate(scales, axis=0), held)]
        if step == 1:
            prepared = prepare(queries, span_order, block_keep, sources, kv_heads, sizes)
        if complete:
            if rows is None:
                rows = scale_rows(scales, sources, tokens, sizes)
            ready = (len(pieces) - done) // batch * batch if step < size // 2 else 0
            now = pieces[done : done + ready]
            if step == size // 2:
                now = pieces[done:] + crossed
                ready = len(now)
            if ready:
                state = absorb((*prepared, *rows), now, done, state, False, tokens)
                done += ready
        sent, crossed, scales, prepared, rows, state = lax.optimization_barrier(
            (sent, crossed, scales, prepared, rows, state)
        )
        fresh = sent
        if step < size // 2:
            forward, backward = fresh[0][0], fresh[1][0]
        pieces = pieces + (sent + crossed if step < size // 2 else crossed + sent)
    return tuple(absorb((*prepared, *rows), pieces[done:], done, state, True, tokens))


def solution(mesh):
    rows = P(("dp", "ctx", "head"), None)
    return jax.shard_map(
        local,
        mesh=mesh,
        in_specs=(rows, rows, rows, P("dp", "head"), P("dp", "head"), P(), P()),
        out_specs=(rows, rows),
        check_vma=False,
    )
```

```python
import functools
import math

import jax
import jax.numpy as jnp
from jax import lax
from jax.experimental import pallas as pl
from jax.experimental.pallas import tpu as pltpu
from jax.sharding import PartitionSpec as P

HEAD_WIDTH = 128
SPAN = 128
LOG2E = 1.4426950408889634
MASKED = -1e30


def source_start(distance, flip, tokens, ctx_size, head_size):
    ctx, head = lax.axis_index("ctx"), lax.axis_index("head")
    size = ctx_size // 2 * head_size
    row = ctx // 2
    place = row * head_size + jnp.where(row % 2 == 0, head, head_size - 1 - head)
    place = lax.rem(place - distance + size, size)
    row, column = place // head_size, place % head_size
    column = jnp.where(row % 2 == 0, column, head_size - 1 - column)
    return ((2 * row + (ctx % 2) ^ flip) * head_size + column) * tokens


def prepare_kernel(order_ref, keep_ref, q_ref, qa_ref, hot_ref, mask_ref, *, groups, per_step, sources, ctx_size, head_size):
    step = pl.program_id(0)
    tokens = q_ref.shape[0]
    row = lax.broadcasted_iota(jnp.int32, (tokens, SPAN), 0)
    lane = lax.broadcasted_iota(jnp.int32, (tokens, SPAN), 1)

    @pl.when(step == 0)
    def _():
        own_start = source_start(0, 0, tokens, ctx_size, head_size)
        own = own_start // SPAN
        for i, source in enumerate(sources):
            start = source_start(*source, tokens, ctx_size, head_size)
            span = start // SPAN
            seen = (order_ref[span] < order_ref[own]) & (keep_ref[own, span] > 0)
            whole = jnp.where(seen, 0.0, MASKED)
            causal = jnp.where(row + (start - own_start) <= lane, 0.0, MASKED)
            mask = jnp.where(own == span, causal, whole)
            mask_ref[i * tokens : (i + 1) * tokens, :] = mask.astype(jnp.bfloat16)
        row_all = lax.broadcasted_iota(jnp.int32, hot_ref.shape, 0)
        lane_all = lax.broadcasted_iota(jnp.int32, hot_ref.shape, 1)
        hot = jnp.where(row_all == lane_all % tokens, 1.0, 0.0)
        hot_ref[...] = hot.astype(jnp.bfloat16)

    for u in range(per_step):
        heads = [
            q_ref[:, (u * groups + h) * HEAD_WIDTH : (u * groups + h + 1) * HEAD_WIDTH]
            for h in range(groups)
        ]
        qa_ref[u] = jnp.transpose(jnp.concatenate(heads, axis=0))


def prepare(queries, span_order, block_keep, sources, kv_heads, sizes):
    tokens, width = queries.shape
    groups = width // HEAD_WIDTH // kv_heads
    per_step = 2 if kv_heads % 2 == 0 else 1
    rows = groups * tokens
    smem = pl.BlockSpec(memory_space=pltpu.SMEM)
    return pl.pallas_call(
        functools.partial(
            prepare_kernel,
            groups=groups,
            per_step=per_step,
            sources=sources,
            ctx_size=sizes[0],
            head_size=sizes[1],
        ),
        grid=(kv_heads // per_step,),
        in_specs=[smem, smem, pl.BlockSpec((tokens, per_step * groups * HEAD_WIDTH), lambda s: (0, s))],
        out_specs=[
            pl.BlockSpec((per_step, HEAD_WIDTH, rows), lambda s: (s, 0, 0)),
            pl.BlockSpec((SPAN, rows), lambda s: (0, 0)),
            pl.BlockSpec((tokens * len(sources), SPAN), lambda s: (0, 0)),
        ],
        out_shape=[
            jax.ShapeDtypeStruct((kv_heads, HEAD_WIDTH, rows), jnp.bfloat16),
            jax.ShapeDtypeStruct((SPAN, rows), jnp.bfloat16),
            jax.ShapeDtypeStruct((tokens * len(sources), SPAN), jnp.bfloat16),
        ],
        compiler_params=pltpu.CompilerParams(vmem_limit_bytes=32 * 1024 * 1024),
        cost_estimate=pl.CostEstimate(
            flops=8 * tokens * width, bytes_accessed=16 * tokens * width, transcendentals=0
        ),
    )(span_order, block_keep, queries)


def scale_rows_kernel(*refs, owners, tokens, kv_local, sources, ctx_size, head_size):
    scale_in = refs[: len(owners)]
    key_scale_ref, value_scale_ref, scale_ref, scale_sem = refs[len(owners) :]
    inverse_root = 1.0 / math.sqrt(HEAD_WIDTH)
    head = lax.axis_index("head")
    copies, flip = [], 0
    for ref, count in zip(scale_in, owners):
        for i in range(count):
            copies.append(
                pltpu.make_async_copy(ref.at[i], scale_ref.at[head ^ flip], scale_sem.at[flip])
            )
            flip += 1
    for copy in copies:
        copy.start()
    spans = [
        source_start(*source, tokens, ctx_size, head_size) // SPAN for source in sources
    ]
    for copy in copies:
        copy.wait()
    lane = lax.broadcasted_iota(jnp.int32, (1, SPAN), 1)
    for g in range(head_size * kv_local):
        owner, member = g // kv_local, g % kv_local
        for i, span in enumerate(spans):
            factor = scale_ref[owner, member, span] * (inverse_root * LOG2E)
            key_scale_ref[g, i : i + 1, :] = jnp.full((1, SPAN), factor, jnp.float32)
        per_tile = SPAN // tokens
        for tile in range(len(sources) // per_tile):
            row = None
            for i in range(per_tile):
                factor = scale_ref[owner, kv_local + member, spans[tile * per_tile + i]]
                if row is None:
                    row = jnp.full((1, SPAN), factor, jnp.float32)
                else:
                    row = jnp.where(lane >= i * tokens, factor, row)
            value_scale_ref[g, :, tile * SPAN : (tile + 1) * SPAN] = row


def scale_rows(scales, sources, tokens, sizes):
    kv_local = scales[0].shape[1] // 2
    kv_heads = sizes[1] * kv_local
    return pl.pallas_call(
        functools.partial(
            scale_rows_kernel,
            owners=[scale.shape[0] for scale in scales],
            tokens=tokens,
            kv_local=kv_local,
            sources=sources,
            ctx_size=sizes[0],
            head_size=sizes[1],
        ),
        in_specs=[pl.BlockSpec(memory_space=pl.ANY)] * len(scales),
        out_specs=[pl.BlockSpec(memory_space=pltpu.VMEM)] * 2,
        out_shape=[
            jax.ShapeDtypeStruct((kv_heads, len(sources), SPAN), jnp.float32),
            jax.ShapeDtypeStruct((kv_heads, 1, len(sources) * tokens), jnp.float32),
        ],
        scratch_shapes=[
            pltpu.SMEM((sizes[1],) + scales[0].shape[1:], jnp.float32),
            pltpu.SemaphoreType.DMA((sizes[1],)),
        ],
        compiler_params=pltpu.CompilerParams(vmem_limit_bytes=32 * 1024 * 1024),
        cost_estimate=pl.CostEstimate(
            flops=10**8, bytes_accessed=10**6, transcendentals=0
        ),
    )(*scales)


def absorb_kernel(*refs, groups, tokens, per_step, begin, count, first, last):
    refs = list(refs)
    pieces = [(refs.pop(0), refs.pop(0)) for _ in range(count)]
    qa_ref, hot_ref, mask_ref, key_scale_ref, value_scale_ref = [refs.pop(0) for _ in range(5)]
    mixed_in, stats_in = (None, None) if first else (refs.pop(0), refs.pop(0))
    result_ref, stats_ref, x_ref, p_ref, check_ref = refs
    step = pl.program_id(0)
    inverse_root = 1.0 / math.sqrt(HEAD_WIDTH)
    for u in range(per_step):
        g = step * per_step + u
        cols = pl.ds(pl.multiple_of(g * HEAD_WIDTH, HEAD_WIDTH), HEAD_WIDTH)
        k = jnp.concatenate([key_ref[:, cols] for key_ref, _ in pieces], axis=0)
        k = jnp.concatenate([k, mask_ref[begin * tokens : (begin + count) * tokens, :]], axis=1)
        x_ref[u] = jnp.dot(
            k,
            jnp.concatenate([qa_ref[u], hot_ref[...]], axis=0),
            preferred_element_type=jnp.float32,
        )
    rows = []
    for u in range(per_step):
        g = step * per_step + u
        cols = pl.ds(pl.multiple_of(g * HEAD_WIDTH, HEAD_WIDTH), HEAD_WIDTH)
        factors = [key_scale_ref[u, begin + i : begin + i + 1, :] for i in range(count)]
        tops, totals, fades = [], [], []
        rows.append((tops, totals, fades))
        for tile in range(groups * tokens // SPAN):
            lanes = slice(tile * SPAN, (tile + 1) * SPAN)
            top = None
            for i, factor in enumerate(factors):
                x = x_ref[u, i * tokens : (i + 1) * tokens, lanes]
                highest = jnp.max(x.reshape(tokens // 8, 8, SPAN), axis=0) * factor
                top = highest if top is None else jnp.maximum(top, highest)
            top = jnp.max(top, axis=0, keepdims=True)
            if not first:
                before = stats_in[u, 0:1, lanes]
                top = jnp.maximum(top, before)
                fades.append(jnp.exp2(before - top))
            total = None
            for i, factor in enumerate(factors):
                keys = slice(i * tokens, (i + 1) * tokens)
                weight = jnp.exp2(x_ref[u, keys, lanes] * factor - top)
                p_ref[u, keys, lanes] = weight.astype(jnp.bfloat16)
                part = jnp.sum(weight.reshape(tokens // 8, 8, SPAN), axis=0)
                total = part if total is None else total + part
            total = jnp.sum(total, axis=0, keepdims=True)
            if not first:
                total = total + fades[tile] * stats_in[u, 1:2, lanes]
            tops.append(top)
            totals.append(total)
    for u in range(per_step):
        g = step * per_step + u
        cols = pl.ds(pl.multiple_of(g * HEAD_WIDTH, HEAD_WIDTH), HEAD_WIDTH)
        tops, totals, fades = rows[u]
        v = jnp.concatenate([value_ref[:, cols] for _, value_ref in pieces], axis=0)
        v = jnp.transpose(v).astype(jnp.float32)
        v = v * value_scale_ref[u, :, begin * tokens : (begin + count) * tokens]
        high = v.astype(jnp.bfloat16)
        low = (v - high.astype(jnp.float32)).astype(jnp.bfloat16)
        v = jnp.concatenate([high, low], axis=0)
        both = jnp.dot(v, p_ref[u], preferred_element_type=jnp.float32)
        for tile in range(groups * tokens // SPAN):
            lanes = slice(tile * SPAN, (tile + 1) * SPAN)
            mixed = both[:HEAD_WIDTH, lanes] + both[HEAD_WIDTH:, lanes]
            if not first:
                mixed = mixed + fades[tile] * mixed_in[u, :, lanes]
            if not last:
                result_ref[u, :, lanes] = mixed
                stats_ref[u, 0:1, lanes] = tops[tile]
                stats_ref[u, 1:2, lanes] = totals[tile]
                continue
            mixed = mixed * (1.0 / totals[tile])
            check = jnp.sum(mixed, axis=0, keepdims=True) * inverse_root
            mixed = jnp.transpose(mixed).astype(result_ref.dtype)
            for j in range(SPAN // tokens):
                h = tile * (SPAN // tokens) + j
                at = (u * groups + h) * HEAD_WIDTH
                result_ref[:, at : at + HEAD_WIDTH] = mixed[j * tokens : (j + 1) * tokens]
                check_ref[pl.ds(g * groups + h, 1), :] = check[:, j * tokens : (j + 1) * tokens]
    if last:

        @pl.when(step == pl.num_programs(0) - 1)
        def _():
            stats_ref[...] = jnp.transpose(check_ref[...])


def absorb(prepared, pieces, begin, state, last, tokens):
    kv_heads, _, rows = prepared[0].shape
    groups = rows // tokens
    count = len(pieces)
    per_step = 4 if kv_heads % 4 == 0 else 1
    keys = tokens * count
    width = kv_heads * groups * HEAD_WIDTH
    first = state is None
    mixed = pl.BlockSpec((per_step, HEAD_WIDTH, rows), lambda s: (s, 0, 0))
    stats = pl.BlockSpec((per_step, 2, rows), lambda s: (s, 0, 0))
    in_specs, operands = [], []
    for piece in pieces:
        joined = len(piece) == 1
        half = (tokens, piece[0].shape[1])
        in_specs.append(pl.BlockSpec(half, lambda s: (0, 0)))
        in_specs.append(pl.BlockSpec(half, lambda s: (1, 0)) if joined else in_specs[-1])
        operands += [piece[0], piece[-1]]
    in_specs += [
        pl.BlockSpec((per_step,) + prepared[0].shape[1:], lambda s: (s, 0, 0)),
        pl.BlockSpec(prepared[1].shape, lambda s: (0, 0)),
        pl.BlockSpec(prepared[2].shape, lambda s: (0, 0)),
        pl.BlockSpec((per_step,) + prepared[3].shape[1:], lambda s: (s, 0, 0)),
        pl.BlockSpec((per_step,) + prepared[4].shape[1:], lambda s: (s, 0, 0)),
    ]
    in_specs += [] if first else [mixed, stats]
    if last:
        out_specs = [
            pl.BlockSpec((tokens, per_step * groups * HEAD_WIDTH), lambda s: (0, s)),
            pl.BlockSpec((tokens, kv_heads * groups), lambda s: (0, 0)),
        ]
        out_shape = [
            jax.ShapeDtypeStruct((tokens, width), jnp.bfloat16),
            jax.ShapeDtypeStruct((tokens, kv_heads * groups), jnp.float32),
        ]
    else:
        out_specs = [mixed, stats]
        out_shape = [
            jax.ShapeDtypeStruct((kv_heads, HEAD_WIDTH, rows), jnp.float32),
            jax.ShapeDtypeStruct((kv_heads, 2, rows), jnp.float32),
        ]
    return pl.pallas_call(
        functools.partial(
            absorb_kernel,
            groups=groups,
            tokens=tokens,
            per_step=per_step,
            begin=begin,
            count=count,
            first=first,
            last=last,
        ),
        grid=(kv_heads // per_step,),
        in_specs=in_specs,
        out_specs=out_specs,
        out_shape=out_shape,
        scratch_shapes=[
            pltpu.VMEM((per_step, keys, rows), jnp.float32),
            pltpu.VMEM((per_step, keys, rows), jnp.bfloat16),
            pltpu.VMEM((kv_heads * groups, tokens), jnp.float32),
        ],
        compiler_params=pltpu.CompilerParams(vmem_limit_bytes=40 * 1024 * 1024),
        cost_estimate=pl.CostEstimate(
            flops=16 * tokens * width * keys,
            bytes_accessed=16 * tokens * width,
            transcendentals=tokens * width // HEAD_WIDTH * keys,
        ),
    )(*operands, *prepared, *(() if first else state))


def local(queries, keys, values, key_scale, value_scale, span_order, block_keep):
    tokens = queries.shape[0]
    kv_heads = keys.shape[1] // HEAD_WIDTH
    sizes = ctx_size, head_size = lax.axis_size("ctx"), lax.axis_size("head")
    size = ctx_size // 2 * head_size
    batch = 2 * SPAN // tokens

    def device(place, core):
        row, column = place // head_size, place % head_size
        return (2 * row + core) * head_size + (column if row % 2 == 0 else head_size - 1 - column)

    def around(block, distance):
        route = [
            (device(p, core), device((p + distance) % size, core))
            for p in range(size)
            for core in range(2)
        ]
        return lax.ppermute(block, ("ctx", "head"), route)

    def to_other_core(piece):
        return [lax.ppermute(block, "ctx", [(i, i ^ 1) for i in range(ctx_size)]) for block in piece]

    def swap_heads(block, flip):
        return lax.ppermute(block, "head", [(i, i ^ flip) for i in range(head_size)])

    sources = [(0, 0)]
    for step in range(1, size // 2 + 2):
        if step < size // 2:
            sources += [(step, 0), (-step, 0)]
        elif step == size // 2:
            sources += [(step - 1, 1), (1 - step, 1), (step, 0)]
        if step == 1:
            sources += [(0, 1)]
        elif step < size // 2:
            sources += [(step - 1, 1), (1 - step, 1)]
        elif step > size // 2:
            sources += [(step - 1, 1)]

    block = lax.optimization_barrier(jnp.concatenate([keys, values], axis=0))
    scale = jnp.concatenate([jnp.transpose(key_scale), jnp.transpose(value_scale)], axis=0)
    scales, pieces, done = [scale[None]], [[block]], 0
    fresh, forward, backward = [[block]], block, block
    prepared, rows, state = None, None, None
    for step in range(1, size // 2 + 2):
        crossed = [to_other_core(piece) for piece in fresh]
        sent = []
        if step < size // 2:
            forward, backward = around(forward, 1), around(backward, -1)
            sent = [[forward], [backward]]
        elif step == size // 2:
            sent = [[around(forward[:tokens], 1), around(backward[tokens:], -1)]]
        held = sum(scale.shape[0] for scale in scales)
        complete = held == head_size
        if not complete:
            scales = scales + [swap_heads(jnp.concatenate(scales, axis=0), held)]
        if step == 1:
            prepared = prepare(queries, span_order, block_keep, sources, kv_heads, sizes)
        if complete:
            if rows is None:
                rows = scale_rows(scales, sources, tokens, sizes)
            ready = (len(pieces) - done) // batch * batch if step < size // 2 else 0
            now = pieces[done : done + ready]
            if step == size // 2:
                now = pieces[done:] + crossed
                ready = len(now)
            if ready:
                state = absorb((*prepared, *rows), now, done, state, False, tokens)
                done += ready
        if step == size // 2 - 1:
            crossed, sent, scales, prepared, rows, state = lax.optimization_barrier(
                (crossed, sent, scales, prepared, rows, state)
            )
        else:
            sent, crossed, scales, prepared, rows, state = lax.optimization_barrier(
                (sent, crossed, scales, prepared, rows, state)
            )
        fresh = sent
        if step < size // 2:
            forward, backward = fresh[0][0], fresh[1][0]
        pieces = pieces + (sent + crossed if step < size // 2 else crossed + sent)
    return tuple(absorb((*prepared, *rows), pieces[done:], done, state, True, tokens))


def solution(mesh):
    rows = P(("dp", "ctx", "head"), None)
    return jax.shard_map(
        local,
        mesh=mesh,
        in_specs=(rows, rows, rows, P("dp", "head"), P("dp", "head"), P(), P()),
        out_specs=(rows, rows),
        check_vma=False,
    )
```

```python
import functools
import math

import jax
import jax.numpy as jnp
from jax import lax
from jax.experimental import pallas as pl
from jax.experimental.pallas import tpu as pltpu
from jax.sharding import PartitionSpec as P

HEAD_WIDTH = 128
SPAN = 128
LOG2E = 1.4426950408889634
MASKED = -1e30


def source_start(distance, flip, tokens, ctx_size, head_size):
    ctx, head = lax.axis_index("ctx"), lax.axis_index("head")
    size = ctx_size // 2 * head_size
    row = ctx // 2
    place = row * head_size + jnp.where(row % 2 == 0, head, head_size - 1 - head)
    place = lax.rem(place - distance + size, size)
    row, column = place // head_size, place % head_size
    column = jnp.where(row % 2 == 0, column, head_size - 1 - column)
    return ((2 * row + (ctx % 2) ^ flip) * head_size + column) * tokens


def prepare_kernel(order_ref, keep_ref, q_ref, qa_ref, hot_ref, mask_ref, *, groups, per_step, sources, ctx_size, head_size):
    step = pl.program_id(0)
    tokens = q_ref.shape[0]
    row = lax.broadcasted_iota(jnp.int32, (tokens, SPAN), 0)
    lane = lax.broadcasted_iota(jnp.int32, (tokens, SPAN), 1)

    @pl.when(step == 0)
    def _():
        own_start = source_start(0, 0, tokens, ctx_size, head_size)
        own = own_start // SPAN
        for i, source in enumerate(sources):
            start = source_start(*source, tokens, ctx_size, head_size)
            span = start // SPAN
            seen = (order_ref[span] < order_ref[own]) & (keep_ref[own, span] > 0)
            whole = jnp.where(seen, 0.0, MASKED)
            causal = jnp.where(row + (start - own_start) <= lane, 0.0, MASKED)
            mask = jnp.where(own == span, causal, whole)
            mask_ref[i * tokens : (i + 1) * tokens, :] = mask.astype(jnp.bfloat16)
        row_all = lax.broadcasted_iota(jnp.int32, hot_ref.shape, 0)
        lane_all = lax.broadcasted_iota(jnp.int32, hot_ref.shape, 1)
        hot = jnp.where(row_all == lane_all % tokens, 1.0, 0.0)
        hot_ref[...] = hot.astype(jnp.bfloat16)

    for u in range(per_step):
        heads = [
            q_ref[:, (u * groups + h) * HEAD_WIDTH : (u * groups + h + 1) * HEAD_WIDTH]
            for h in range(groups)
        ]
        qa_ref[u] = jnp.transpose(jnp.concatenate(heads, axis=0))


def prepare(queries, span_order, block_keep, sources, kv_heads, sizes):
    tokens, width = queries.shape
    groups = width // HEAD_WIDTH // kv_heads
    per_step = 2 if kv_heads % 2 == 0 else 1
    rows = groups * tokens
    smem = pl.BlockSpec(memory_space=pltpu.SMEM)
    return pl.pallas_call(
        functools.partial(
            prepare_kernel,
            groups=groups,
            per_step=per_step,
            sources=sources,
            ctx_size=sizes[0],
            head_size=sizes[1],
        ),
        grid=(kv_heads // per_step,),
        in_specs=[smem, smem, pl.BlockSpec((tokens, per_step * groups * HEAD_WIDTH), lambda s: (0, s))],
        out_specs=[
            pl.BlockSpec((per_step, HEAD_WIDTH, rows), lambda s: (s, 0, 0)),
            pl.BlockSpec((SPAN, rows), lambda s: (0, 0)),
            pl.BlockSpec((tokens * len(sources), SPAN), lambda s: (0, 0)),
        ],
        out_shape=[
            jax.ShapeDtypeStruct((kv_heads, HEAD_WIDTH, rows), jnp.bfloat16),
            jax.ShapeDtypeStruct((SPAN, rows), jnp.bfloat16),
            jax.ShapeDtypeStruct((tokens * len(sources), SPAN), jnp.bfloat16),
        ],
        compiler_params=pltpu.CompilerParams(vmem_limit_bytes=32 * 1024 * 1024),
        cost_estimate=pl.CostEstimate(
            flops=8 * tokens * width, bytes_accessed=16 * tokens * width, transcendentals=0
        ),
    )(span_order, block_keep, queries)


def scale_rows_kernel(*refs, owners, tokens, kv_local, sources, ctx_size, head_size):
    scale_in = refs[: len(owners)]
    _, key_scale_ref, value_scale_ref, scale_ref, scale_sem = refs[len(owners) :]
    inverse_root = 1.0 / math.sqrt(HEAD_WIDTH)
    head = lax.axis_index("head")
    copies, flip = [], 0
    for ref, count in zip(scale_in, owners):
        for i in range(count):
            copies.append(
                pltpu.make_async_copy(ref.at[i], scale_ref.at[head ^ flip], scale_sem.at[flip])
            )
            flip += 1
    for copy in copies:
        copy.start()
    spans = [
        source_start(*source, tokens, ctx_size, head_size) // SPAN for source in sources
    ]
    for copy in copies:
        copy.wait()
    lane = lax.broadcasted_iota(jnp.int32, (1, SPAN), 1)
    for g in range(head_size * kv_local):
        owner, member = g // kv_local, g % kv_local
        for i, span in enumerate(spans):
            factor = scale_ref[owner, member, span] * (inverse_root * LOG2E)
            key_scale_ref[g, i : i + 1, :] = jnp.full((1, SPAN), factor, jnp.float32)
        per_tile = SPAN // tokens
        for tile in range(len(sources) // per_tile):
            row = None
            for i in range(per_tile):
                factor = scale_ref[owner, kv_local + member, spans[tile * per_tile + i]]
                if row is None:
                    row = jnp.full((1, SPAN), factor, jnp.float32)
                else:
                    row = jnp.where(lane >= i * tokens, factor, row)
            value_scale_ref[g, :, tile * SPAN : (tile + 1) * SPAN] = row


def scale_rows(scales, gate, sources, tokens, sizes):
    kv_local = scales[0].shape[1] // 2
    kv_heads = sizes[1] * kv_local
    return pl.pallas_call(
        functools.partial(
            scale_rows_kernel,
            owners=[scale.shape[0] for scale in scales],
            tokens=tokens,
            kv_local=kv_local,
            sources=sources,
            ctx_size=sizes[0],
            head_size=sizes[1],
        ),
        in_specs=[pl.BlockSpec(memory_space=pl.ANY)] * (len(scales) + 1),
        out_specs=[pl.BlockSpec(memory_space=pltpu.VMEM)] * 2,
        out_shape=[
            jax.ShapeDtypeStruct((kv_heads, len(sources), SPAN), jnp.float32),
            jax.ShapeDtypeStruct((kv_heads, 1, len(sources) * tokens), jnp.float32),
        ],
        scratch_shapes=[
            pltpu.SMEM((sizes[1],) + scales[0].shape[1:], jnp.float32),
            pltpu.SemaphoreType.DMA((sizes[1],)),
        ],
        compiler_params=pltpu.CompilerParams(vmem_limit_bytes=32 * 1024 * 1024),
        cost_estimate=pl.CostEstimate(
            flops=10**8, bytes_accessed=10**6, transcendentals=0
        ),
    )(*scales, gate)


def absorb_kernel(*refs, groups, tokens, per_step, begin, count, first, last):
    refs = list(refs)
    pieces = [(refs.pop(0), refs.pop(0)) for _ in range(count)]
    qa_ref, hot_ref, mask_ref, key_scale_ref, value_scale_ref = [refs.pop(0) for _ in range(5)]
    mixed_in, stats_in = (None, None) if first else (refs.pop(0), refs.pop(0))
    result_ref, stats_ref, x_ref, p_ref, check_ref = refs
    step = pl.program_id(0)
    inverse_root = 1.0 / math.sqrt(HEAD_WIDTH)
    for u in range(per_step):
        g = step * per_step + u
        cols = pl.ds(pl.multiple_of(g * HEAD_WIDTH, HEAD_WIDTH), HEAD_WIDTH)
        k = jnp.concatenate([key_ref[:, cols] for key_ref, _ in pieces], axis=0)
        k = jnp.concatenate([k, mask_ref[begin * tokens : (begin + count) * tokens, :]], axis=1)
        x_ref[u] = jnp.dot(
            k,
            jnp.concatenate([qa_ref[u], hot_ref[...]], axis=0),
            preferred_element_type=jnp.float32,
        )
    rows = []
    for u in range(per_step):
        g = step * per_step + u
        cols = pl.ds(pl.multiple_of(g * HEAD_WIDTH, HEAD_WIDTH), HEAD_WIDTH)
        factors = [key_scale_ref[u, begin + i : begin + i + 1, :] for i in range(count)]
        tops, totals, fades = [], [], []
        rows.append((tops, totals, fades))
        for tile in range(groups * tokens // SPAN):
            lanes = slice(tile * SPAN, (tile + 1) * SPAN)
            top = None
            for i, factor in enumerate(factors):
                x = x_ref[u, i * tokens : (i + 1) * tokens, lanes]
                highest = jnp.max(x.reshape(tokens // 8, 8, SPAN), axis=0) * factor
                top = highest if top is None else jnp.maximum(top, highest)
            top = jnp.max(top, axis=0, keepdims=True)
            if not first:
                before = stats_in[u, 0:1, lanes]
                top = jnp.maximum(top, before)
                fades.append(jnp.exp2(before - top))
            total = None
            for i, factor in enumerate(factors):
                keys = slice(i * tokens, (i + 1) * tokens)
                weight = jnp.exp2(x_ref[u, keys, lanes] * factor - top)
                p_ref[u, keys, lanes] = weight.astype(jnp.bfloat16)
                part = jnp.sum(weight.reshape(tokens // 8, 8, SPAN), axis=0)
                total = part if total is None else total + part
            total = jnp.sum(total, axis=0, keepdims=True)
            if not first:
                total = total + fades[tile] * stats_in[u, 1:2, lanes]
            tops.append(top)
            totals.append(total)
    for u in range(per_step):
        g = step * per_step + u
        cols = pl.ds(pl.multiple_of(g * HEAD_WIDTH, HEAD_WIDTH), HEAD_WIDTH)
        tops, totals, fades = rows[u]
        v = jnp.concatenate([value_ref[:, cols] for _, value_ref in pieces], axis=0)
        v = jnp.transpose(v).astype(jnp.float32)
        v = v * value_scale_ref[u, :, begin * tokens : (begin + count) * tokens]
        high = v.astype(jnp.bfloat16)
        low = (v - high.astype(jnp.float32)).astype(jnp.bfloat16)
        v = jnp.concatenate([high, low], axis=0)
        both = jnp.dot(v, p_ref[u], preferred_element_type=jnp.float32)
        for tile in range(groups * tokens // SPAN):
            lanes = slice(tile * SPAN, (tile + 1) * SPAN)
            mixed = both[:HEAD_WIDTH, lanes] + both[HEAD_WIDTH:, lanes]
            if not first:
                mixed = mixed + fades[tile] * mixed_in[u, :, lanes]
            if not last:
                result_ref[u, :, lanes] = mixed
                stats_ref[u, 0:1, lanes] = tops[tile]
                stats_ref[u, 1:2, lanes] = totals[tile]
                continue
            mixed = mixed * (1.0 / totals[tile])
            check = jnp.sum(mixed, axis=0, keepdims=True) * inverse_root
            mixed = jnp.transpose(mixed).astype(result_ref.dtype)
            for j in range(SPAN // tokens):
                h = tile * (SPAN // tokens) + j
                at = (u * groups + h) * HEAD_WIDTH
                result_ref[:, at : at + HEAD_WIDTH] = mixed[j * tokens : (j + 1) * tokens]
                check_ref[pl.ds(g * groups + h, 1), :] = check[:, j * tokens : (j + 1) * tokens]
    if last:

        @pl.when(step == pl.num_programs(0) - 1)
        def _():
            stats_ref[...] = jnp.transpose(check_ref[...])


def absorb(prepared, pieces, begin, state, last, tokens):
    kv_heads, _, rows = prepared[0].shape
    groups = rows // tokens
    count = len(pieces)
    per_step = 4 if kv_heads % 4 == 0 else 1
    keys = tokens * count
    width = kv_heads * groups * HEAD_WIDTH
    first = state is None
    mixed = pl.BlockSpec((per_step, HEAD_WIDTH, rows), lambda s: (s, 0, 0))
    stats = pl.BlockSpec((per_step, 2, rows), lambda s: (s, 0, 0))
    in_specs, operands = [], []
    for piece in pieces:
        joined = len(piece) == 1
        half = (tokens, piece[0].shape[1])
        in_specs.append(pl.BlockSpec(half, lambda s: (0, 0)))
        in_specs.append(pl.BlockSpec(half, lambda s: (1, 0)) if joined else in_specs[-1])
        operands += [piece[0], piece[-1]]
    in_specs += [
        pl.BlockSpec((per_step,) + prepared[0].shape[1:], lambda s: (s, 0, 0)),
        pl.BlockSpec(prepared[1].shape, lambda s: (0, 0)),
        pl.BlockSpec(prepared[2].shape, lambda s: (0, 0)),
        pl.BlockSpec((per_step,) + prepared[3].shape[1:], lambda s: (s, 0, 0)),
        pl.BlockSpec((per_step,) + prepared[4].shape[1:], lambda s: (s, 0, 0)),
    ]
    in_specs += [] if first else [mixed, stats]
    if last:
        out_specs = [
            pl.BlockSpec((tokens, per_step * groups * HEAD_WIDTH), lambda s: (0, s)),
            pl.BlockSpec((tokens, kv_heads * groups), lambda s: (0, 0)),
        ]
        out_shape = [
            jax.ShapeDtypeStruct((tokens, width), jnp.bfloat16),
            jax.ShapeDtypeStruct((tokens, kv_heads * groups), jnp.float32),
        ]
    else:
        out_specs = [mixed, stats]
        out_shape = [
            jax.ShapeDtypeStruct((kv_heads, HEAD_WIDTH, rows), jnp.float32),
            jax.ShapeDtypeStruct((kv_heads, 2, rows), jnp.float32),
        ]
    return pl.pallas_call(
        functools.partial(
            absorb_kernel,
            groups=groups,
            tokens=tokens,
            per_step=per_step,
            begin=begin,
            count=count,
            first=first,
            last=last,
        ),
        grid=(kv_heads // per_step,),
        in_specs=in_specs,
        out_specs=out_specs,
        out_shape=out_shape,
        scratch_shapes=[
            pltpu.VMEM((per_step, keys, rows), jnp.float32),
            pltpu.VMEM((per_step, keys, rows), jnp.bfloat16),
            pltpu.VMEM((kv_heads * groups, tokens), jnp.float32),
        ],
        compiler_params=pltpu.CompilerParams(vmem_limit_bytes=40 * 1024 * 1024),
        cost_estimate=pl.CostEstimate(
            flops=16 * tokens * width * keys,
            bytes_accessed=16 * tokens * width,
            transcendentals=tokens * width // HEAD_WIDTH * keys,
        ),
    )(*operands, *prepared, *(() if first else state))


def local(queries, keys, values, key_scale, value_scale, span_order, block_keep):
    tokens = queries.shape[0]
    kv_heads = keys.shape[1] // HEAD_WIDTH
    sizes = ctx_size, head_size = lax.axis_size("ctx"), lax.axis_size("head")
    size = ctx_size // 2 * head_size
    batch = 2 * SPAN // tokens

    def device(place, core):
        row, column = place // head_size, place % head_size
        return (2 * row + core) * head_size + (column if row % 2 == 0 else head_size - 1 - column)

    def around(block, distance):
        route = [
            (device(p, core), device((p + distance) % size, core))
            for p in range(size)
            for core in range(2)
        ]
        return lax.ppermute(block, ("ctx", "head"), route)

    def to_other_core(piece):
        return [lax.ppermute(block, "ctx", [(i, i ^ 1) for i in range(ctx_size)]) for block in piece]

    def swap_heads(block, flip):
        return lax.ppermute(block, "head", [(i, i ^ flip) for i in range(head_size)])

    sources = [(0, 0)]
    for step in range(1, size // 2 + 2):
        if step < size // 2:
            sources += [(step, 0), (-step, 0)]
        elif step == size // 2:
            sources += [(step - 1, 1), (1 - step, 1), (step, 0)]
        if step == 1:
            sources += [(0, 1)]
        elif step < size // 2:
            sources += [(step - 1, 1), (1 - step, 1)]
        elif step > size // 2:
            sources += [(step - 1, 1)]

    block = lax.optimization_barrier(jnp.concatenate([keys, values], axis=0))
    scale = jnp.concatenate([jnp.transpose(key_scale), jnp.transpose(value_scale)], axis=0)
    scales, pieces, done = [scale[None]], [[block]], 0
    fresh, forward, backward = [[block]], block, block
    prepared, rows, state, gate = None, None, None, span_order
    for step in range(1, size // 2 + 2):
        crossed = [to_other_core(piece) for piece in fresh]
        sent = []
        if step < size // 2:
            forward, backward = around(forward, 1), around(backward, -1)
            sent = [[forward], [backward]]
        elif step == size // 2:
            sent = [[around(halves[0], 1), around(halves[1], -1)]]
        held = sum(scale.shape[0] for scale in scales)
        complete = held == head_size
        if not complete:
            scales = scales + [swap_heads(jnp.concatenate(scales, axis=0), held)]
        if step == 1:
            prepared = prepare(queries, span_order, block_keep, sources, kv_heads, sizes)
        if complete:
            if rows is None:
                rows = scale_rows(scales, gate, sources, tokens, sizes)
            ready = (len(pieces) - done) // batch * batch if step < size // 2 else 0
            now = pieces[done : done + ready]
            if step == size // 2:
                now = pieces[done:] + crossed
                ready = len(now)
            if ready:
                state = absorb((*prepared, *rows), now, done, state, False, tokens)
                done += ready
        if step == size // 2 - 1:
            halves = [sent[0][0][:tokens], sent[1][0][tokens:]]
            crossed, halves, sent, prepared, rows, state = lax.optimization_barrier(
                (crossed, halves, sent, prepared, rows, state)
            )
        elif sum(scale.shape[0] for scale in scales) < head_size:
            crossed, sent, scales, prepared, rows, state = lax.optimization_barrier(
                (crossed, sent, scales, prepared, rows, state)
            )
        else:
            crossed, sent, gate, prepared, rows, state = lax.optimization_barrier(
                (crossed, sent, gate, prepared, rows, state)
            )
        fresh = sent
        if step < size // 2:
            forward, backward = fresh[0][0], fresh[1][0]
        pieces = pieces + (sent + crossed if step < size // 2 else crossed + sent)
    return tuple(absorb((*prepared, *rows), pieces[done:], done, state, True, tokens))


def solution(mesh):
    rows = P(("dp", "ctx", "head"), None)
    return jax.shard_map(
        local,
        mesh=mesh,
        in_specs=(rows, rows, rows, P("dp", "head"), P("dp", "head"), P(), P()),
        out_specs=(rows, rows),
        check_vma=False,
    )
```

```python
import functools
import math

import jax
import jax.numpy as jnp
from jax import lax
from jax.experimental import pallas as pl
from jax.experimental.pallas import tpu as pltpu
from jax.sharding import PartitionSpec as P

HEAD_WIDTH = 128
SPAN = 128
LOG2E = 1.4426950408889634
MASKED = -1e30


def source_start(distance, flip, tokens, ctx_size, head_size):
    ctx, head = lax.axis_index("ctx"), lax.axis_index("head")
    size = ctx_size // 2 * head_size
    row = ctx // 2
    place = row * head_size + jnp.where(row % 2 == 0, head, head_size - 1 - head)
    place = lax.rem(place - distance + size, size)
    row, column = place // head_size, place % head_size
    column = jnp.where(row % 2 == 0, column, head_size - 1 - column)
    return ((2 * row + (ctx % 2) ^ flip) * head_size + column) * tokens


def prepare_kernel(order_ref, keep_ref, q_ref, qa_ref, hot_ref, mask_ref, *, groups, per_step, sources, ctx_size, head_size):
    step = pl.program_id(0)
    tokens = q_ref.shape[0]
    row = lax.broadcasted_iota(jnp.int32, (tokens, SPAN), 0)
    lane = lax.broadcasted_iota(jnp.int32, (tokens, SPAN), 1)

    @pl.when(step == 0)
    def _():
        own_start = source_start(0, 0, tokens, ctx_size, head_size)
        own = own_start // SPAN
        for i, source in enumerate(sources):
            start = source_start(*source, tokens, ctx_size, head_size)
            span = start // SPAN
            seen = (order_ref[span] < order_ref[own]) & (keep_ref[own, span] > 0)
            whole = jnp.where(seen, 0.0, MASKED)
            causal = jnp.where(row + (start - own_start) <= lane, 0.0, MASKED)
            mask = jnp.where(own == span, causal, whole)
            mask_ref[i * tokens : (i + 1) * tokens, :] = mask.astype(jnp.bfloat16)
        row_all = lax.broadcasted_iota(jnp.int32, hot_ref.shape, 0)
        lane_all = lax.broadcasted_iota(jnp.int32, hot_ref.shape, 1)
        hot = jnp.where(row_all == lane_all % tokens, 1.0, 0.0)
        hot_ref[...] = hot.astype(jnp.bfloat16)

    for u in range(per_step):
        heads = [
            q_ref[:, (u * groups + h) * HEAD_WIDTH : (u * groups + h + 1) * HEAD_WIDTH]
            for h in range(groups)
        ]
        qa_ref[u] = jnp.transpose(jnp.concatenate(heads, axis=0))


def prepare(queries, span_order, block_keep, sources, kv_heads, sizes):
    tokens, width = queries.shape
    groups = width // HEAD_WIDTH // kv_heads
    per_step = 2 if kv_heads % 2 == 0 else 1
    rows = groups * tokens
    smem = pl.BlockSpec(memory_space=pltpu.SMEM)
    return pl.pallas_call(
        functools.partial(
            prepare_kernel,
            groups=groups,
            per_step=per_step,
            sources=sources,
            ctx_size=sizes[0],
            head_size=sizes[1],
        ),
        grid=(kv_heads // per_step,),
        in_specs=[smem, smem, pl.BlockSpec((tokens, per_step * groups * HEAD_WIDTH), lambda s: (0, s))],
        out_specs=[
            pl.BlockSpec((per_step, HEAD_WIDTH, rows), lambda s: (s, 0, 0)),
            pl.BlockSpec((SPAN, rows), lambda s: (0, 0)),
            pl.BlockSpec((tokens * len(sources), SPAN), lambda s: (0, 0)),
        ],
        out_shape=[
            jax.ShapeDtypeStruct((kv_heads, HEAD_WIDTH, rows), jnp.bfloat16),
            jax.ShapeDtypeStruct((SPAN, rows), jnp.bfloat16),
            jax.ShapeDtypeStruct((tokens * len(sources), SPAN), jnp.bfloat16),
        ],
        compiler_params=pltpu.CompilerParams(vmem_limit_bytes=32 * 1024 * 1024),
        cost_estimate=pl.CostEstimate(
            flops=8 * tokens * width, bytes_accessed=16 * tokens * width, transcendentals=0
        ),
    )(span_order, block_keep, queries)


def scale_rows_kernel(*refs, owners, tokens, kv_local, sources, ctx_size, head_size):
    scale_in = refs[: len(owners)]
    _, key_scale_ref, value_scale_ref, scale_ref, scale_sem = refs[len(owners) :]
    inverse_root = 1.0 / math.sqrt(HEAD_WIDTH)
    head = lax.axis_index("head")
    copies, flip = [], 0
    for ref, count in zip(scale_in, owners):
        for i in range(count):
            copies.append(
                pltpu.make_async_copy(ref.at[i], scale_ref.at[head ^ flip], scale_sem.at[flip])
            )
            flip += 1
    for copy in copies:
        copy.start()
    spans = [
        source_start(*source, tokens, ctx_size, head_size) // SPAN for source in sources
    ]
    for copy in copies:
        copy.wait()
    lane = lax.broadcasted_iota(jnp.int32, (1, SPAN), 1)
    for g in range(head_size * kv_local):
        owner, member = g // kv_local, g % kv_local
        for i, span in enumerate(spans):
            factor = scale_ref[owner, member, span] * (inverse_root * LOG2E)
            key_scale_ref[g, i : i + 1, :] = jnp.full((1, SPAN), factor, jnp.float32)
        per_tile = SPAN // tokens
        for tile in range(len(sources) // per_tile):
            row = None
            for i in range(per_tile):
                factor = scale_ref[owner, kv_local + member, spans[tile * per_tile + i]]
                if row is None:
                    row = jnp.full((1, SPAN), factor, jnp.float32)
                else:
                    row = jnp.where(lane >= i * tokens, factor, row)
            value_scale_ref[g, :, tile * SPAN : (tile + 1) * SPAN] = row


def scale_rows(scales, gate, sources, tokens, sizes):
    kv_local = scales[0].shape[1] // 2
    kv_heads = sizes[1] * kv_local
    return pl.pallas_call(
        functools.partial(
            scale_rows_kernel,
            owners=[scale.shape[0] for scale in scales],
            tokens=tokens,
            kv_local=kv_local,
            sources=sources,
            ctx_size=sizes[0],
            head_size=sizes[1],
        ),
        in_specs=[pl.BlockSpec(memory_space=pl.ANY)] * (len(scales) + 1),
        out_specs=[pl.BlockSpec(memory_space=pltpu.VMEM)] * 2,
        out_shape=[
            jax.ShapeDtypeStruct((kv_heads, len(sources), SPAN), jnp.float32),
            jax.ShapeDtypeStruct((kv_heads, 1, len(sources) * tokens), jnp.float32),
        ],
        scratch_shapes=[
            pltpu.SMEM((sizes[1],) + scales[0].shape[1:], jnp.float32),
            pltpu.SemaphoreType.DMA((sizes[1],)),
        ],
        compiler_params=pltpu.CompilerParams(vmem_limit_bytes=32 * 1024 * 1024),
        cost_estimate=pl.CostEstimate(
            flops=10**8, bytes_accessed=10**6, transcendentals=0
        ),
    )(*scales, gate)


def absorb_kernel(*refs, groups, tokens, per_step, begin, count, first, last):
    refs = list(refs)
    pieces = [(refs.pop(0), refs.pop(0)) for _ in range(count)]
    qa_ref, hot_ref, mask_ref, key_scale_ref, value_scale_ref = [refs.pop(0) for _ in range(5)]
    mixed_in, stats_in = (None, None) if first else (refs.pop(0), refs.pop(0))
    result_ref, stats_ref, x_ref, p_ref, check_ref = refs
    step = pl.program_id(0)
    inverse_root = 1.0 / math.sqrt(HEAD_WIDTH)
    for u in range(per_step):
        g = step * per_step + u
        cols = pl.ds(pl.multiple_of(g * HEAD_WIDTH, HEAD_WIDTH), HEAD_WIDTH)
        k = jnp.concatenate([key_ref[:, cols] for key_ref, _ in pieces], axis=0)
        k = jnp.concatenate([k, mask_ref[begin * tokens : (begin + count) * tokens, :]], axis=1)
        x_ref[u] = jnp.dot(
            k,
            jnp.concatenate([qa_ref[u], hot_ref[...]], axis=0),
            preferred_element_type=jnp.float32,
        )
    rows = []
    for u in range(per_step):
        g = step * per_step + u
        cols = pl.ds(pl.multiple_of(g * HEAD_WIDTH, HEAD_WIDTH), HEAD_WIDTH)
        factors = [key_scale_ref[u, begin + i : begin + i + 1, :] for i in range(count)]
        tops, totals, fades = [], [], []
        rows.append((tops, totals, fades))
        for tile in range(groups * tokens // SPAN):
            lanes = slice(tile * SPAN, (tile + 1) * SPAN)
            top = None
            for i, factor in enumerate(factors):
                x = x_ref[u, i * tokens : (i + 1) * tokens, lanes]
                highest = jnp.max(x.reshape(tokens // 8, 8, SPAN), axis=0) * factor
                top = highest if top is None else jnp.maximum(top, highest)
            top = jnp.max(top, axis=0, keepdims=True)
            if not first:
                before = stats_in[u, 0:1, lanes]
                top = jnp.maximum(top, before)
                fades.append(jnp.exp2(before - top))
            total = None
            for i, factor in enumerate(factors):
                keys = slice(i * tokens, (i + 1) * tokens)
                weight = jnp.exp2(x_ref[u, keys, lanes] * factor - top)
                p_ref[u, keys, lanes] = weight.astype(jnp.bfloat16)
                part = jnp.sum(weight.reshape(tokens // 8, 8, SPAN), axis=0)
                total = part if total is None else total + part
            total = jnp.sum(total, axis=0, keepdims=True)
            if not first:
                total = total + fades[tile] * stats_in[u, 1:2, lanes]
            tops.append(top)
            totals.append(total)
    for u in range(per_step):
        g = step * per_step + u
        cols = pl.ds(pl.multiple_of(g * HEAD_WIDTH, HEAD_WIDTH), HEAD_WIDTH)
        tops, totals, fades = rows[u]
        v = jnp.concatenate([value_ref[:, cols] for _, value_ref in pieces], axis=0)
        v = jnp.transpose(v).astype(jnp.float32)
        v = v * value_scale_ref[u, :, begin * tokens : (begin + count) * tokens]
        high = v.astype(jnp.bfloat16)
        low = (v - high.astype(jnp.float32)).astype(jnp.bfloat16)
        v = jnp.concatenate([high, low], axis=0)
        both = jnp.dot(v, p_ref[u], preferred_element_type=jnp.float32)
        for tile in range(groups * tokens // SPAN):
            lanes = slice(tile * SPAN, (tile + 1) * SPAN)
            mixed = both[:HEAD_WIDTH, lanes] + both[HEAD_WIDTH:, lanes]
            if not first:
                mixed = mixed + fades[tile] * mixed_in[u, :, lanes]
            if not last:
                result_ref[u, :, lanes] = mixed
                stats_ref[u, 0:1, lanes] = tops[tile]
                stats_ref[u, 1:2, lanes] = totals[tile]
                continue
            mixed = mixed * (1.0 / totals[tile])
            check = jnp.sum(mixed, axis=0, keepdims=True) * inverse_root
            mixed = jnp.transpose(mixed).astype(result_ref.dtype)
            for j in range(SPAN // tokens):
                h = tile * (SPAN // tokens) + j
                at = (u * groups + h) * HEAD_WIDTH
                result_ref[:, at : at + HEAD_WIDTH] = mixed[j * tokens : (j + 1) * tokens]
                check_ref[pl.ds(g * groups + h, 1), :] = check[:, j * tokens : (j + 1) * tokens]
    if last:

        @pl.when(step == pl.num_programs(0) - 1)
        def _():
            stats_ref[...] = jnp.transpose(check_ref[...])


def absorb(prepared, pieces, begin, state, last, tokens):
    kv_heads, _, rows = prepared[0].shape
    groups = rows // tokens
    count = len(pieces)
    per_step = 4 if kv_heads % 4 == 0 else 1
    keys = tokens * count
    width = kv_heads * groups * HEAD_WIDTH
    first = state is None
    mixed = pl.BlockSpec((per_step, HEAD_WIDTH, rows), lambda s: (s, 0, 0))
    stats = pl.BlockSpec((per_step, 2, rows), lambda s: (s, 0, 0))
    in_specs, operands = [], []
    for piece in pieces:
        joined = len(piece) == 1
        half = (tokens, piece[0].shape[1])
        in_specs.append(pl.BlockSpec(half, lambda s: (0, 0)))
        in_specs.append(pl.BlockSpec(half, lambda s: (1, 0)) if joined else in_specs[-1])
        operands += [piece[0], piece[-1]]
    in_specs += [
        pl.BlockSpec((per_step,) + prepared[0].shape[1:], lambda s: (s, 0, 0)),
        pl.BlockSpec(prepared[1].shape, lambda s: (0, 0)),
        pl.BlockSpec(prepared[2].shape, lambda s: (0, 0)),
        pl.BlockSpec((per_step,) + prepared[3].shape[1:], lambda s: (s, 0, 0)),
        pl.BlockSpec((per_step,) + prepared[4].shape[1:], lambda s: (s, 0, 0)),
    ]
    in_specs += [] if first else [mixed, stats]
    if last:
        out_specs = [
            pl.BlockSpec((tokens, per_step * groups * HEAD_WIDTH), lambda s: (0, s)),
            pl.BlockSpec((tokens, kv_heads * groups), lambda s: (0, 0)),
        ]
        out_shape = [
            jax.ShapeDtypeStruct((tokens, width), jnp.bfloat16),
            jax.ShapeDtypeStruct((tokens, kv_heads * groups), jnp.float32),
        ]
    else:
        out_specs = [mixed, stats]
        out_shape = [
            jax.ShapeDtypeStruct((kv_heads, HEAD_WIDTH, rows), jnp.float32),
            jax.ShapeDtypeStruct((kv_heads, 2, rows), jnp.float32),
        ]
    return pl.pallas_call(
        functools.partial(
            absorb_kernel,
            groups=groups,
            tokens=tokens,
            per_step=per_step,
            begin=begin,
            count=count,
            first=first,
            last=last,
        ),
        grid=(kv_heads // per_step,),
        in_specs=in_specs,
        out_specs=out_specs,
        out_shape=out_shape,
        scratch_shapes=[
            pltpu.VMEM((per_step, keys, rows), jnp.float32),
            pltpu.VMEM((per_step, keys, rows), jnp.bfloat16),
            pltpu.VMEM((kv_heads * groups, tokens), jnp.float32),
        ],
        compiler_params=pltpu.CompilerParams(vmem_limit_bytes=40 * 1024 * 1024),
        cost_estimate=pl.CostEstimate(
            flops=16 * tokens * width * keys,
            bytes_accessed=16 * tokens * width,
            transcendentals=tokens * width // HEAD_WIDTH * keys,
        ),
    )(*operands, *prepared, *(() if first else state))


def local(queries, keys, values, key_scale, value_scale, span_order, block_keep):
    tokens = queries.shape[0]
    kv_heads = keys.shape[1] // HEAD_WIDTH
    sizes = ctx_size, head_size = lax.axis_size("ctx"), lax.axis_size("head")
    size = ctx_size // 2 * head_size
    batch = 2 * SPAN // tokens

    def device(place, core):
        row, column = place // head_size, place % head_size
        return (2 * row + core) * head_size + (column if row % 2 == 0 else head_size - 1 - column)

    def around(block, distance):
        route = [
            (device(p, core), device((p + distance) % size, core))
            for p in range(size)
            for core in range(2)
        ]
        return lax.ppermute(block, ("ctx", "head"), route)

    def to_other_core(piece):
        return [lax.ppermute(block, "ctx", [(i, i ^ 1) for i in range(ctx_size)]) for block in piece]

    def swap_heads(block, flip):
        return lax.ppermute(block, "head", [(i, i ^ flip) for i in range(head_size)])

    sources = [(0, 0)]
    for step in range(1, size // 2 + 2):
        if step < size // 2:
            sources += [(step, 0), (-step, 0)]
        elif step == size // 2:
            sources += [(step - 1, 1), (1 - step, 1), (step, 0)]
        if step == 1:
            sources += [(0, 1)]
        elif step < size // 2:
            sources += [(step - 1, 1), (1 - step, 1)]
        elif step > size // 2:
            sources += [(step - 1, 1)]

    block = lax.optimization_barrier(jnp.concatenate([keys, values], axis=0))
    scale = jnp.concatenate([jnp.transpose(key_scale), jnp.transpose(value_scale)], axis=0)
    scales, pieces, done = [scale[None]], [[block]], 0
    fresh, forward, backward = [[block]], block, block
    prepared, rows, state, gate = None, None, None, span_order
    for step in range(1, size // 2 + 2):
        crossed = [to_other_core(piece) for piece in fresh]
        sent = []
        if step < size // 2:
            forward, backward = around(forward, 1), around(backward, -1)
            sent = [[forward], [backward]]
        elif step == size // 2:
            sent = [[around(forward[:tokens], 1), around(backward[tokens:], -1)]]
        held = sum(scale.shape[0] for scale in scales)
        complete = held == head_size
        if not complete:
            scales = scales + [swap_heads(jnp.concatenate(scales, axis=0), held)]
        if step == 1:
            prepared = prepare(queries, span_order, block_keep, sources, kv_heads, sizes)
        if complete:
            if rows is None:
                rows = scale_rows(scales, gate, sources, tokens, sizes)
            ready = (len(pieces) - done) // batch * batch if step < size // 2 else 0
            now = pieces[done : done + ready]
            if step == size // 2:
                now = pieces[done:] + crossed
                ready = len(now)
            if ready:
                state = absorb((*prepared, *rows), now, done, state, False, tokens)
                done += ready
        if sum(scale.shape[0] for scale in scales) < head_size:
            sent, crossed, scales, prepared, rows, state = lax.optimization_barrier(
                (sent, crossed, scales, prepared, rows, state)
            )
        elif step == size // 2 - 1:
            crossed, sent, prepared, rows, state = lax.optimization_barrier(
                (crossed, sent, prepared, rows, state)
            )
        else:
            sent, crossed, gate, prepared, rows, state = lax.optimization_barrier(
                (sent, crossed, gate, prepared, rows, state)
            )
        fresh = sent
        if step < size // 2:
            forward, backward = fresh[0][0], fresh[1][0]
        pieces = pieces + (sent + crossed if step < size // 2 else crossed + sent)
    return tuple(absorb((*prepared, *rows), pieces[done:], done, state, True, tokens))


def solution(mesh):
    rows = P(("dp", "ctx", "head"), None)
    return jax.shard_map(
        local,
        mesh=mesh,
        in_specs=(rows, rows, rows, P("dp", "head"), P("dp", "head"), P(), P()),
        out_specs=(rows, rows),
        check_vma=False,
    )
```

```python
import functools
import math

import jax
import jax.numpy as jnp
from jax import lax
from jax.experimental import pallas as pl
from jax.experimental.pallas import tpu as pltpu
from jax.sharding import PartitionSpec as P

HEAD_WIDTH = 128
SPAN = 128
LOG2E = 1.4426950408889634
MASKED = -1e30


def source_start(distance, flip, tokens, ctx_size, head_size):
    ctx, head = lax.axis_index("ctx"), lax.axis_index("head")
    size = ctx_size // 2 * head_size
    row = ctx // 2
    place = row * head_size + jnp.where(row % 2 == 0, head, head_size - 1 - head)
    place = lax.rem(place - distance + size, size)
    row, column = place // head_size, place % head_size
    column = jnp.where(row % 2 == 0, column, head_size - 1 - column)
    return ((2 * row + (ctx % 2) ^ flip) * head_size + column) * tokens


def prepare_kernel(order_ref, keep_ref, q_ref, qa_ref, hot_ref, mask_ref, *, groups, per_step, sources, ctx_size, head_size):
    step = pl.program_id(0)
    tokens = q_ref.shape[0]
    row = lax.broadcasted_iota(jnp.int32, (tokens, SPAN), 0)
    lane = lax.broadcasted_iota(jnp.int32, (tokens, SPAN), 1)

    @pl.when(step == 0)
    def _():
        own_start = source_start(0, 0, tokens, ctx_size, head_size)
        own = own_start // SPAN
        for i, source in enumerate(sources):
            start = source_start(*source, tokens, ctx_size, head_size)
            span = start // SPAN
            seen = (order_ref[span] < order_ref[own]) & (keep_ref[own, span] > 0)
            whole = jnp.where(seen, 0.0, MASKED)
            causal = jnp.where(row + (start - own_start) <= lane, 0.0, MASKED)
            mask = jnp.where(own == span, causal, whole)
            mask_ref[i * tokens : (i + 1) * tokens, :] = mask.astype(jnp.bfloat16)
        row_all = lax.broadcasted_iota(jnp.int32, hot_ref.shape, 0)
        lane_all = lax.broadcasted_iota(jnp.int32, hot_ref.shape, 1)
        hot = jnp.where(row_all == lane_all % tokens, 1.0, 0.0)
        hot_ref[...] = hot.astype(jnp.bfloat16)

    for u in range(per_step):
        heads = [
            q_ref[:, (u * groups + h) * HEAD_WIDTH : (u * groups + h + 1) * HEAD_WIDTH]
            for h in range(groups)
        ]
        qa_ref[u] = jnp.transpose(jnp.concatenate(heads, axis=0))


def prepare(queries, span_order, block_keep, sources, kv_heads, sizes):
    tokens, width = queries.shape
    groups = width // HEAD_WIDTH // kv_heads
    per_step = 2 if kv_heads % 2 == 0 else 1
    rows = groups * tokens
    smem = pl.BlockSpec(memory_space=pltpu.SMEM)
    return pl.pallas_call(
        functools.partial(
            prepare_kernel,
            groups=groups,
            per_step=per_step,
            sources=sources,
            ctx_size=sizes[0],
            head_size=sizes[1],
        ),
        grid=(kv_heads // per_step,),
        in_specs=[smem, smem, pl.BlockSpec((tokens, per_step * groups * HEAD_WIDTH), lambda s: (0, s))],
        out_specs=[
            pl.BlockSpec((per_step, HEAD_WIDTH, rows), lambda s: (s, 0, 0)),
            pl.BlockSpec((SPAN, rows), lambda s: (0, 0)),
            pl.BlockSpec((tokens * len(sources), SPAN), lambda s: (0, 0)),
        ],
        out_shape=[
            jax.ShapeDtypeStruct((kv_heads, HEAD_WIDTH, rows), jnp.bfloat16),
            jax.ShapeDtypeStruct((SPAN, rows), jnp.bfloat16),
            jax.ShapeDtypeStruct((tokens * len(sources), SPAN), jnp.bfloat16),
        ],
        compiler_params=pltpu.CompilerParams(vmem_limit_bytes=32 * 1024 * 1024),
        cost_estimate=pl.CostEstimate(
            flops=8 * tokens * width, bytes_accessed=16 * tokens * width, transcendentals=0
        ),
    )(span_order, block_keep, queries)


def scale_rows_kernel(*refs, owners, tokens, kv_local, sources, ctx_size, head_size):
    scale_in = refs[: len(owners)]
    _, key_scale_ref, value_scale_ref, scale_ref, scale_sem = refs[len(owners) :]
    inverse_root = 1.0 / math.sqrt(HEAD_WIDTH)
    head = lax.axis_index("head")
    copies, flip = [], 0
    for ref, count in zip(scale_in, owners):
        for i in range(count):
            copies.append(
                pltpu.make_async_copy(ref.at[i], scale_ref.at[head ^ flip], scale_sem.at[flip])
            )
            flip += 1
    for copy in copies:
        copy.start()
    spans = [
        source_start(*source, tokens, ctx_size, head_size) // SPAN for source in sources
    ]
    for copy in copies:
        copy.wait()
    lane = lax.broadcasted_iota(jnp.int32, (1, SPAN), 1)
    for g in range(head_size * kv_local):
        owner, member = g // kv_local, g % kv_local
        for i, span in enumerate(spans):
            factor = scale_ref[owner, member, span] * (inverse_root * LOG2E)
            key_scale_ref[g, i : i + 1, :] = jnp.full((1, SPAN), factor, jnp.float32)
        per_tile = SPAN // tokens
        for tile in range(len(sources) // per_tile):
            row = None
            for i in range(per_tile):
                factor = scale_ref[owner, kv_local + member, spans[tile * per_tile + i]]
                if row is None:
                    row = jnp.full((1, SPAN), factor, jnp.float32)
                else:
                    row = jnp.where(lane >= i * tokens, factor, row)
            value_scale_ref[g, :, tile * SPAN : (tile + 1) * SPAN] = row


def scale_rows(scales, gate, sources, tokens, sizes):
    kv_local = scales[0].shape[1] // 2
    kv_heads = sizes[1] * kv_local
    return pl.pallas_call(
        functools.partial(
            scale_rows_kernel,
            owners=[scale.shape[0] for scale in scales],
            tokens=tokens,
            kv_local=kv_local,
            sources=sources,
            ctx_size=sizes[0],
            head_size=sizes[1],
        ),
        in_specs=[pl.BlockSpec(memory_space=pl.ANY)] * (len(scales) + 1),
        out_specs=[pl.BlockSpec(memory_space=pltpu.VMEM)] * 2,
        out_shape=[
            jax.ShapeDtypeStruct((kv_heads, len(sources), SPAN), jnp.float32),
            jax.ShapeDtypeStruct((kv_heads, 1, len(sources) * tokens), jnp.float32),
        ],
        scratch_shapes=[
            pltpu.SMEM((sizes[1],) + scales[0].shape[1:], jnp.float32),
            pltpu.SemaphoreType.DMA((sizes[1],)),
        ],
        compiler_params=pltpu.CompilerParams(vmem_limit_bytes=32 * 1024 * 1024),
        cost_estimate=pl.CostEstimate(
            flops=10**8, bytes_accessed=10**6, transcendentals=0
        ),
    )(*scales, gate)


def absorb_kernel(*refs, groups, tokens, per_step, begin, count, first, last):
    refs = list(refs)
    pieces = [(refs.pop(0), refs.pop(0)) for _ in range(count)]
    qa_ref, hot_ref, mask_ref, key_scale_ref, value_scale_ref = [refs.pop(0) for _ in range(5)]
    mixed_in, stats_in = (None, None) if first else (refs.pop(0), refs.pop(0))
    result_ref, stats_ref, x_ref, p_ref, check_ref = refs
    step = pl.program_id(0)
    inverse_root = 1.0 / math.sqrt(HEAD_WIDTH)
    for u in range(per_step):
        g = step * per_step + u
        cols = pl.ds(pl.multiple_of(g * HEAD_WIDTH, HEAD_WIDTH), HEAD_WIDTH)
        k = jnp.concatenate([key_ref[:, cols] for key_ref, _ in pieces], axis=0)
        k = jnp.concatenate([k, mask_ref[begin * tokens : (begin + count) * tokens, :]], axis=1)
        x_ref[u] = jnp.dot(
            k,
            jnp.concatenate([qa_ref[u], hot_ref[...]], axis=0),
            preferred_element_type=jnp.float32,
        )
    rows = []
    for u in range(per_step):
        g = step * per_step + u
        cols = pl.ds(pl.multiple_of(g * HEAD_WIDTH, HEAD_WIDTH), HEAD_WIDTH)
        factors = [key_scale_ref[u, begin + i : begin + i + 1, :] for i in range(count)]
        tops, totals, fades = [], [], []
        rows.append((tops, totals, fades))
        for tile in range(groups * tokens // SPAN):
            lanes = slice(tile * SPAN, (tile + 1) * SPAN)
            top = None
            for i, factor in enumerate(factors):
                x = x_ref[u, i * tokens : (i + 1) * tokens, lanes]
                highest = jnp.max(x.reshape(tokens // 8, 8, SPAN), axis=0) * factor
                top = highest if top is None else jnp.maximum(top, highest)
            top = jnp.max(top, axis=0, keepdims=True)
            if not first:
                before = stats_in[u, 0:1, lanes]
                top = jnp.maximum(top, before)
                fades.append(jnp.exp2(before - top))
            total = None
            for i, factor in enumerate(factors):
                keys = slice(i * tokens, (i + 1) * tokens)
                weight = jnp.exp2(x_ref[u, keys, lanes] * factor - top)
                p_ref[u, keys, lanes] = weight.astype(jnp.bfloat16)
                part = jnp.sum(weight.reshape(tokens // 8, 8, SPAN), axis=0)
                total = part if total is None else total + part
            total = jnp.sum(total, axis=0, keepdims=True)
            if not first:
                total = total + fades[tile] * stats_in[u, 1:2, lanes]
            tops.append(top)
            totals.append(total)
    for u in range(per_step):
        g = step * per_step + u
        cols = pl.ds(pl.multiple_of(g * HEAD_WIDTH, HEAD_WIDTH), HEAD_WIDTH)
        tops, totals, fades = rows[u]
        v = jnp.concatenate([value_ref[:, cols] for _, value_ref in pieces], axis=0)
        v = jnp.transpose(v).astype(jnp.float32)
        v = v * value_scale_ref[u, :, begin * tokens : (begin + count) * tokens]
        high = v.astype(jnp.bfloat16)
        low = (v - high.astype(jnp.float32)).astype(jnp.bfloat16)
        v = jnp.concatenate([high, low], axis=0)
        both = jnp.dot(v, p_ref[u], preferred_element_type=jnp.float32)
        for tile in range(groups * tokens // SPAN):
            lanes = slice(tile * SPAN, (tile + 1) * SPAN)
            mixed = both[:HEAD_WIDTH, lanes] + both[HEAD_WIDTH:, lanes]
            if not first:
                mixed = mixed + fades[tile] * mixed_in[u, :, lanes]
            if not last:
                result_ref[u, :, lanes] = mixed
                stats_ref[u, 0:1, lanes] = tops[tile]
                stats_ref[u, 1:2, lanes] = totals[tile]
                continue
            mixed = mixed * (1.0 / totals[tile])
            check = jnp.sum(mixed, axis=0, keepdims=True) * inverse_root
            mixed = jnp.transpose(mixed).astype(result_ref.dtype)
            for j in range(SPAN // tokens):
                h = tile * (SPAN // tokens) + j
                at = (u * groups + h) * HEAD_WIDTH
                result_ref[:, at : at + HEAD_WIDTH] = mixed[j * tokens : (j + 1) * tokens]
                check_ref[pl.ds(g * groups + h, 1), :] = check[:, j * tokens : (j + 1) * tokens]
    if last:

        @pl.when(step == pl.num_programs(0) - 1)
        def _():
            stats_ref[...] = jnp.transpose(check_ref[...])


def absorb(prepared, pieces, begin, state, last, tokens):
    kv_heads, _, rows = prepared[0].shape
    groups = rows // tokens
    count = len(pieces)
    per_step = 4 if kv_heads % 4 == 0 else 1
    per_step = per_step if last else kv_heads
    keys = tokens * count
    width = kv_heads * groups * HEAD_WIDTH
    first = state is None
    mixed = pl.BlockSpec((per_step, HEAD_WIDTH, rows), lambda s: (s, 0, 0))
    stats = pl.BlockSpec((per_step, 2, rows), lambda s: (s, 0, 0))
    in_specs, operands = [], []
    for piece in pieces:
        joined = len(piece) == 1
        half = (tokens, piece[0].shape[1])
        in_specs.append(pl.BlockSpec(half, lambda s: (0, 0)))
        in_specs.append(pl.BlockSpec(half, lambda s: (1, 0)) if joined else in_specs[-1])
        operands += [piece[0], piece[-1]]
    in_specs += [
        pl.BlockSpec((per_step,) + prepared[0].shape[1:], lambda s: (s, 0, 0)),
        pl.BlockSpec(prepared[1].shape, lambda s: (0, 0)),
        pl.BlockSpec(prepared[2].shape, lambda s: (0, 0)),
        pl.BlockSpec((per_step,) + prepared[3].shape[1:], lambda s: (s, 0, 0)),
        pl.BlockSpec((per_step,) + prepared[4].shape[1:], lambda s: (s, 0, 0)),
    ]
    in_specs += [] if first else [mixed, stats]
    if last:
        out_specs = [
            pl.BlockSpec((tokens, per_step * groups * HEAD_WIDTH), lambda s: (0, s)),
            pl.BlockSpec((tokens, kv_heads * groups), lambda s: (0, 0)),
        ]
        out_shape = [
            jax.ShapeDtypeStruct((tokens, width), jnp.bfloat16),
            jax.ShapeDtypeStruct((tokens, kv_heads * groups), jnp.float32),
        ]
    else:
        out_specs = [mixed, stats]
        out_shape = [
            jax.ShapeDtypeStruct((kv_heads, HEAD_WIDTH, rows), jnp.float32),
            jax.ShapeDtypeStruct((kv_heads, 2, rows), jnp.float32),
        ]
    return pl.pallas_call(
        functools.partial(
            absorb_kernel,
            groups=groups,
            tokens=tokens,
            per_step=per_step,
            begin=begin,
            count=count,
            first=first,
            last=last,
        ),
        grid=(kv_heads // per_step,),
        in_specs=in_specs,
        out_specs=out_specs,
        out_shape=out_shape,
        scratch_shapes=[
            pltpu.VMEM((per_step, keys, rows), jnp.float32),
            pltpu.VMEM((per_step, keys, rows), jnp.bfloat16),
            pltpu.VMEM((kv_heads * groups, tokens), jnp.float32),
        ],
        compiler_params=pltpu.CompilerParams(vmem_limit_bytes=44 * 1024 * 1024),
        cost_estimate=pl.CostEstimate(
            flops=16 * tokens * width * keys,
            bytes_accessed=16 * tokens * width,
            transcendentals=tokens * width // HEAD_WIDTH * keys,
        ),
    )(*operands, *prepared, *(() if first else state))


def local(queries, keys, values, key_scale, value_scale, span_order, block_keep):
    tokens = queries.shape[0]
    kv_heads = keys.shape[1] // HEAD_WIDTH
    sizes = ctx_size, head_size = lax.axis_size("ctx"), lax.axis_size("head")
    size = ctx_size // 2 * head_size
    batch = 2 * SPAN // tokens

    def device(place, core):
        row, column = place // head_size, place % head_size
        return (2 * row + core) * head_size + (column if row % 2 == 0 else head_size - 1 - column)

    def around(block, distance):
        route = [
            (device(p, core), device((p + distance) % size, core))
            for p in range(size)
            for core in range(2)
        ]
        return lax.ppermute(block, ("ctx", "head"), route)

    def to_other_core(piece):
        return [lax.ppermute(block, "ctx", [(i, i ^ 1) for i in range(ctx_size)]) for block in piece]

    def swap_heads(block, flip):
        return lax.ppermute(block, "head", [(i, i ^ flip) for i in range(head_size)])

    sources = [(0, 0)]
    for step in range(1, size // 2 + 2):
        if step < size // 2:
            sources += [(step, 0), (-step, 0)]
        elif step == size // 2:
            sources += [(step - 1, 1), (1 - step, 1), (step, 0)]
        if step == 1:
            sources += [(0, 1)]
        elif step < size // 2:
            sources += [(step - 1, 1), (1 - step, 1)]
        elif step > size // 2:
            sources += [(step - 1, 1)]

    block = lax.optimization_barrier(jnp.concatenate([keys, values], axis=0))
    scale = jnp.concatenate([jnp.transpose(key_scale), jnp.transpose(value_scale)], axis=0)
    scales, pieces, done = [scale[None]], [[block]], 0
    fresh, forward, backward = [[block]], block, block
    prepared, rows, state, gate = None, None, None, span_order
    for step in range(1, size // 2 + 2):
        crossed = [to_other_core(piece) for piece in fresh]
        sent = []
        if step < size // 2:
            forward, backward = around(forward, 1), around(backward, -1)
            sent = [[forward], [backward]]
        elif step == size // 2:
            sent = [[around(forward[:tokens], 1), around(backward[tokens:], -1)]]
        held = sum(scale.shape[0] for scale in scales)
        complete = held == head_size
        if not complete:
            scales = scales + [swap_heads(jnp.concatenate(scales, axis=0), held)]
        if step == 1:
            prepared = prepare(queries, span_order, block_keep, sources, kv_heads, sizes)
        if complete:
            if rows is None:
                rows = scale_rows(scales, gate, sources, tokens, sizes)
            ready = (len(pieces) - done) // batch * batch if step < size // 2 else 0
            now = pieces[done : done + ready]
            if step == size // 2:
                now = pieces[done:] + crossed
                ready = len(now)
            if ready:
                state = absorb((*prepared, *rows), now, done, state, False, tokens)
                done += ready
        if sum(scale.shape[0] for scale in scales) < head_size:
            sent, crossed, scales, prepared, rows, state = lax.optimization_barrier(
                (sent, crossed, scales, prepared, rows, state)
            )
        elif step == size // 2 - 1:
            crossed, sent, prepared, rows, state = lax.optimization_barrier(
                (crossed, sent, prepared, rows, state)
            )
        else:
            sent, crossed, gate, prepared, rows, state = lax.optimization_barrier(
                (sent, crossed, gate, prepared, rows, state)
            )
        fresh = sent
        if step < size // 2:
            forward, backward = fresh[0][0], fresh[1][0]
        pieces = pieces + (sent + crossed if step < size // 2 else crossed + sent)
    return tuple(absorb((*prepared, *rows), pieces[done:], done, state, True, tokens))


def solution(mesh):
    rows = P(("dp", "ctx", "head"), None)
    return jax.shard_map(
        local,
        mesh=mesh,
        in_specs=(rows, rows, rows, P("dp", "head"), P("dp", "head"), P(), P()),
        out_specs=(rows, rows),
        check_vma=False,
    )
```
